32 devices in a mesh: wide: 8 (over y, x, core), narrow: 4 (over z).
Axes of the slice: x: 2, y: 2, z: 4, core: 2. Of those that a mesh axis runs over, the one named last changes fastest.
Arguments:
- token_ids: int32 [2, 32, 384], P(None, ('wide', 'narrow')), may hold values from 0 to 30591
- seq_lengths: int32 [2, 32], P(None, ('wide', 'narrow')), may hold values from 24 to 384, as said below
- mlm_slots: int32 [2, 32, 56], P(None, ('wide', 'narrow')), may hold values from 0 to 383
- mlm_labels: int32 [2, 32, 56], P(None, ('wide', 'narrow')), may hold values from 0 to 30591
- nsp_labels: int32 [2, 32], P(None, ('wide', 'narrow')), may hold values from 0 to 1
- table_master: float32 [30592, 768], P(('wide', 'narrow')), may hold values from -0.375 to 0.375
- table_first: float32 [30592, 768], P(('wide', 'narrow')), may hold values from -2.3841858e-06 to 2.3841858e-06
- table_second: float32 [30592, 768], P(('wide', 'narrow')), may hold values from 6.2315795e-15 to 9.970527e-14
- position_master: float32 [384, 768], P(None, ('wide', 'narrow')), may hold values from -0.375 to 0.375
- position_first: float32 [384, 768], P(None, ('wide', 'narrow')), may hold values from -2.3841858e-06 to 2.3841858e-06
- position_second: float32 [384, 768], P(None, ('wide', 'narrow')), may hold values from 6.2315795e-15 to 9.970527e-14
- pair_master: float32 [2, 768, 2], P(None, ('wide', 'narrow')), may hold values from -0.75 to 0.75
- pair_first: float32 [2, 768, 2], P(None, ('wide', 'narrow')), may hold values from -2.3841858e-06 to 2.3841858e-06
- pair_second: float32 [2, 768, 2], P(None, ('wide', 'narrow')), may hold values from 6.2315795e-15 to 9.970527e-14
- input_master: float32 [768, 2304], P(('wide', 'narrow')), may hold values from -0.21875 to 0.21875
- input_first: float32 [768, 2304], P(('wide', 'narrow')), may hold values from -2.3841858e-06 to 2.3841858e-06
- input_second: float32 [768, 2304], P(('wide', 'narrow')), may hold values from 6.2315795e-15 to 9.970527e-14
- output_master: float32 [768, 768], P(('wide', 'narrow')), may hold values from -0.875 to 0.875
- output_first: float32 [768, 768], P(('wide', 'narrow')), may hold values from -2.3841858e-06 to 2.3841858e-06
- output_second: float32 [768, 768], P(('wide', 'narrow')), may hold values from 6.2315795e-15 to 9.970527e-14
- dense_master: float32 [2, 768, 768], P(None, ('wide', 'narrow')), may hold values from -0.21875 to 0.21875
- dense_first: float32 [2, 768, 768], P(None, ('wide', 'narrow')), may hold values from -2.3841858e-06 to 2.3841858e-06
- dense_second: float32 [2, 768, 768], P(None, ('wide', 'narrow')), may hold values from 6.2315795e-15 to 9.970527e-14
- feed_master: float32 [2, 768, 3072], P(None, ('wide', 'narrow')), may hold values from -0.21875 to 0.21875
- feed_first: float32 [2, 768, 3072], P(None, ('wide', 'narrow')), may hold values from -2.3841858e-06 to 2.3841858e-06
- feed_second: float32 [2, 768, 3072], P(None, ('wide', 'narrow')), may hold values from 6.2315795e-15 to 9.970527e-14
- vector_master: float32 [44416], P(('wide', 'narrow')), may hold values from -1.75 to 2.4
- vector_first: float32 [44416], P(('wide', 'narrow')), may hold values from -9.536743e-06 to 9.536743e-06
- vector_second: float32 [44416], P(('wide', 'narrow')), may hold values from 9.970527e-14 to 1.5952843e-12
Outputs:
- masked_sums: float32 [2], replicated
- pair_sum: float32 [], replicated
- grad_norm: float32 [], replicated
- table_new: float32 [30592, 768], P(('wide', 'narrow'))
- table_first_new: float32 [30592, 768], P(('wide', 'narrow'))
- table_second_new: float32 [30592, 768], P(('wide', 'narrow'))
- position_new: float32 [384, 768], P(None, ('wide', 'narrow'))
- position_first_new: float32 [384, 768], P(None, ('wide', 'narrow'))
- position_second_new: float32 [384, 768], P(None, ('wide', 'narrow'))
- pair_new: float32 [2, 768, 2], P(None, ('wide', 'narrow'))
- pair_first_new: float32 [2, 768, 2], P(None, ('wide', 'narrow'))
- pair_second_new: float32 [2, 768, 2], P(None, ('wide', 'narrow'))
- input_new: float32 [768, 2304], P(('wide', 'narrow'))
- input_first_new: float32 [768, 2304], P(('wide', 'narrow'))
- input_second_new: float32 [768, 2304], P(('wide', 'narrow'))
- output_new: float32 [768, 768], P(('wide', 'narrow'))
- output_first_new: float32 [768, 768], P(('wide', 'narrow'))
- output_second_new: float32 [768, 768], P(('wide', 'narrow'))
- dense_new: float32 [2, 768, 768], P(None, ('wide', 'narrow'))
- dense_first_new: float32 [2, 768, 768], P(None, ('wide', 'narrow'))
- dense_second_new: float32 [2, 768, 768], P(None, ('wide', 'narrow'))
- feed_new: float32 [2, 768, 3072], P(None, ('wide', 'narrow'))
- feed_first_new: float32 [2, 768, 3072], P(None, ('wide', 'narrow'))
- feed_second_new: float32 [2, 768, 3072], P(None, ('wide', 'narrow'))
- vector_new: float32 [44416], P(('wide', 'narrow'))
- vector_first_new: float32 [44416], P(('wide', 'narrow'))
- vector_second_new: float32 [44416], P(('wide', 'narrow'))
The draws below stay inside these ranges and needn't reach their ends.
Inputs may be any that keep to these rules, and one draw needn't show every extreme that they name: `seq_lengths`: in each micro-batch one sequence, drawn from the seed, has length 384.
All inputs are finite; a program needn't handle non-finite values.
Results may differ from the reference program's by a relative error of at most 0.007.
The reference program's roundings to bfloat16 on the way (of `table`, `mixed`, `context` and `active`) count: a program that leaves them out, or rounds other values in their place, can miss the bound.
Values may be sent and summed in bfloat16 or wider, within the bound.
No kernel may reach another device: no remote copies, remote signals or barrier semaphores. Data moves between devices by JAX's collectives and lax.ppermute only.
A program may use at most 960 MiB of HBM per device.

```python
import math
import jax
import jax.numpy as jnp
import numpy as np
from jax import lax

D = 768
HEADS = 12
HEAD = 64
FF = 3072
V = 30592
SEQ = 384
MB = 2
STEP_COUNT = 10
MLMP = 56
NSEQ = 32
NPAR = 32094592
N_WIDE = 8
N_NARROW = 4


def draw_seq_lengths(key, part):
    key = jax.random.fold_in(key, 11)
    level_key, pick_key = jax.random.split(key)
    level = jax.random.randint(level_key, (MB, NSEQ), 0, 17)
    order = jnp.arange(NSEQ, dtype=jnp.int32)
    wide_ramp = N_WIDE + 2 * (order // N_NARROW)
    narrow_ramp = N_NARROW + 2 * (order % N_NARROW)
    shortest = SEQ // 16
    weight_part = wide_ramp[None, :] * narrow_ramp[None, :] * level * level * level // (N_WIDE * N_NARROW)
    lengths = shortest + (SEQ - shortest) * weight_part // (9 * 4096)
    chosen = jax.random.randint(pick_key, (MB,), 0, NSEQ)
    lengths = jnp.where(order[None, :] == chosen[:, None], SEQ, lengths)
    return lengths.astype(jnp.int32)


def draw_vector_master(key, part):
    key = jax.random.fold_in(key, 23)
    noise_key, shift_key = jax.random.split(key)
    total = 14 * D + FF + V
    index = jnp.arange(total, dtype=jnp.int32)
    column = (index % D).astype(jnp.float32) / (D - 1)
    gain_slot = (index < 8 * D) & (index // D % 2 == 0)
    vocab_slot = index >= 14 * D + FF
    ramp = 0.6 + 1.2 * column
    noise = jnp.clip(0.1 * jax.random.normal(noise_key, (total,), jnp.float32), -0.3, 0.3)
    shifts = jnp.clip(0.1 * jax.random.normal(shift_key, (total,), jnp.float32), -0.35, 0.35)
    return jnp.where(gain_slot, ramp * (1.0 + noise), jnp.where(vocab_slot, 5.0 * shifts, shifts))


def plant(values, key, low, high):
    shape = values.shape
    index_at = [jax.random.randint(jax.random.fold_in(key, axis), (), 0, shape[axis]) for axis in range(len(shape))]
    values = values.at[tuple(index_at)].set(low)
    longest = shape.index(max(shape))
    index_at[longest] = (index_at[longest] + 1) % shape[longest]
    return values.at[tuple(index_at)].set(high)


def steps_of(key, shape, shards, low, largest):
    loudness = 1.0
    for dim, blocks in shards:
        heights = jax.random.uniform(jax.random.fold_in(jax.random.fold_in(key, 6), dim), (blocks,), jnp.float32, low / len(shards), largest / len(shards))
        loudness = loudness * jnp.repeat(jnp.exp(heights), shape[dim] // blocks).reshape((-1,) + (1,) * (len(shape) - 1 - dim))
    return loudness


def rank_bounds(number_of, slope):
    portions = [(1 << 20) // math.isqrt(rank ** slope) + 1 for rank in range(1, number_of + 1)]
    deviation = 1 + sum(portions) // (1 << 30)
    return np.cumsum(np.array([max(1, weight // deviation) for weight in portions]))


def ranked_ids(stream_key, shape, number_of, slope):
    listing = rank_bounds(number_of, slope)
    pick = jax.random.randint(jax.random.fold_in(stream_key, 1), shape, 0, int(listing[number_of - 1]))
    grade = jnp.searchsorted(jnp.asarray(listing, jnp.int32), pick, side="right")
    return jax.random.permutation(jax.random.fold_in(stream_key, 2), number_of)[grade].astype(jnp.int32)


def centred(key, dims, scale, bound, cuts=(), held_as=jnp.bfloat16):
    level = steps_of(key, dims, cuts, -0.22, 0.18) if cuts else 1.0
    array = jax.random.normal(key, dims, jnp.float32) * scale * level
    return jnp.minimum(jnp.maximum(array, -bound), bound).astype(held_as)


def setup_inputs(seed: int = 0) -> dict:
    arg_keys = jax.random.split(jax.random.key(seed), 30)
    token_ids = plant(ranked_ids(arg_keys[0], (MB, NSEQ, SEQ), V, 2), jax.random.fold_in(arg_keys[0], 3), 0, V - 1).astype(jnp.int32)
    seq_lengths = draw_seq_lengths(jax.random.fold_in(arg_keys[29], 71), 0)
    mlm_slots = plant(jax.random.randint(arg_keys[2], (MB, NSEQ, MLMP), 0, SEQ), jax.random.fold_in(arg_keys[2], 1), 0, SEQ - 1).astype(jnp.int32)
    mlm_labels = plant(ranked_ids(arg_keys[3], (MB, NSEQ, MLMP), V, 2), jax.random.fold_in(arg_keys[3], 3), 0, V - 1).astype(jnp.int32)
    nsp_labels = plant(jax.random.randint(arg_keys[4], (MB, NSEQ), 0, 2), jax.random.fold_in(arg_keys[4], 1), 0, 1).astype(jnp.int32)
    table_master = centred(arg_keys[5], (V, D), 0.06, 0.375, ((0, 32),), jnp.float32)
    table_first = centred(arg_keys[6], (V, D), (0.111 * 0.02 / NPAR ** 0.5), 2.384185791015625e-06, ((0, 32),), jnp.float32)
    table_second = jnp.clip(jnp.exp(math.log(9.970527143710398e-14) - 2.7725887 * jax.random.uniform(arg_keys[7], (V, D), jnp.float32) ** steps_of(arg_keys[7], (V, D), ((0, 32),), -0.2, 0.2)), 6.2315794648189985e-15, 9.970527143710398e-14)
    position_master = centred(arg_keys[8], (SEQ, D), 0.06, 0.375, ((1, 32),), jnp.float32)
    position_first = centred(arg_keys[9], (SEQ, D), (0.111 * 0.02 / NPAR ** 0.5), 2.384185791015625e-06, ((1, 32),), jnp.float32)
    position_second = jnp.clip(jnp.exp(math.log(9.970527143710398e-14) - 2.7725887 * jax.random.uniform(arg_keys[10], (SEQ, D), jnp.float32) ** steps_of(arg_keys[10], (SEQ, D), ((1, 32),), -0.2, 0.2)), 6.2315794648189985e-15, 9.970527143710398e-14)
    pair_master = centred(arg_keys[11], (2, D, 2), 0.12, 0.75, ((1, 32),), jnp.float32)
    pair_first = centred(arg_keys[12], (2, D, 2), (0.111 * 0.02 / NPAR ** 0.5), 2.384185791015625e-06, ((1, 32),), jnp.float32)
    pair_second = jnp.clip(jnp.exp(math.log(9.970527143710398e-14) - 2.7725887 * jax.random.uniform(arg_keys[13], (2, D, 2), jnp.float32) ** steps_of(arg_keys[13], (2, D, 2), ((1, 32),), -0.2, 0.2)), 6.2315794648189985e-15, 9.970527143710398e-14)
    input_master = centred(arg_keys[14], (D, 3 * D), D ** -0.5, 0.21875, ((0, 32),), jnp.float32)
    input_first = centred(arg_keys[15], (D, 3 * D), (0.111 * 0.02 / NPAR ** 0.5), 2.384185791015625e-06, ((0, 32),), jnp.float32)
    input_second = jnp.clip(jnp.exp(math.log(9.970527143710398e-14) - 2.7725887 * jax.random.uniform(arg_keys[16], (D, 3 * D), jnp.float32) ** steps_of(arg_keys[16], (D, 3 * D), ((0, 32),), -0.2, 0.2)), 6.2315794648189985e-15, 9.970527143710398e-14)
    output_master = centred(arg_keys[17], (D, D), (D // 16) ** -0.5, 0.875, ((0, 32),), jnp.float32)
    output_first = centred(arg_keys[18], (D, D), (0.111 * 0.02 / NPAR ** 0.5), 2.384185791015625e-06, ((0, 32),), jnp.float32)
    output_second = jnp.clip(jnp.exp(math.log(9.970527143710398e-14) - 2.7725887 * jax.random.uniform(arg_keys[19], (D, D), jnp.float32) ** steps_of(arg_keys[19], (D, D), ((0, 32),), -0.2, 0.2)), 6.2315794648189985e-15, 9.970527143710398e-14)
    dense_master = centred(arg_keys[20], (2, D, D), D ** -0.5, 0.21875, ((1, 32),), jnp.float32)
    dense_first = centred(arg_keys[21], (2, D, D), (0.111 * 0.02 / NPAR ** 0.5), 2.384185791015625e-06, ((1, 32),), jnp.float32)
    dense_second = jnp.clip(jnp.exp(math.log(9.970527143710398e-14) - 2.7725887 * jax.random.uniform(arg_keys[22], (2, D, D), jnp.float32) ** steps_of(arg_keys[22], (2, D, D), ((1, 32),), -0.2, 0.2)), 6.2315794648189985e-15, 9.970527143710398e-14)
    feed_master = centred(arg_keys[23], (2, D, FF), D ** -0.5, 0.21875, ((1, 32),), jnp.float32)
    feed_first = centred(arg_keys[24], (2, D, FF), (0.111 * 0.02 / NPAR ** 0.5), 2.384185791015625e-06, ((1, 32),), jnp.float32)
    feed_second = jnp.clip(jnp.exp(math.log(9.970527143710398e-14) - 2.7725887 * jax.random.uniform(arg_keys[25], (2, D, FF), jnp.float32) ** steps_of(arg_keys[25], (2, D, FF), ((1, 32),), -0.2, 0.2)), 6.2315794648189985e-15, 9.970527143710398e-14)
    vector_master = draw_vector_master(jax.random.fold_in(arg_keys[29], 71), 0)
    vector_first = centred(arg_keys[27], (14 * D + FF + V,), (0.444 * 0.02 / NPAR ** 0.5), 9.5367431640625e-06, ((0, 32),), jnp.float32)
    vector_second = jnp.clip(jnp.exp(math.log(1.5952843429936636e-12) - 2.7725887 * jax.random.uniform(arg_keys[28], (14 * D + FF + V,), jnp.float32) ** steps_of(arg_keys[28], (14 * D + FF + V,), ((0, 32),), -0.2, 0.2)), 9.970527143710398e-14, 1.5952843429936636e-12)
    return dict(token_ids=token_ids, seq_lengths=seq_lengths, mlm_slots=mlm_slots, mlm_labels=mlm_labels, nsp_labels=nsp_labels, table_master=table_master, table_first=table_first, table_second=table_second, position_master=position_master, position_first=position_first, position_second=position_second, pair_master=pair_master, pair_first=pair_first, pair_second=pair_second, input_master=input_master, input_first=input_first, input_second=input_second, output_master=output_master, output_first=output_first, output_second=output_second, dense_master=dense_master, dense_first=dense_first, dense_second=dense_second, feed_master=feed_master, feed_first=feed_first, feed_second=feed_second, vector_master=vector_master, vector_first=vector_first, vector_second=vector_second)


HIGH = lax.Precision.HIGHEST
NORM_EPS = 1e-12
CLIP_NORM = 0.02
BETA_ONE = 0.9
BETA_TWO = 0.999
ADAM_EPS = 1e-08
DECAY_RATE = 0.01
LEARN_RATE = 0.1
MASKED_FILL = -1000000000.0

@jax.custom_vjp
def low(v):
    return lax.optimization_barrier(v.astype(jnp.bfloat16)).astype(jnp.float32)

@jax.custom_vjp
def low_back(v):
    return v

def low_keep(v):
    return (low(v), None)

def low_pass(kept, grad):
    return (grad,)

def back_keep(v):
    return (v, None)

def back_low(kept, grad):
    return (low(grad),)
low.defvjp(low_keep, low_pass)
low_back.defvjp(back_keep, back_low)

def matmul(left, right):
    return jnp.dot(left, right, precision=HIGH)

def layer_norm(values, gain, shift):
    average = lax.optimization_barrier(jnp.mean(values, axis=-1, keepdims=True))
    centered = values - average
    spread = lax.optimization_barrier(jnp.mean(centered * centered, axis=-1, keepdims=True))
    return centered * lax.rsqrt(spread + NORM_EPS) * gain + shift

def gelu_exact(values):
    return jax.nn.gelu(values, approximate=False)

def split_vectors(vectors):
    extents = [D] * 11 + [FF] + [D] * 3
    pieces = []
    start = 0
    for extent in extents:
        pieces.append(vectors[start:start + extent])
        start += extent
    pieces.append(vectors[start:])
    return pieces

def sequence_loss(params, token_row, length, slots, labels, pair_label, inv_count, inv_seqs):
    table, position, pair_cols, input_proj, output_proj, dense_pair, feed_pair, vectors = [low(item) for item in params]
    parts = split_vectors(vectors)
    places = jnp.arange(SEQ, dtype=jnp.int32)
    second = places >= length // 2
    embedded = table[token_row] + position + jnp.where(second[:, None], pair_cols[0][:, 1], pair_cols[0][:, 0])
    normed = layer_norm(embedded, parts[0], parts[1])
    bias_mixed = jnp.concatenate([parts[8], jnp.zeros((D,), parts[8].dtype), parts[9]])
    mixed = low(low_back(matmul(low(normed), input_proj) + bias_mixed))
    queries = mixed[:, :D].reshape(SEQ, HEADS, HEAD)
    keys = mixed[:, D:2 * D].reshape(SEQ, HEADS, HEAD)
    values = mixed[:, 2 * D:].reshape(SEQ, HEADS, HEAD)
    raw = jnp.einsum('qhd,khd->hqk', queries, keys, precision=HIGH) * HEAD ** (-0.5)
    alive = places[None, None, :] < length
    scores = low_back(jnp.where(alive, raw, MASKED_FILL))
    attention = jax.nn.softmax(scores, axis=-1)
    context = jnp.einsum('hqk,khd->qhd', low(attention), values, precision=HIGH).reshape(SEQ, D)
    context = low(low_back(context))
    branch = low_back(matmul(context, output_proj) + parts[10])
    hidden_one = layer_norm(normed + branch, parts[2], parts[3])
    inner = low_back(matmul(low(hidden_one), feed_pair[0]) + parts[11])
    active = low(gelu_exact(inner))
    outer = low_back(matmul(active, feed_pair[1].T) + parts[12])
    hidden_two = layer_norm(hidden_one + outer, parts[4], parts[5])
    picked = hidden_two[slots]
    transform = low_back(matmul(low(picked), dense_pair[0]) + parts[13])
    head_out = layer_norm(gelu_exact(transform), parts[6], parts[7])
    logits = low_back(matmul(low(head_out), table.T) + parts[15])
    log_total = jax.nn.logsumexp(logits, axis=-1)
    target = jnp.take_along_axis(logits, labels[:, None], axis=-1)[:, 0]
    counted = (slots < length).astype(logits.dtype)
    masked_sum = jnp.sum(counted * (log_total - target))
    pooled = jnp.tanh(low_back(matmul(low(hidden_two[0:1]), dense_pair[1]) + parts[14]))
    pair_logits = low_back(matmul(low(pooled), pair_cols[1]))[0]
    pair_loss = jax.nn.logsumexp(pair_logits) - pair_logits[pair_label]
    return (masked_sum * inv_count + pair_loss * inv_seqs, (masked_sum, pair_loss))

def reference(token_ids, seq_lengths, mlm_slots, mlm_labels, nsp_labels, table_master, table_first, table_second, position_master, position_first, position_second, pair_master, pair_first, pair_second, input_master, input_first, input_second, output_master, output_first, output_second, dense_master, dense_first, dense_second, feed_master, feed_first, feed_second, vector_master, vector_first, vector_second):
    masters = (table_master, position_master, pair_master, input_master, output_master, dense_master, feed_master, vector_master)
    firsts = (table_first, position_first, pair_first, input_first, output_first, dense_first, feed_first, vector_first)
    seconds = (table_second, position_second, pair_second, input_second, output_second, dense_second, feed_second, vector_second)
    counted = (mlm_slots < seq_lengths[:, :, None]).astype(table_master.dtype)
    masked_count = jnp.sum(counted)
    inv_count = 1.0 / masked_count
    inv_seqs = 1.0 / (MB * NSEQ)
    rows = (token_ids.reshape(MB * NSEQ, SEQ), seq_lengths.reshape(MB * NSEQ), mlm_slots.reshape(MB * NSEQ, MLMP), mlm_labels.reshape(MB * NSEQ, MLMP), nsp_labels.reshape(MB * NSEQ))

    def one_sequence(carry, row):
        grads, masked_total, pair_total = carry
        token_row, length, slots, labels, pair_label = row

        def loss_of(params):
            return sequence_loss(params, token_row, length, slots, labels, pair_label, inv_count, inv_seqs)
        value, pullback, extra = jax.vjp(loss_of, masters, has_aux=True)
        grad_here, = pullback(jnp.ones_like(value))
        grads = jax.tree.map(jnp.add, grads, grad_here)
        return ((grads, masked_total + extra[0], pair_total + extra[1]), None)
    start = (tuple((jnp.zeros_like(item) for item in masters)), jnp.zeros((), table_master.dtype), jnp.zeros((), table_master.dtype))
    (grads, masked_total, pair_total), unused = lax.scan(one_sequence, start, rows)
    norm = jnp.sqrt(sum((jnp.sum(item * item) for item in grads)))
    factor = CLIP_NORM / (norm + 1e-06)
    correct_one = 1.0 - BETA_ONE ** STEP_COUNT
    correct_two = 1.0 - BETA_TWO ** STEP_COUNT
    updated = []
    for number in range(8):
        grad = grads[number] * factor
        moment_one = BETA_ONE * firsts[number] + (1.0 - BETA_ONE) * grad
        moment_two = BETA_TWO * seconds[number] + (1.0 - BETA_TWO) * grad * grad
        direction = moment_one / correct_one / (jnp.sqrt(moment_two / correct_two) + ADAM_EPS)
        decay = DECAY_RATE if number < 7 else 0.0
        updated.extend([masters[number] - LEARN_RATE * (direction + decay * masters[number]), moment_one, moment_two])
    masked_sums = jnp.stack([masked_total, masked_count])
    return (masked_sums, pair_total, norm, updated[0], updated[1], updated[2], updated[3], updated[4], updated[5], updated[6], updated[7], updated[8], updated[9], updated[10], updated[11], updated[12], updated[13], updated[14], updated[15], updated[16], updated[17], updated[18], updated[19], updated[20], updated[21], updated[22], updated[23])
```

```python
from functools import partial

import jax
import jax.numpy as jnp
from jax import lax
from jax.experimental import pallas as pl
from jax.experimental.pallas import tpu as pltpu
from jax.sharding import PartitionSpec as P

D = 768
HEAD = 64
FF = 3072
STEP_COUNT = 10


NORM_EPS = 1e-12
CLIP_NORM = 0.02
BETA_ONE = 0.9
BETA_TWO = 0.999
ADAM_EPS = 1e-08
DECAY_RATE = 0.01
LEARN_RATE = 0.1
MASKED_FILL = -1000000000.0
AXES = ("wide", "narrow")
ROWS_AHEAD = 96
LANES = 128


def product(left, right):
    return jnp.dot(left, right, preferred_element_type=jnp.float32)


def product_right(left, right):
    return lax.dot_general(
        left, right, (((1,), (1,)), ((), ())), preferred_element_type=jnp.float32
    )


def product_left(left, right):
    return lax.dot_general(
        left, right, (((0,), (0,)), ((), ())), preferred_element_type=jnp.float32
    )


def norm_forward(values, gain, shift):
    average = jnp.mean(values, axis=-1, keepdims=True)
    centered = values - average
    spread = jnp.mean(centered * centered, axis=-1, keepdims=True)
    inverse = lax.rsqrt(spread + NORM_EPS)
    normal = centered * inverse
    return (normal * gain + shift, (normal, inverse))


def norm_backward(grad, saved, gain):
    normal, inverse = saved
    scaled = grad * gain
    inner = (
        scaled
        - jnp.mean(scaled, axis=-1, keepdims=True)
        - normal * jnp.mean(scaled * normal, axis=-1, keepdims=True)
    )
    return (inner * inverse, jnp.sum(grad * normal, axis=0), jnp.sum(grad, axis=0))


def gelu_exact(values):
    return jax.nn.gelu(values, approximate=False)


def gelu_back(values, grad):
    return jax.vjp(gelu_exact, values)[1](grad)[0]


def split_vectors(vectors):
    extents = [D] * 11 + [FF] + [D] * 3
    pieces = []
    start = 0
    for extent in extents:
        pieces.append(vectors[start : start + extent])
        start += extent
    pieces.append(vectors[start:])
    return pieces


def bits_of(size):
    return size.bit_length() - 1


def orders():
    far = [("wide", bit) for bit in range(1, bits_of(lax.axis_size("wide")))]
    return far, far[::-1]


CORE = ("wide", 0)


def my_bit(dim):
    return (lax.axis_index(dim[0]) >> dim[1]) & 1


def swap(values, dim):
    size = lax.axis_size(dim[0])
    return lax.ppermute(values, dim[0], [(i, i ^ (1 << dim[1])) for i in range(size)])


def pin(values, *others):
    return lax.optimization_barrier((values, others))[0]


def place_blocks(spreads, starts, middle, me_ref, *refs):
    count = len(spreads[0])
    outs = refs[8 : 8 + len(starts) - 1]
    held = refs[8 + len(outs) : 10 + len(outs)]
    arrive, leave = refs[10 + len(outs) :]
    me = me_ref[0]
    inward, outward = [], []
    for side in range(2):
        pieces = refs[4 * side : 4 * side + 4]
        each = pieces[0].shape[0]
        left = 0 if side == 0 else middle
        right = middle if side == 0 else starts[-1]
        for code, offset in enumerate(spreads[side]):
            number = side * count + code
            inward.append(
                pltpu.make_async_copy(
                    pieces[code // each].at[code % each], held[side].at[code], arrive.at[number]
                )
            )
            group = []
            for out_ref, start, stop in zip(outs, starts, starts[1:]):
                low, high = max(start, left), min(stop, right)
                if low < high:
                    group.append(
                        pltpu.make_async_copy(
                            held[side].at[code, :, :, low - left : high - left],
                            out_ref.at[me ^ offset, :, :, low - start : high - start],
                            leave.at[number, len(group)],
                        )
                    )
            outward.append(group)
    for copy in inward:
        copy.start()
    for first, group in zip(inward, outward):
        first.wait()
        for copy in group:
            copy.start()
    for group in outward:
        for copy in group:
            copy.wait()


def along_line(block):
    size = lax.axis_size("narrow")
    me = lax.axis_index("narrow")
    rights, lefts = [], []
    right = left = block
    for step in range(1, size):
        right = lax.ppermute(right, "narrow", [(z, z + 1) for z in range(step - 1, size - 1)])
        left = lax.ppermute(left, "narrow", [(z, z - 1) for z in range(1, size - step + 1)])
        rights.append(right)
        lefts.append(left)
    blocks = []
    for spot in range(size):
        chosen = block
        for other in range(size):
            if other > spot:
                chosen = jnp.where(me == other, rights[other - spot - 1], chosen)
            if other < spot:
                chosen = jnp.where(me == other, lefts[spot - other - 1], chosen)
        blocks.append(chosen)
    return blocks


class Gather:
    def __init__(self, arrays):
        self.columns = [array.shape[1] for array in arrays]
        self.rows = arrays[0].shape[0]
        total = sum(self.columns)
        self.middle = total // 2 // LANES * LANES
        self.packed = jnp.concatenate(arrays, axis=1) if len(arrays) > 1 else arrays[0]

    def line(self):
        blocks = along_line(self.packed)
        self.halves = [
            jnp.stack([block[:, : self.middle] for block in blocks])[None],
            jnp.stack([block[:, self.middle :] for block in blocks])[None],
        ]
        return self.halves

    def plane(self):
        self.pieces = []
        for held, order in zip(self.halves, orders()):
            for dim in order[:-1]:
                held = jnp.concatenate([held, swap(held, dim)], axis=0)
            self.pieces.append([held, swap(held, order[-1])])
        return self.pieces

    def finish(self):
        pieces = [half + [swap(piece, CORE) for piece in half] for half in self.pieces]
        count = lax.axis_size("wide")
        spreads = [
            [
                sum(((code >> k) & 1) << dim[1] for k, dim in enumerate(order + [CORE]))
                for code in range(count)
            ]
            for order in orders()
        ]
        starts = [sum(self.columns[:k]) for k in range(len(self.columns) + 1)]
        line = lax.axis_size("narrow")
        dtype = self.packed.dtype
        me = lax.axis_index("wide").astype(jnp.int32).reshape(1)
        moved = 2 * count * line * self.rows * starts[-1] * dtype.itemsize
        outs = pl.pallas_call(
            partial(place_blocks, spreads, starts, self.middle),
            out_shape=tuple(
                jax.ShapeDtypeStruct((count, line, self.rows, columns), dtype)
                for columns in self.columns
            ),
            in_specs=[pl.BlockSpec(memory_space=pltpu.SMEM)]
            + [pl.BlockSpec(memory_space=pl.ANY)] * 8,
            out_specs=(pl.BlockSpec(memory_space=pl.ANY),) * len(self.columns),
            scratch_shapes=[
                pltpu.VMEM((count, line, self.rows, self.middle), dtype),
                pltpu.VMEM((count, line, self.rows, starts[-1] - self.middle), dtype),
                pltpu.SemaphoreType.DMA((2 * count,)),
                pltpu.SemaphoreType.DMA((2 * count, len(self.columns))),
            ],
            compiler_params=pltpu.CompilerParams(vmem_limit_bytes=40 << 20),
            cost_estimate=pl.CostEstimate(flops=0, bytes_accessed=moved, transcendentals=0),
        )(me, *pieces[0], *pieces[1])
        return [out.reshape(count * line * self.rows, -1) for out in outs]


class Scatter:
    def __init__(self, items):
        wide, line = lax.axis_size("wide"), lax.axis_size("narrow")
        self.labels, self.terms, self.dims = [], [], []
        for blocks, which in items:
            self.labels.append([("wide", bit) for bit in range(bits_of(wide))][::-1])
            self.terms.append(
                [blocks.reshape((2,) * bits_of(wide) + (line,) + blocks.shape[1:])]
            )
            self.dims.append([CORE] + orders()[which][::-1])

    def send(self):
        self.away = []
        for labels, terms, dims in zip(self.labels, self.terms, self.dims):
            axis, bit = labels.index(dims[0]), my_bit(dims[0])
            self.away.append(
                sum(
                    lax.dynamic_index_in_dim(term, 1 - bit, axis, keepdims=False).astype(
                        jnp.float32
                    )
                    for term in terms
                ).astype(jnp.bfloat16)
            )
        return self.away

    def receive(self):
        arrived = []
        for number, away in enumerate(self.away):
            dim = self.dims[number].pop(0)
            axis, bit = self.labels[number].index(dim), my_bit(dim)
            arrived.append(swap(away, dim))
            self.terms[number] = [
                lax.dynamic_index_in_dim(term, bit, axis, keepdims=False)
                for term in self.terms[number]
            ] + [arrived[-1]]
            self.labels[number].remove(dim)
        return arrived

    def step(self):
        self.send()
        return self.receive()

    def line(self):
        sums = [sum(term.astype(jnp.float32) for term in terms) for terms in self.terms]
        size = lax.axis_size("narrow")
        me = lax.axis_index("narrow")
        depth = min(item.shape[1] for item in sums)
        flat, cuts = [], []
        for item in sums:
            parts = [item[:, k : k + depth] for k in range(0, item.shape[1], depth)]
            flat.extend(parts)
            cuts.append((len(parts), item.shape[2]))
        whole = jnp.concatenate(flat, axis=2) if len(flat) > 1 else flat[0]
        right = left = None
        for step in range(1, size):
            spot = jnp.clip(me + size - step, 0, size - 1)
            goes = lax.dynamic_index_in_dim(whole, spot, 0, keepdims=False)
            if right is not None:
                goes = goes + right.astype(jnp.float32)
            right = lax.ppermute(
                goes.astype(jnp.bfloat16), "narrow", [(z, z + 1) for z in range(step)]
            )
            spot = jnp.clip(me - size + step, 0, size - 1)
            goes = lax.dynamic_index_in_dim(whole, spot, 0, keepdims=False)
            if left is not None:
                goes = goes + left.astype(jnp.float32)
            left = lax.ppermute(
                goes.astype(jnp.bfloat16),
                "narrow",
                [(z, z - 1) for z in range(size - step, size)],
            )
        total = (
            lax.dynamic_index_in_dim(whole, me, 0, keepdims=False)
            + right.astype(jnp.float32)
            + left.astype(jnp.float32)
        )
        results, start = [], 0
        for parts, columns in cuts:
            pieces = [
                total[:, start + k * columns : start + (k + 1) * columns] for k in range(parts)
            ]
            start += parts * columns
            results.append(jnp.concatenate(pieces, axis=0) if parts > 1 else pieces[0])
        return results


def share_small(values):
    count = lax.axis_size(AXES)
    spread = jnp.broadcast_to(values[None], (count,) + values.shape)
    return lax.all_to_all(spread, AXES, 0, 0)


def pack_kernel(length_ref, ids_ref, slot_ref, label_ref, out_ref):
    out_ref[...] = jnp.zeros_like(out_ref)
    micro, local, tokens = ids_ref.shape
    slots = slot_ref.shape[2]
    row = 0
    for index in range(micro * local):
        for start in range(0, tokens, LANES):
            out_ref[row : row + 1, :] = ids_ref[
                index // local, index % local : index % local + 1, start : start + LANES
            ]
            row += 1
    for ref in (slot_ref, label_ref):
        for index in range(micro * local):
            out_ref[row : row + 1, :slots] = ref[
                index // local, index % local : index % local + 1, :
            ]
            row += 1
    for index in range(micro * local):
        out_ref[row : row + 1, :] = jnp.full(
            (1, LANES), length_ref[index // local, index % local], jnp.int32
        )
        row += 1


def stack_kernel(*refs):
    sources, out_ref, rows_ref = refs[:-2], refs[-2], refs[-1]
    rows_ref[...] = jnp.zeros_like(rows_ref)
    row = 0
    for ref in sources:
        rows_ref[row : row + ref.shape[0], :] = ref[...]
        row += ref.shape[0]
    out_ref[...] = rows_ref[...].T


def stack_columns(rows):
    width = rows[0].shape[1]
    return pl.pallas_call(
        stack_kernel,
        out_shape=jax.ShapeDtypeStruct((width, LANES), jnp.float32),
        scratch_shapes=[pltpu.VMEM((LANES, width), jnp.float32)],
    )(*rows)


def gelu_parts(values):
    below = 0.5 + 0.5 * lax.erf(values * (0.5**0.5))
    density = jnp.exp(-0.5 * values * values) * ((0.5 / jnp.pi) ** 0.5)
    return values * below, below + values * density


def softmax_head(queries, keys, alive):
    raw = lax.dot_general(
        queries, keys, (((1,), (1,)), ((), ())), preferred_element_type=jnp.float32
    ) * HEAD ** (-0.5)
    scores = jnp.where(alive, raw, MASKED_FILL)
    expo = jnp.exp(scores - jnp.max(scores, axis=-1, keepdims=True))
    return expo / jnp.sum(expo, axis=-1, keepdims=True)


def attend_kernel(length_ref, query_ref, key_ref, value_ref, context_ref):
    tokens = query_ref.shape[0]
    alive = lax.broadcasted_iota(jnp.int32, (tokens, tokens), 1) < length_ref[pl.program_id(0)]
    contexts = []
    for start in (0, HEAD):
        part = slice(start, start + HEAD)
        attention = softmax_head(query_ref[:, part], key_ref[:, part], alive)
        contexts.append(product(attention.astype(jnp.bfloat16), value_ref[:, part]))
    context_ref[...] = jnp.concatenate(contexts, axis=1).astype(jnp.bfloat16)


def attend_back_kernel(length_ref, query_ref, key_ref, value_ref, grad_ref, query_out, key_out, value_out):
    tokens = query_ref.shape[0]
    alive = lax.broadcasted_iota(jnp.int32, (tokens, tokens), 1) < length_ref[pl.program_id(0)]
    outs = ([], [], [])
    for start in (0, HEAD):
        part = slice(start, start + HEAD)
        queries, keys, values = query_ref[:, part], key_ref[:, part], value_ref[:, part]
        grad = grad_ref[:, part]
        attention = softmax_head(queries, keys, alive)
        grad_attention = product_right(grad, values)
        grad_scores = attention * (
            grad_attention - jnp.sum(grad_attention * attention, axis=-1, keepdims=True)
        )
        grad_raw = (grad_scores.astype(jnp.bfloat16).astype(jnp.float32) * HEAD ** (-0.5)).astype(
            jnp.bfloat16
        )
        outs[0].append(product(grad_raw, keys))
        outs[1].append(product_left(grad_raw, queries))
        outs[2].append(product_left(attention.astype(jnp.bfloat16), grad))
    for out_ref, pair in zip((query_out, key_out, value_out), outs):
        out_ref[...] = jnp.concatenate(pair, axis=1).astype(jnp.bfloat16)


def head_specs(tokens, pairs, count):
    return [
        pl.BlockSpec((tokens, LANES), lambda s, h, lengths, k=k: (s, k * pairs + h))
        for k in range(count)
    ]


def attend(lengths, mixed, tokens):
    width = mixed.shape[1] // 3
    pairs = width // LANES
    rows = mixed.shape[0]
    return pl.pallas_call(
        attend_kernel,
        grid_spec=pltpu.PrefetchScalarGridSpec(
            num_scalar_prefetch=1,
            grid=(rows // tokens, pairs),
            in_specs=head_specs(tokens, pairs, 3),
            out_specs=head_specs(tokens, pairs, 1)[0],
        ),
        out_shape=jax.ShapeDtypeStruct((rows, width), jnp.bfloat16),
        compiler_params=pltpu.CompilerParams(vmem_limit_bytes=32 << 20),
        cost_estimate=pl.CostEstimate(
            flops=8 * rows * tokens * width,
            bytes_accessed=8 * rows * width,
            transcendentals=rows * tokens * width // HEAD,
        ),
    )(lengths, mixed, mixed, mixed)


def attend_back(lengths, mixed, grad_context, tokens):
    width = mixed.shape[1] // 3
    pairs = width // LANES
    rows = mixed.shape[0]
    out = jax.ShapeDtypeStruct((rows, width), jnp.bfloat16)
    return pl.pallas_call(
        attend_back_kernel,
        grid_spec=pltpu.PrefetchScalarGridSpec(
            num_scalar_prefetch=1,
            grid=(rows // tokens, pairs),
            in_specs=head_specs(tokens, pairs, 3) + head_specs(tokens, pairs, 1),
            out_specs=head_specs(tokens, pairs, 1) * 3,
        ),
        out_shape=(out, out, out),
        compiler_params=pltpu.CompilerParams(vmem_limit_bytes=32 << 20),
        cost_estimate=pl.CostEstimate(
            flops=20 * rows * tokens * width,
            bytes_accessed=14 * rows * width,
            transcendentals=rows * tokens * width // HEAD,
        ),
    )(lengths, mixed, mixed, mixed, grad_context)


def one_hot(count, index):
    return (
        lax.broadcasted_iota(jnp.int32, (count, index.shape[0]), 0) == index[None, :]
    ).astype(jnp.bfloat16)


def exact(left, right):
    return jnp.dot(left, right, precision=lax.Precision.HIGHEST, preferred_element_type=jnp.float32)


def shards(
    token_ids,
    seq_lengths,
    mlm_slots,
    mlm_labels,
    nsp_labels,
    *weights,
):
    masters, firsts, seconds = weights[0::3], weights[1::3], weights[2::3]
    (
        table_master,
        position_master,
        pair_master,
        input_master,
        output_master,
        dense_master,
        feed_master,
        vector_master,
    ) = masters
    micro, local, tokens = token_ids.shape
    slots_each = mlm_slots.shape[2]
    devices = lax.axis_size(AXES)
    me = lax.axis_index(AXES)
    seqs = micro * local
    total = seqs * tokens
    picked = seqs * slots_each
    depth, width = input_master.shape[0], output_master.shape[1]
    inner_width = feed_master.shape[2]
    vocab_rows = table_master.shape[0]
    low = jnp.bfloat16
    places = jnp.arange(tokens, dtype=jnp.int32)

    id_rows = total // LANES
    pack_rows = -(-(id_rows + 3 * seqs) // 8) * 8
    packed = pl.pallas_call(
        pack_kernel,
        out_shape=jax.ShapeDtypeStruct((pack_rows, LANES), jnp.int32),
        in_specs=[pl.BlockSpec(memory_space=pltpu.SMEM)]
        + [pl.BlockSpec(memory_space=pltpu.VMEM)] * 3,
    )(seq_lengths, token_ids, mlm_slots, mlm_labels)
    shared = share_small(packed)
    all_ids = shared[:, :id_rows].reshape(devices * seqs, tokens)
    all_slots, all_labels = (
        shared[:, id_rows + k * seqs : id_rows + (k + 1) * seqs, :slots_each] for k in (0, 1)
    )
    all_lengths = shared[:, id_rows + 2 * seqs : id_rows + 3 * seqs, :1]
    all_counted = (all_slots < all_lengths).astype(jnp.float32).reshape(-1)
    all_labels = all_labels.reshape(-1)
    masked_count = jnp.sum(all_counted)
    inv_count = 1.0 / masked_count
    inv_seqs = 1.0 / (devices * seqs)

    table_low = table_master.astype(low)
    vector_each = vector_master.shape[0]
    vector_columns = -(-vector_each // depth)
    small_used = tokens + 4 + vector_columns
    small_columns = -(-small_used // LANES) * LANES
    small_low = jnp.concatenate(
        [
            position_master.T,
            jnp.moveaxis(pair_master, 0, 1).reshape(depth, 4),
            jnp.pad(vector_master, (0, depth * vector_columns - vector_each)).reshape(
                depth, vector_columns
            ),
            jnp.zeros((depth, small_columns - small_used), jnp.float32),
        ],
        axis=1,
    ).astype(low)
    first_group = Gather([input_master.astype(low), small_low, output_master.astype(low)])
    first_group.line()

    lane_rows = -(-vocab_rows // LANES)

    def split_ids(ids, alive):
        owner = ids // vocab_rows
        within = ids - owner * vocab_rows
        high = owner * lane_rows + within // LANES
        return owner, jnp.where(alive, high, -1), within % LANES

    _, all_high, all_low = split_ids(
        all_ids, places[None, :] < all_lengths.reshape(devices * seqs, 1)
    )
    hits = product_right(
        one_hot(devices * lane_rows, all_high.reshape(-1)), one_hot(LANES, all_low.reshape(-1))
    )
    used = (hits > 0).astype(jnp.float32)
    lane = jnp.arange(LANES)
    before = exact(used, (lane[:, None] < lane[None, :]).astype(jnp.float32))
    row_totals = jnp.sum(used, axis=1).reshape(devices, lane_rows)
    row_index = jnp.arange(lane_rows)
    earlier = jnp.sum(
        jnp.where(row_index[None, :, None] < row_index[None, None, :], row_totals[:, :, None], 0.0),
        axis=1,
    )
    rank = before + earlier.reshape(-1, 1)
    most = jnp.max(jnp.sum(row_totals, axis=1)).astype(jnp.int32)
    ahead = ROWS_AHEAD
    rounds = -(-most // ahead)

    lengths = seq_lengths.reshape(-1)
    my_alive = (places[None, :] < lengths[:, None]).reshape(-1)
    my_owner, my_high, my_low = split_ids(token_ids.reshape(-1), my_alive)
    looked = exact(rank.T, one_hot(devices * lane_rows, my_high).astype(jnp.float32))
    my_rank = jnp.sum(looked * one_hot(LANES, my_low).astype(jnp.float32), axis=0).astype(jnp.int32)

    own_rank = lax.dynamic_slice_in_dim(rank, me * lane_rows, lane_rows, 0).reshape(-1)[:vocab_rows]
    own_used = lax.dynamic_slice_in_dim(used, me * lane_rows, lane_rows, 0).reshape(-1)[:vocab_rows]
    own_slot = jnp.where(own_used > 0, own_rank.astype(jnp.int32), -1)

    def picks(start):
        own = one_hot(ahead, jnp.where(own_slot >= start, own_slot - start, -1))
        inside = my_alive & (my_rank >= start) & (my_rank < start + ahead)
        mine = one_hot(devices * ahead, jnp.where(inside, my_owner * ahead + my_rank - start, -1))
        return own, mine

    own_first, mine_first = picks(0)
    word_group = Gather([product(own_first, table_low).astype(low)])
    word_line = word_group.line()
    first_group.plane()
    late = pin(
        [
            feed_master[0].astype(low),
            feed_master[1].astype(low),
            dense_master[0].astype(low),
            dense_master[1].astype(low),
        ],
        word_line,
    )
    second_group = Gather(late)
    second_group.line()
    word_group.plane()
    input_all, small_all, output_all = first_group.finish()
    (word_rows,) = word_group.finish()
    words = product_left(mine_first, word_rows)

    def fetch_more(state):
        turn, words = state
        own, mine = picks(turn * ahead)
        rows = lax.all_gather(product(own, table_low).astype(low), AXES, axis=0, tiled=True)
        return turn + 1, words + product_left(mine, rows)

    _, words = lax.while_loop(lambda state: state[0] < rounds, fetch_more, (jnp.int32(1), words))

    position = small_all[:, :tokens].T.astype(jnp.float32)
    pair_cols = jnp.moveaxis(small_all[:, tokens : tokens + 4].reshape(width, 2, 2), 1, 0)
    vectors = small_all[:, tokens + 4 : small_used].reshape(devices, depth * vector_columns)
    parts = split_vectors(vectors[:, :vector_each].reshape(-1).astype(jnp.float32))

    second = (places[None, :] >= lengths[:, None] // 2).reshape(-1)
    type_cols = pair_cols[0].astype(jnp.float32)
    embedded = (
        words
        + jnp.tile(position, (seqs, 1))
        + jnp.where(second[:, None], type_cols[:, 1], type_cols[:, 0])
    )
    normed, saved_zero = norm_forward(embedded, parts[0], parts[1])
    normed_low = normed.astype(low)
    bias_mixed = jnp.concatenate([parts[8], jnp.zeros((width,), jnp.float32), parts[9]])
    mixed = (product(normed_low, input_all) + bias_mixed).astype(low)
    second_group.pieces = pin(second_group.plane(), mixed)
    context_low = attend(lengths, mixed, tokens)
    feed_in, feed_out, dense_one, dense_two = second_group.finish()
    branch = product(context_low, output_all) + parts[10]
    hidden_one, saved_one = norm_forward(normed + branch, parts[2], parts[3])
    one_low = hidden_one.astype(low)
    active, slope = gelu_parts(product(one_low, feed_in) + parts[11])
    active_low, slope = lax.optimization_barrier((active.astype(low), slope))
    outer = product_right(active_low, feed_out) + parts[12]
    hidden_two, saved_two = norm_forward(hidden_one + outer, parts[4], parts[5])
    two_low = hidden_two.astype(low)

    my_slots = mlm_slots.reshape(seqs, slots_each) + tokens * jnp.arange(seqs, dtype=jnp.int32)[:, None]
    slot_hot = one_hot(total, my_slots.reshape(-1))
    picked_low = product_left(slot_hot, two_low).astype(low)
    lifted, head_slope = gelu_parts(product(picked_low, dense_one) + parts[13])
    head_out, saved_head = norm_forward(lifted, parts[6], parts[7])
    head_group = Gather([head_out.astype(low)])
    head_group.line()
    head_group.plane()

    first_hot = one_hot(total, tokens * jnp.arange(seqs, dtype=jnp.int32))
    first_low = product_left(first_hot, two_low).astype(low)
    pooled = jnp.tanh(product(first_low, dense_two) + parts[14])
    pooled_low = pooled.astype(low)
    pair_logits = product(pooled_low, pair_cols[1])
    pair_top = jnp.max(pair_logits, axis=-1, keepdims=True)
    pair_total = pair_top + jnp.log(
        jnp.sum(jnp.exp(pair_logits - pair_top), axis=-1, keepdims=True)
    )
    pair_hit = jnp.arange(2, dtype=jnp.int32)[None, :] == nsp_labels.reshape(-1, 1)
    pair_local = jnp.sum(pair_total[:, 0] - jnp.sum(jnp.where(pair_hit, pair_logits, 0.0), axis=1))

    vocab_bias = lax.dynamic_slice_in_dim(parts[15], me * vocab_rows, vocab_rows, 0)
    (heads,) = head_group.finish()
    logits = product_right(heads, table_low) + vocab_bias
    top = jnp.max(logits, axis=-1)
    local_totals = top + jnp.log(jnp.sum(jnp.exp(logits - top[:, None]), axis=-1))
    all_totals = share_small(local_totals.reshape(-1, LANES))
    highest = jnp.max(all_totals, axis=0)
    log_totals = (highest + jnp.log(jnp.sum(jnp.exp(all_totals - highest), axis=0))).reshape(-1)
    vocab_index = me * vocab_rows + jnp.arange(vocab_rows, dtype=jnp.int32)
    masked_shared = jnp.sum(all_counted * log_totals)
    hit = vocab_index[None, :] == all_labels[:, None]
    target_local = jnp.sum(all_counted[:, None] * jnp.where(hit, logits, 0.0))
    grad_logits = (
        (jnp.exp(logits - log_totals[:, None]) - hit.astype(jnp.float32))
        * (all_counted * inv_count)[:, None]
    ).astype(low)
    grad_heads = product(grad_logits, table_low).reshape(devices, picked, width)
    middle = width // 2
    head_sum = Scatter([(grad_heads[:, :, :middle], 0), (grad_heads[:, :, middle:], 1)])
    sent = head_sum.send()
    grad_table = product_left(pin(grad_logits, sent), heads)
    head_sum.receive()
    for _ in range(1, bits_of(lax.axis_size("wide"))):
        head_sum.step()
    grad_vocab = jnp.sum(grad_logits.astype(jnp.float32), axis=0)
    vocab_pad = -(-vocab_rows // (8 * LANES)) * 8 * LANES
    all_vocab = share_small(jnp.pad(grad_vocab, (0, vocab_pad - vocab_rows)).reshape(-1, LANES))
    grad_head = jnp.concatenate(head_sum.line(), axis=1)

    def owners(values):
        return values.reshape(devices, -1, values.shape[1])

    def column_sum(values):
        return jnp.sum(values.astype(jnp.float32), axis=0, keepdims=True)

    grad_gelu, grad_head_gain, grad_head_shift = norm_backward(grad_head, saved_head, parts[6])
    grad_transform = (grad_gelu * head_slope).astype(low)
    grad_dense_zero = product_left(picked_low, grad_transform)
    grad_pair_logits = (
        (jnp.exp(pair_logits - pair_total) - pair_hit.astype(jnp.float32)) * inv_seqs
    ).astype(low)
    grad_classifier = product_left(pooled_low, grad_pair_logits)
    grad_pooled = product_right(grad_pair_logits, pair_cols[1])
    grad_pool_pre = (grad_pooled * (1.0 - pooled * pooled)).astype(low)
    grad_pooler = product_left(first_low, grad_pool_pre)
    grad_two = exact(
        slot_hot.astype(jnp.float32), product_right(grad_transform, dense_one)
    ) + exact(first_hot.astype(jnp.float32), product_right(grad_pool_pre, dense_two))
    grad_sum_two, grad_feed_gain, grad_feed_shift = norm_backward(grad_two, saved_two, parts[4])
    grad_outer = grad_sum_two.astype(low)
    grad_feed_out = product_left(grad_outer, active_low)
    grad_inner = (product(grad_outer, feed_out) * slope).astype(low)
    grad_feed_in = product_left(one_low, grad_inner)
    feed_sum = Scatter(
        [
            (owners(grad_feed_in), 0),
            (owners(grad_dense_zero), 0),
            (owners(grad_feed_out), 1),
            (owners(grad_pooler), 1),
        ]
    )
    sent = feed_sum.send()
    grad_one = grad_sum_two + product_right(pin(grad_inner, sent), feed_in)
    grad_sum_one, grad_attend_gain, grad_attend_shift = norm_backward(grad_one, saved_one, parts[2])
    grad_branch = grad_sum_one.astype(low)
    grad_context = product_right(grad_branch, output_all).astype(low)
    came = feed_sum.receive()
    sent = feed_sum.send()
    grad_context = pin(grad_context, came, sent)
    grad_q, grad_k, grad_v = attend_back(lengths, mixed, grad_context, tokens)
    grad_mixed = jnp.concatenate([grad_q, grad_k, grad_v], axis=1)
    came = feed_sum.receive()
    sent = feed_sum.send()
    grad_mixed = pin(grad_mixed, came, sent)
    grad_normed = grad_sum_one + product_right(grad_mixed, input_all)
    grad_embedded, grad_embed_gain, grad_embed_shift = norm_backward(
        grad_normed, saved_zero, parts[0]
    )
    embedded_low = grad_embedded.astype(low)
    grad_words = product(mine_first, embedded_low).reshape(devices, ahead, width)
    grad_input = product_left(normed_low, grad_mixed)
    grad_output = product_left(context_low, grad_branch)
    while feed_sum.dims[0]:
        feed_sum.receive()
        if feed_sum.dims[0]:
            feed_sum.send()
    in_second = second[:, None]
    rows = [
        jnp.sum(jnp.where(in_second, 0.0, grad_embedded), axis=0, keepdims=True),
        jnp.sum(jnp.where(in_second, grad_embedded, 0.0), axis=0, keepdims=True),
        grad_classifier.T,
    ]
    vector_rows = [
        grad_embed_gain[None],
        grad_embed_shift[None],
        grad_attend_gain[None],
        grad_attend_shift[None],
        grad_feed_gain[None],
        grad_feed_shift[None],
        grad_head_gain[None],
        grad_head_shift[None],
        column_sum(grad_q),
        column_sum(grad_v),
        column_sum(grad_branch),
        column_sum(grad_inner).reshape(-1, width),
        column_sum(grad_outer),
        column_sum(grad_transform),
        column_sum(grad_pool_pre),
    ]
    vector_count = sum(item.shape[0] for item in vector_rows)
    grad_position = jnp.sum(grad_embedded.reshape(seqs, tokens, width), axis=0).T
    grad_small = jnp.concatenate([grad_position, stack_columns(rows + vector_rows)], axis=1)
    last_sum = Scatter(
        [
            (owners(grad_input), 0),
            (owners(grad_output), 1),
            (owners(grad_small), 1),
            (grad_words[:, :, :middle], 0),
            (grad_words[:, :, middle:], 1),
        ]
    )
    for _ in range(bits_of(lax.axis_size("wide"))):
        last_sum.step()
    sum_feed_in, sum_dense, sum_feed_out, sum_pooler = feed_sum.line()
    sum_input, sum_output, sum_small, words_left, words_right = last_sum.line()
    grad_table = grad_table + exact(
        own_first.T.astype(jnp.float32), jnp.concatenate([words_left, words_right], axis=1)
    )

    def return_more(state):
        turn, grad_table = state
        own, mine = picks(turn * ahead)
        back = lax.psum_scatter(
            product(mine, embedded_low), AXES, scatter_dimension=0, tiled=True
        )
        return turn + 1, grad_table + exact(own.T.astype(jnp.float32), back)

    _, grad_table = lax.while_loop(
        lambda state: state[0] < rounds, return_more, (jnp.int32(1), grad_table)
    )

    sum_vector = sum_small[:, tokens + 4 : tokens + 4 + vector_count]
    pieces = [
        grad_table,
        sum_small[:, :tokens],
        jnp.moveaxis(sum_small[:, tokens : tokens + 4].reshape(depth, 2, 2), 1, 0),
        sum_input,
        sum_output,
        jnp.stack([sum_dense, sum_pooler]),
        jnp.stack([sum_feed_in, sum_feed_out]),
    ]
    squares = sum((jnp.sum(item * item) for item in pieces + [sum_vector, grad_vocab]))
    payload = jnp.concatenate(
        [
            jnp.stack([squares, target_local, pair_local]),
            jnp.zeros((LANES - 3,), jnp.float32),
            sum_vector.reshape(-1),
        ]
    )
    payload_pad = -(-payload.shape[0] // LANES) * LANES
    answers = share_small(
        jnp.pad(payload, (0, payload_pad - payload.shape[0])).reshape(-1, LANES)
    )
    totals = jnp.sum(answers[:, 0, :3], axis=0)
    grad_vector = jnp.concatenate(
        [
            answers.reshape(devices, -1)[:, LANES : LANES + depth * vector_count]
            .reshape(devices * depth, vector_count)
            .T.reshape(-1),
            all_vocab.reshape(devices, -1)[:, :vocab_rows].reshape(-1),
        ]
    )
    pieces.append(lax.dynamic_slice_in_dim(grad_vector, me * vector_each, vector_each, 0))
    norm = jnp.sqrt(totals[0])
    masked_total = masked_shared - totals[1]
    pair_total_sum = totals[2]
    factor = CLIP_NORM / (norm + 1e-06)
    correct_one = 1.0 - BETA_ONE**STEP_COUNT
    correct_two = 1.0 - BETA_TWO**STEP_COUNT
    updated = []
    for number in range(8):
        turned = (lambda item: item.T) if number == 1 else (lambda item: item)
        master = turned(masters[number])
        grad = pieces[number] * factor
        moment_one = BETA_ONE * turned(firsts[number]) + (1.0 - BETA_ONE) * grad
        moment_two = BETA_TWO * turned(seconds[number]) + (1.0 - BETA_TWO) * grad * grad
        direction = moment_one / correct_one / (jnp.sqrt(moment_two / correct_two) + ADAM_EPS)
        decay = DECAY_RATE if number < 7 else 0.0
        updated.extend(
            [
                turned(master - LEARN_RATE * (direction + decay * master)),
                turned(moment_one),
                turned(moment_two),
            ]
        )
    masked_sums = jnp.stack([masked_total, masked_count])
    return (masked_sums, pair_total_sum, norm) + tuple(updated)


def solution(mesh):
    placed = (
        P(None, ("wide", "narrow"), None),
        P(None, ("wide", "narrow")),
        P(None, ("wide", "narrow"), None),
        P(None, ("wide", "narrow"), None),
        P(None, ("wide", "narrow")),
        P(("wide", "narrow"), None),
        P(("wide", "narrow"), None),
        P(("wide", "narrow"), None),
        P(None, ("wide", "narrow")),
        P(None, ("wide", "narrow")),
        P(None, ("wide", "narrow")),
        P(None, ("wide", "narrow"), None),
        P(None, ("wide", "narrow"), None),
        P(None, ("wide", "narrow"), None),
        P(("wide", "narrow"), None),
        P(("wide", "narrow"), None),
        P(("wide", "narrow"), None),
        P(("wide", "narrow"), None),
        P(("wide", "narrow"), None),
        P(("wide", "narrow"), None),
        P(None, ("wide", "narrow"), None),
        P(None, ("wide", "narrow"), None),
        P(None, ("wide", "narrow"), None),
        P(None, ("wide", "narrow"), None),
        P(None, ("wide", "narrow"), None),
        P(None, ("wide", "narrow"), None),
        P(("wide", "narrow")),
        P(("wide", "narrow")),
        P(("wide", "narrow")),
    )
    return jax.shard_map(
        shards,
        mesh=mesh,
        in_specs=placed,
        out_specs=(
            P(),
            P(),
            P(),
            P(("wide", "narrow"), None),
            P(("wide", "narrow"), None),
            P(("wide", "narrow"), None),
            P(None, ("wide", "narrow")),
            P(None, ("wide", "narrow")),
            P(None, ("wide", "narrow")),
            P(None, ("wide", "narrow"), None),
            P(None, ("wide", "narrow"), None),
            P(None, ("wide", "narrow"), None),
            P(("wide", "narrow"), None),
            P(("wide", "narrow"), None),
            P(("wide", "narrow"), None),
            P(("wide", "narrow"), None),
            P(("wide", "narrow"), None),
            P(("wide", "narrow"), None),
            P(None, ("wide", "narrow"), None),
            P(None, ("wide", "narrow"), None),
            P(None, ("wide", "narrow"), None),
            P(None, ("wide", "narrow"), None),
            P(None, ("wide", "narrow"), None),
            P(None, ("wide", "narrow"), None),
            P(("wide", "narrow")),
            P(("wide", "narrow")),
            P(("wide", "narrow")),
        ),
        check_vma=False,
    )
```

```python
from functools import partial

import jax
import jax.numpy as jnp
from jax import lax
from jax.experimental import pallas as pl
from jax.experimental.pallas import tpu as pltpu
from jax.sharding import PartitionSpec as P

D = 768
HEAD = 64
FF = 3072
STEP_COUNT = 10


NORM_EPS = 1e-12
CLIP_NORM = 0.02
BETA_ONE = 0.9
BETA_TWO = 0.999
ADAM_EPS = 1e-08
DECAY_RATE = 0.01
LEARN_RATE = 0.1
MASKED_FILL = -1000000000.0
AXES = ("wide", "narrow")
ROWS_AHEAD = 96
LANES = 128


def product(left, right):
    return jnp.dot(left, right, preferred_element_type=jnp.float32)


def product_right(left, right):
    return lax.dot_general(
        left, right, (((1,), (1,)), ((), ())), preferred_element_type=jnp.float32
    )


def product_left(left, right):
    return lax.dot_general(
        left, right, (((0,), (0,)), ((), ())), preferred_element_type=jnp.float32
    )


def norm_forward(values, gain, shift):
    average = jnp.mean(values, axis=-1, keepdims=True)
    centered = values - average
    spread = jnp.mean(centered * centered, axis=-1, keepdims=True)
    inverse = lax.rsqrt(spread + NORM_EPS)
    normal = centered * inverse
    return (normal * gain + shift, (normal, inverse))


def norm_backward(grad, saved, gain):
    normal, inverse = saved
    scaled = grad * gain
    inner = (
        scaled
        - jnp.mean(scaled, axis=-1, keepdims=True)
        - normal * jnp.mean(scaled * normal, axis=-1, keepdims=True)
    )
    return (inner * inverse, jnp.sum(grad * normal, axis=0), jnp.sum(grad, axis=0))


def gelu_exact(values):
    return jax.nn.gelu(values, approximate=False)


def gelu_back(values, grad):
    return jax.vjp(gelu_exact, values)[1](grad)[0]


def split_vectors(vectors):
    extents = [D] * 11 + [FF] + [D] * 3
    pieces = []
    start = 0
    for extent in extents:
        pieces.append(vectors[start : start + extent])
        start += extent
    pieces.append(vectors[start:])
    return pieces


def bits_of(size):
    return size.bit_length() - 1


def orders():
    far = [("wide", bit) for bit in range(1, bits_of(lax.axis_size("wide")))]
    return far, far[::-1]


CORE = ("wide", 0)


def my_bit(dim):
    return (lax.axis_index(dim[0]) >> dim[1]) & 1


def swap(values, dim):
    size = lax.axis_size(dim[0])
    return lax.ppermute(values, dim[0], [(i, i ^ (1 << dim[1])) for i in range(size)])


def pin(values, *others):
    return lax.optimization_barrier((values, others))[0]


def place_blocks(spreads, starts, middle, me_ref, *refs):
    count = len(spreads[0])
    outs = refs[8 : 8 + len(starts) - 1]
    held = refs[8 + len(outs) : 10 + len(outs)]
    arrive, leave = refs[10 + len(outs) :]
    me = me_ref[0]
    inward, outward = [], []
    for side in range(2):
        pieces = refs[4 * side : 4 * side + 4]
        each = pieces[0].shape[0]
        left = 0 if side == 0 else middle
        right = middle if side == 0 else starts[-1]
        for code, offset in enumerate(spreads[side]):
            number = side * count + code
            inward.append(
                pltpu.make_async_copy(
                    pieces[code // each].at[code % each], held[side].at[code], arrive.at[number]
                )
            )
            group = []
            for out_ref, start, stop in zip(outs, starts, starts[1:]):
                low, high = max(start, left), min(stop, right)
                if low < high:
                    group.append(
                        pltpu.make_async_copy(
                            held[side].at[code, :, :, low - left : high - left],
                            out_ref.at[me ^ offset, :, :, low - start : high - start],
                            leave.at[number, len(group)],
                        )
                    )
            outward.append(group)
    for copy in inward:
        copy.start()
    for first, group in zip(inward, outward):
        first.wait()
        for copy in group:
            copy.start()
    for group in outward:
        for copy in group:
            copy.wait()


def reach(values, step):
    size = lax.axis_size("narrow")
    return lax.ppermute(values, "narrow", [(z, z ^ step) for z in range(size)])


class Gather:
    def __init__(self, arrays):
        self.columns = [array.shape[1] for array in arrays]
        self.rows = arrays[0].shape[0]
        total = sum(self.columns)
        self.middle = total // 2 // LANES * LANES
        self.packed = jnp.concatenate(arrays, axis=1) if len(arrays) > 1 else arrays[0]

    def line(self, *before):
        size = lax.axis_size("narrow")
        me = lax.axis_index("narrow")
        arrived = pin([reach(self.packed, step) for step in range(1, size)], *before)
        blocks = []
        for spot in range(size):
            chosen = self.packed
            for step in range(1, size):
                chosen = jnp.where(me == spot ^ step, arrived[step - 1], chosen)
            blocks.append(chosen)
        self.halves = [
            jnp.stack([block[:, : self.middle] for block in blocks])[None],
            jnp.stack([block[:, self.middle :] for block in blocks])[None],
        ]
        return self.halves

    def plane(self):
        self.pieces = []
        for held, order in zip(self.halves, orders()):
            for dim in order[:-1]:
                held = jnp.concatenate([held, swap(held, dim)], axis=0)
            self.pieces.append([held, swap(held, order[-1])])
        return self.pieces

    def core(self):
        self.pieces = [half + [swap(piece, CORE) for piece in half] for half in self.pieces]
        return self.pieces

    def finish(self):
        pieces = self.pieces
        count = lax.axis_size("wide")
        spreads = [
            [
                sum(((code >> k) & 1) << dim[1] for k, dim in enumerate(order + [CORE]))
                for code in range(count)
            ]
            for order in orders()
        ]
        starts = [sum(self.columns[:k]) for k in range(len(self.columns) + 1)]
        line = lax.axis_size("narrow")
        dtype = self.packed.dtype
        me = lax.axis_index("wide").astype(jnp.int32).reshape(1)
        moved = 2 * count * line * self.rows * starts[-1] * dtype.itemsize
        outs = pl.pallas_call(
            partial(place_blocks, spreads, starts, self.middle),
            out_shape=tuple(
                jax.ShapeDtypeStruct((count, line, self.rows, columns), dtype)
                for columns in self.columns
            ),
            in_specs=[pl.BlockSpec(memory_space=pltpu.SMEM)]
            + [pl.BlockSpec(memory_space=pl.ANY)] * 8,
            out_specs=(pl.BlockSpec(memory_space=pl.ANY),) * len(self.columns),
            scratch_shapes=[
                pltpu.VMEM((count, line, self.rows, self.middle), dtype),
                pltpu.VMEM((count, line, self.rows, starts[-1] - self.middle), dtype),
                pltpu.SemaphoreType.DMA((2 * count,)),
                pltpu.SemaphoreType.DMA((2 * count, len(self.columns))),
            ],
            compiler_params=pltpu.CompilerParams(vmem_limit_bytes=40 << 20),
            cost_estimate=pl.CostEstimate(flops=0, bytes_accessed=moved, transcendentals=0),
        )(me, *pieces[0], *pieces[1])
        return [out.reshape(count * line * self.rows, -1) for out in outs]


class Scatter:
    def __init__(self, items):
        wide, line = lax.axis_size("wide"), lax.axis_size("narrow")
        self.terms, self.dims, self.fixed = [], [], []
        for blocks, which in items:
            labels = tuple(("wide", bit) for bit in range(bits_of(wide)))[::-1]
            shape = (2,) * bits_of(wide) + (line,) + blocks.shape[1:]
            self.terms.append([(blocks.reshape(shape), labels)])
            self.dims.append([CORE] + orders()[which][::-1])
            self.fixed.append({})

    def cut(self, number, fixed):
        total = None
        for array, labels in self.terms[number]:
            starts = [fixed.get(label, 0) for label in labels]
            sizes = [1 if label in fixed else 2 for label in labels]
            starts += [0, 0, 0]
            sizes += list(array.shape[-3:])
            starts = [jnp.asarray(start, jnp.int32) for start in starts]
            kept = [2 for label in labels if label not in fixed] + sizes[-3:]
            part = lax.dynamic_slice(array, starts, sizes).reshape(kept).astype(jnp.float32)
            total = part if total is None else total + part
        return total

    def send(self):
        self.away = []
        for number, dims in enumerate(self.dims):
            fixed = dict(self.fixed[number])
            fixed[dims[0]] = 1 - my_bit(dims[0])
            self.away.append(self.cut(number, fixed).astype(jnp.bfloat16))
        return self.away

    def receive(self):
        arrived = []
        for number, away in enumerate(self.away):
            dim = self.dims[number].pop(0)
            self.fixed[number][dim] = my_bit(dim)
            arrived.append(swap(away, dim))
            labels = self.terms[number][0][1]
            left = tuple(label for label in labels if label not in self.fixed[number])
            self.terms[number].append((arrived[-1], left))
        return arrived

    def step(self):
        self.send()
        return self.receive()

    def hold(self, *others):
        arrays = pin([[term[0] for term in terms] for terms in self.terms], *others)
        self.terms = [
            [(array, term[1]) for array, term in zip(held, terms)]
            for held, terms in zip(arrays, self.terms)
        ]

    def line(self):
        size = lax.axis_size("narrow")
        me = lax.axis_index("narrow")
        depth = min(terms[0][0].shape[-2] for terms in self.terms)
        sums = [self.cut(number, fixed) for number, fixed in enumerate(self.fixed)]
        sums = lax.optimization_barrier(sums)

        def columns_of(spot):
            flat = []
            for item in sums:
                block = lax.dynamic_index_in_dim(item, spot, 0, keepdims=False)
                flat.extend(block[k : k + depth] for k in range(0, block.shape[0], depth))
            return jnp.concatenate(flat, axis=1) if len(flat) > 1 else flat[0]

        self.goes = [columns_of(me ^ step).astype(jnp.bfloat16) for step in range(1, size)]
        self.own = columns_of(me)
        return self.goes

    def finish(self, *before):
        arrived = [reach(item, step + 1) for step, item in enumerate(self.goes)]
        arrived = pin(arrived, *before)
        depth = self.own.shape[0]
        total = self.own + sum(item.astype(jnp.float32) for item in arrived)
        results, start = [], 0
        for terms in self.terms:
            parts, columns = terms[0][0].shape[-2] // depth, terms[0][0].shape[-1]
            pieces = [
                total[:, start + k * columns : start + (k + 1) * columns] for k in range(parts)
            ]
            start += parts * columns
            results.append(jnp.concatenate(pieces, axis=0) if parts > 1 else pieces[0])
        return results


def share_small(values):
    count = lax.axis_size(AXES)
    spread = jnp.broadcast_to(values[None], (count,) + values.shape)
    return lax.all_to_all(spread, AXES, 0, 0)


def pack_kernel(length_ref, ids_ref, slot_ref, label_ref, out_ref):
    out_ref[...] = jnp.zeros_like(out_ref)
    micro, local, tokens = ids_ref.shape
    slots = slot_ref.shape[2]
    row = 0
    for index in range(micro * local):
        for start in range(0, tokens, LANES):
            out_ref[row : row + 1, :] = ids_ref[
                index // local, index % local : index % local + 1, start : start + LANES
            ]
            row += 1
    for ref in (slot_ref, label_ref):
        for index in range(micro * local):
            out_ref[row : row + 1, :slots] = ref[
                index // local, index % local : index % local + 1, :
            ]
            row += 1
    for index in range(micro * local):
        out_ref[row : row + 1, :] = jnp.full(
            (1, LANES), length_ref[index // local, index % local], jnp.int32
        )
        row += 1


def norm_back_rows(grad, normal, inverse, gain):
    scaled = grad * gain
    inner = (
        scaled
        - jnp.mean(scaled, axis=-1, keepdims=True)
        - normal * jnp.mean(scaled * normal, axis=-1, keepdims=True)
    )
    return (
        inner * inverse,
        jnp.sum(grad * normal, axis=0, keepdims=True),
        jnp.sum(grad, axis=0, keepdims=True),
    )


SMALL_ROWS = 32
VECTOR_AT = 4


def feed_back_kernel(
    grad_ref,
    normal_two_ref,
    inverse_two_ref,
    gain_two_ref,
    slope_ref,
    out_proj_ref,
    in_proj_ref,
    normal_one_ref,
    inverse_one_ref,
    gain_one_ref,
    attend_proj_ref,
    outer_ref,
    inner_ref,
    sum_ref,
    branch_ref,
    context_ref,
    rows_ref,
):
    @pl.when(pl.program_id(0) == 0)
    def _():
        rows_ref[...] = jnp.zeros_like(rows_ref)

    def add_row(place, row):
        at = VECTOR_AT + place
        rows_ref[at : at + 1, :] = rows_ref[at : at + 1, :] + row

    def column_sum(values):
        return jnp.sum(values.astype(jnp.float32), axis=0, keepdims=True)

    width = grad_ref.shape[1]
    grad, gain_sum, shift_sum = norm_back_rows(
        grad_ref[...], normal_two_ref[...], inverse_two_ref[...], gain_two_ref[...]
    )
    add_row(4, gain_sum)
    add_row(5, shift_sum)
    outer = grad.astype(jnp.bfloat16)
    outer_ref[...] = outer
    add_row(15, column_sum(outer))
    for number, start in enumerate(range(0, slope_ref.shape[1], width)):
        part = slice(start, start + width)
        inner = (product(outer, out_proj_ref[:, part]) * slope_ref[:, part]).astype(jnp.bfloat16)
        inner_ref[:, part] = inner
        add_row(11 + number, column_sum(inner))
        grad = grad + product_right(inner, in_proj_ref[:, part])
    grad, gain_sum, shift_sum = norm_back_rows(
        grad, normal_one_ref[...], inverse_one_ref[...], gain_one_ref[...]
    )
    add_row(2, gain_sum)
    add_row(3, shift_sum)
    sum_ref[...] = grad
    branch = grad.astype(jnp.bfloat16)
    branch_ref[...] = branch
    add_row(10, column_sum(branch))
    context_ref[...] = product_right(branch, attend_proj_ref[...]).astype(jnp.bfloat16)


def feed_back(grad, saved_two, gain_two, slope, feed_out, feed_in, saved_one, gain_one, output_all):
    rows, width = grad.shape
    inner = slope.shape[1]
    tile = 256 if rows % 256 == 0 else rows

    def tiled(columns):
        return pl.BlockSpec((tile, columns), lambda i: (i, 0))

    def whole(array):
        return pl.BlockSpec(array.shape, lambda i: (0, 0), pipeline_mode=pl.Buffered(1))

    low = jnp.bfloat16
    gain_two, gain_one = gain_two[None], gain_one[None]
    return pl.pallas_call(
        feed_back_kernel,
        grid=(rows // tile,),
        in_specs=[
            tiled(width),
            tiled(width),
            tiled(1),
            whole(gain_two),
            tiled(inner),
            whole(feed_out),
            whole(feed_in),
            tiled(width),
            tiled(1),
            whole(gain_one),
            whole(output_all),
        ],
        out_specs=(
            tiled(width),
            tiled(inner),
            tiled(width),
            tiled(width),
            tiled(width),
            pl.BlockSpec((SMALL_ROWS, width), lambda i: (0, 0)),
        ),
        out_shape=(
            jax.ShapeDtypeStruct((rows, width), low),
            jax.ShapeDtypeStruct((rows, inner), low),
            jax.ShapeDtypeStruct((rows, width), jnp.float32),
            jax.ShapeDtypeStruct((rows, width), low),
            jax.ShapeDtypeStruct((rows, width), low),
            jax.ShapeDtypeStruct((SMALL_ROWS, width), jnp.float32),
        ),
        compiler_params=pltpu.CompilerParams(vmem_limit_bytes=56 << 20),
        cost_estimate=pl.CostEstimate(
            flops=2 * rows * width * (2 * inner + width),
            bytes_accessed=rows * (6 * inner + 22 * width) + 2 * width * (2 * inner + width),
            transcendentals=0,
        ),
    )(
        grad,
        *saved_two,
        gain_two,
        slope,
        feed_out,
        feed_in,
        *saved_one,
        gain_one,
        output_all,
    )


def embed_back_kernel(
    length_ref,
    mixed_ref,
    proj_ref,
    sum_ref,
    normal_ref,
    inverse_ref,
    gain_ref,
    feed_rows_ref,
    pair_rows_ref,
    head_gain_ref,
    head_shift_ref,
    transform_ref,
    pool_ref,
    low_ref,
    small_ref,
    position_ref,
    rows_ref,
):
    step = pl.program_id(0)
    tokens, width = sum_ref.shape

    @pl.when(step == 0)
    def _():
        position_ref[...] = jnp.zeros_like(position_ref)
        rows_ref[...] = jnp.zeros_like(rows_ref)
        rows_ref[:SMALL_ROWS, :] = feed_rows_ref[...]
        rows_ref[2:4, :] = pair_rows_ref[...]
        for place, ref in ((6, head_gain_ref), (7, head_shift_ref), (16, transform_ref), (17, pool_ref)):
            rows_ref[VECTOR_AT + place : VECTOR_AT + place + 1, :] = ref[...]

    def add_row(at, row):
        rows_ref[at : at + 1, :] = rows_ref[at : at + 1, :] + row

    def column_sum(values):
        return jnp.sum(values.astype(jnp.float32), axis=0, keepdims=True)

    grad = sum_ref[...]
    for number in range(3):
        grad = grad + product_right(
            mixed_ref[:, number * width : (number + 1) * width],
            proj_ref[:, number * width : (number + 1) * width],
        )
    grad, gain_sum, shift_sum = norm_back_rows(
        grad, normal_ref[...], inverse_ref[...], gain_ref[...]
    )
    low_ref[...] = grad.astype(jnp.bfloat16)
    position_ref[...] = position_ref[...] + grad
    second = lax.broadcasted_iota(jnp.int32, (tokens, 1), 0) >= length_ref[step] // 2
    late = jnp.sum(jnp.where(second, grad, 0.0), axis=0, keepdims=True)
    early = jnp.sum(jnp.where(second, 0.0, grad), axis=0, keepdims=True)
    add_row(0, early)
    add_row(1, late)
    add_row(VECTOR_AT, gain_sum)
    add_row(VECTOR_AT + 1, shift_sum)
    add_row(VECTOR_AT + 8, column_sum(mixed_ref[:, :width]))
    add_row(VECTOR_AT + 9, column_sum(mixed_ref[:, 2 * width :]))

    @pl.when(step == pl.num_programs(0) - 1)
    def _():
        small_ref[:, :tokens] = position_ref[...].T
        small_ref[:, tokens:] = rows_ref[...].T


def embed_back(lengths, grad_mixed, input_all, grad_sum, saved, gain, feed_rows, head_rows, tokens):
    rows, width = grad_sum.shape
    gain = gain[None]

    def tiled(columns):
        return pl.BlockSpec((tokens, columns), lambda i, lengths: (i, 0))

    def whole(array):
        return pl.BlockSpec(
            array.shape, lambda i, lengths: (0, 0), pipeline_mode=pl.Buffered(1)
        )

    small = jax.ShapeDtypeStruct((width, tokens + LANES), jnp.float32)
    return pl.pallas_call(
        embed_back_kernel,
        grid_spec=pltpu.PrefetchScalarGridSpec(
            num_scalar_prefetch=1,
            grid=(rows // tokens,),
            in_specs=[
                tiled(3 * width),
                whole(input_all),
                tiled(width),
                tiled(width),
                tiled(1),
                whole(gain),
                whole(feed_rows),
            ]
            + [whole(item) for item in head_rows],
            out_specs=(tiled(width), whole(small)),
            scratch_shapes=[
                pltpu.VMEM((tokens, width), jnp.float32),
                pltpu.VMEM((LANES, width), jnp.float32),
            ],
        ),
        out_shape=(jax.ShapeDtypeStruct((rows, width), jnp.bfloat16), small),
        compiler_params=pltpu.CompilerParams(vmem_limit_bytes=48 << 20),
        cost_estimate=pl.CostEstimate(
            flops=6 * rows * width * width,
            bytes_accessed=rows * width * 16 + 6 * width * width,
            transcendentals=0,
        ),
    )(lengths, grad_mixed, input_all, grad_sum, *saved, gain, feed_rows, *head_rows)


def gelu_parts(values):
    below = 0.5 + 0.5 * lax.erf(values * (0.5**0.5))
    density = jnp.exp(-0.5 * values * values) * ((0.5 / jnp.pi) ** 0.5)
    return values * below, below + values * density


def softmax_head(queries, keys, alive):
    raw = lax.dot_general(
        queries, keys, (((1,), (1,)), ((), ())), preferred_element_type=jnp.float32
    ) * HEAD ** (-0.5)
    scores = jnp.where(alive, raw, MASKED_FILL)
    expo = jnp.exp(scores - jnp.max(scores, axis=-1, keepdims=True))
    return expo / jnp.sum(expo, axis=-1, keepdims=True)


def attend_kernel(length_ref, query_ref, key_ref, value_ref, context_ref):
    tokens = query_ref.shape[0]
    alive = lax.broadcasted_iota(jnp.int32, (tokens, tokens), 1) < length_ref[pl.program_id(0)]
    contexts = []
    for start in (0, HEAD):
        part = slice(start, start + HEAD)
        attention = softmax_head(query_ref[:, part], key_ref[:, part], alive)
        contexts.append(product(attention.astype(jnp.bfloat16), value_ref[:, part]))
    context_ref[...] = jnp.concatenate(contexts, axis=1).astype(jnp.bfloat16)


def attend_back_kernel(length_ref, query_ref, key_ref, value_ref, grad_ref, out_ref):
    tokens = query_ref.shape[0]
    alive = lax.broadcasted_iota(jnp.int32, (tokens, tokens), 1) < length_ref[pl.program_id(0)]
    outs = ([], [], [])
    for start in (0, HEAD):
        part = slice(start, start + HEAD)
        queries, keys, values = query_ref[:, part], key_ref[:, part], value_ref[:, part]
        grad = grad_ref[:, part]
        attention = softmax_head(queries, keys, alive)
        grad_attention = product_right(grad, values)
        grad_scores = attention * (
            grad_attention - jnp.sum(grad_attention * attention, axis=-1, keepdims=True)
        )
        grad_raw = (grad_scores.astype(jnp.bfloat16).astype(jnp.float32) * HEAD ** (-0.5)).astype(
            jnp.bfloat16
        )
        outs[0].append(product(grad_raw, keys))
        outs[1].append(product_left(grad_raw, queries))
        outs[2].append(product_left(attention.astype(jnp.bfloat16), grad))
    for number, pair in enumerate(outs):
        start = number * (out_ref.shape[1] // 3) + pl.program_id(1) * LANES
        out_ref[:, pl.ds(pl.multiple_of(start, LANES), LANES)] = jnp.concatenate(
            pair, axis=1
        ).astype(jnp.bfloat16)


def head_specs(tokens, pairs, count):
    return [
        pl.BlockSpec((tokens, LANES), lambda s, h, lengths, k=k: (s, k * pairs + h))
        for k in range(count)
    ]


def attend(lengths, mixed, tokens):
    width = mixed.shape[1] // 3
    pairs = width // LANES
    rows = mixed.shape[0]
    return pl.pallas_call(
        attend_kernel,
        grid_spec=pltpu.PrefetchScalarGridSpec(
            num_scalar_prefetch=1,
            grid=(rows // tokens, pairs),
            in_specs=head_specs(tokens, pairs, 3),
            out_specs=head_specs(tokens, pairs, 1)[0],
        ),
        out_shape=jax.ShapeDtypeStruct((rows, width), jnp.bfloat16),
        compiler_params=pltpu.CompilerParams(vmem_limit_bytes=32 << 20),
        cost_estimate=pl.CostEstimate(
            flops=8 * rows * tokens * width,
            bytes_accessed=8 * rows * width,
            transcendentals=rows * tokens * width // HEAD,
        ),
    )(lengths, mixed, mixed, mixed)


def attend_back(lengths, mixed, grad_context, tokens):
    width = mixed.shape[1] // 3
    pairs = width // LANES
    rows = mixed.shape[0]
    out = jax.ShapeDtypeStruct((rows, 3 * width), jnp.bfloat16)
    return pl.pallas_call(
        attend_back_kernel,
        grid_spec=pltpu.PrefetchScalarGridSpec(
            num_scalar_prefetch=1,
            grid=(rows // tokens, pairs),
            in_specs=head_specs(tokens, pairs, 3) + head_specs(tokens, pairs, 1),
            out_specs=pl.BlockSpec((tokens, 3 * width), lambda s, h, lengths: (s, 0)),
        ),
        out_shape=out,
        compiler_params=pltpu.CompilerParams(vmem_limit_bytes=32 << 20),
        cost_estimate=pl.CostEstimate(
            flops=20 * rows * tokens * width,
            bytes_accessed=14 * rows * width,
            transcendentals=rows * tokens * width // HEAD,
        ),
    )(lengths, mixed, mixed, mixed, grad_context)


def one_hot(count, index):
    return (
        lax.broadcasted_iota(jnp.int32, (count, index.shape[0]), 0) == index[None, :]
    ).astype(jnp.bfloat16)


def exact(left, right):
    return jnp.dot(left, right, precision=lax.Precision.HIGHEST, preferred_element_type=jnp.float32)


def shards(
    token_ids,
    seq_lengths,
    mlm_slots,
    mlm_labels,
    nsp_labels,
    *weights,
):
    masters, firsts, seconds = weights[0::3], weights[1::3], weights[2::3]
    (
        table_master,
        position_master,
        pair_master,
        input_master,
        output_master,
        dense_master,
        feed_master,
        vector_master,
    ) = masters
    micro, local, tokens = token_ids.shape
    slots_each = mlm_slots.shape[2]
    devices = lax.axis_size(AXES)
    me = lax.axis_index(AXES)
    seqs = micro * local
    total = seqs * tokens
    picked = seqs * slots_each
    depth, width = input_master.shape[0], output_master.shape[1]
    inner_width = feed_master.shape[2]
    vocab_rows = table_master.shape[0]
    low = jnp.bfloat16
    places = jnp.arange(tokens, dtype=jnp.int32)

    id_rows = total // LANES
    pack_rows = -(-(id_rows + 3 * seqs) // 8) * 8
    packed = pl.pallas_call(
        pack_kernel,
        out_shape=jax.ShapeDtypeStruct((pack_rows, LANES), jnp.int32),
        in_specs=[pl.BlockSpec(memory_space=pltpu.SMEM)]
        + [pl.BlockSpec(memory_space=pltpu.VMEM)] * 3,
    )(seq_lengths, token_ids, mlm_slots, mlm_labels)
    spread = jnp.broadcast_to(packed[None], (devices,) + packed.shape)
    shared = lax.all_to_all(spread, AXES, 0, 0)
    all_ids = shared[:, :id_rows].reshape(devices * seqs, tokens)
    all_slots, all_labels = (
        shared[:, id_rows + k * seqs : id_rows + (k + 1) * seqs, :slots_each] for k in (0, 1)
    )
    all_lengths = shared[:, id_rows + 2 * seqs : id_rows + 3 * seqs, :1]
    all_counted = (all_slots < all_lengths).astype(jnp.float32).reshape(-1)
    all_labels = all_labels.reshape(-1)
    masked_count = jnp.sum(all_counted)
    inv_count = 1.0 / masked_count
    inv_seqs = 1.0 / (devices * seqs)

    table_low = table_master.astype(low)
    vector_each = vector_master.shape[0]
    vector_columns = -(-vector_each // depth)
    small_used = tokens + 4 + vector_columns
    small_columns = -(-small_used // LANES) * LANES
    small_low = jnp.concatenate(
        [
            position_master.T,
            jnp.moveaxis(pair_master, 0, 1).reshape(depth, 4),
            jnp.pad(vector_master, (0, depth * vector_columns - vector_each)).reshape(
                depth, vector_columns
            ),
            jnp.zeros((depth, small_columns - small_used), jnp.float32),
        ],
        axis=1,
    ).astype(low)
    first_group = Gather(pin([input_master.astype(low), small_low], spread))

    lane_rows = -(-vocab_rows // LANES)

    def split_ids(ids, alive):
        owner = ids // vocab_rows
        within = ids - owner * vocab_rows
        high = owner * lane_rows + within // LANES
        return owner, jnp.where(alive, high, -1), within % LANES

    _, all_high, all_low = split_ids(
        all_ids, places[None, :] < all_lengths.reshape(devices * seqs, 1)
    )
    hits = product_right(
        one_hot(devices * lane_rows, all_high.reshape(-1)), one_hot(LANES, all_low.reshape(-1))
    )
    used = (hits > 0).astype(jnp.float32)
    lane = jnp.arange(LANES)
    before = exact(used, (lane[:, None] < lane[None, :]).astype(jnp.float32))
    row_totals = jnp.sum(used, axis=1).reshape(devices, lane_rows)
    row_index = jnp.arange(lane_rows)
    earlier = jnp.sum(
        jnp.where(row_index[None, :, None] < row_index[None, None, :], row_totals[:, :, None], 0.0),
        axis=1,
    )
    rank = before + earlier.reshape(-1, 1)
    most = jnp.max(jnp.sum(row_totals, axis=1)).astype(jnp.int32)
    ahead = ROWS_AHEAD
    rounds = -(-most // ahead)

    lengths = seq_lengths.reshape(-1)
    my_alive = (places[None, :] < lengths[:, None]).reshape(-1)
    my_owner, my_high, my_low = split_ids(token_ids.reshape(-1), my_alive)
    looked = exact(rank.T, one_hot(devices * lane_rows, my_high).astype(jnp.float32))
    my_rank = jnp.sum(looked * one_hot(LANES, my_low).astype(jnp.float32), axis=0).astype(jnp.int32)

    own_rank = lax.dynamic_slice_in_dim(rank, me * lane_rows, lane_rows, 0).reshape(-1)[:vocab_rows]
    own_used = lax.dynamic_slice_in_dim(used, me * lane_rows, lane_rows, 0).reshape(-1)[:vocab_rows]
    own_slot = jnp.where(own_used > 0, own_rank.astype(jnp.int32), -1)

    def picks(start):
        own = one_hot(ahead, jnp.where(own_slot >= start, own_slot - start, -1))
        inside = my_alive & (my_rank >= start) & (my_rank < start + ahead)
        mine = one_hot(devices * ahead, jnp.where(inside, my_owner * ahead + my_rank - start, -1))
        return own, mine

    own_first, mine_first = picks(0)
    own_rows = product(own_first, table_low).astype(low)
    word_group = Gather([own_rows])
    first_group.line(own_rows)
    first_plane = first_group.plane()
    word_group.line()
    word_plane = word_group.plane()
    second_group = Gather(
        pin(
            [output_master.astype(low), feed_master[0].astype(low)],
            [half[0] for half in word_plane],
            first_plane,
        )
    )
    first_core = first_group.core()
    second_group.line(word_plane, first_core)
    word_group.pieces = pin(word_plane, first_core, all_counted, all_labels)
    input_all, small_all = first_group.finish()
    word_core = word_group.core()
    (word_rows,) = word_group.finish()
    second_plane = second_group.plane()
    third_group = Gather(
        pin(
            [
                feed_master[1].astype(low),
                dense_master[0].astype(low),
                dense_master[1].astype(low),
            ],
            word_plane,
            first_core,
        )
    )
    third_group.line([half[0] for half in second_plane])
    words = product_left(mine_first, word_rows)

    def fetch_more(state):
        turn, words = state
        own, mine = picks(turn * ahead)
        rows = lax.all_gather(product(own, table_low).astype(low), AXES, axis=0, tiled=True)
        return turn + 1, words + product_left(mine, rows)

    _, words = lax.while_loop(lambda state: state[0] < rounds, fetch_more, (jnp.int32(1), words))

    position = small_all[:, :tokens].T.astype(jnp.float32)
    pair_cols = jnp.moveaxis(small_all[:, tokens : tokens + 4].reshape(width, 2, 2), 1, 0)
    vectors = small_all[:, tokens + 4 : small_used].reshape(devices, depth * vector_columns)
    parts = split_vectors(vectors[:, :vector_each].reshape(-1).astype(jnp.float32))

    second = (places[None, :] >= lengths[:, None] // 2).reshape(-1)
    type_cols = pair_cols[0].astype(jnp.float32)
    embedded = (
        words
        + jnp.tile(position, (seqs, 1))
        + jnp.where(second[:, None], type_cols[:, 1], type_cols[:, 0])
    )
    normed, saved_zero = norm_forward(embedded, parts[0], parts[1])
    normed_low = normed.astype(low)
    bias_mixed = jnp.concatenate([parts[8], jnp.zeros((width,), jnp.float32), parts[9]])
    mixed = (product(normed_low, input_all) + bias_mixed).astype(low)
    third_group.plane()
    context_low = attend(lengths, mixed, tokens)
    second_group.pieces = pin(second_group.pieces, mixed)
    second_group.core()
    output_all, feed_in = second_group.finish()
    third_group.pieces = pin(third_group.pieces, context_low)
    third_group.core()
    feed_out, dense_one, dense_two = third_group.finish()
    branch = product(context_low, output_all) + parts[10]
    hidden_one, saved_one = norm_forward(normed + branch, parts[2], parts[3])
    one_low = hidden_one.astype(low)
    active, slope = gelu_parts(product(one_low, feed_in) + parts[11])
    active_low, slope = lax.optimization_barrier((active.astype(low), slope))
    outer = product_right(active_low, feed_out) + parts[12]
    hidden_two, saved_two = norm_forward(hidden_one + outer, parts[4], parts[5])
    two_low = hidden_two.astype(low)

    my_slots = mlm_slots.reshape(seqs, slots_each) + tokens * jnp.arange(seqs, dtype=jnp.int32)[:, None]
    slot_hot = one_hot(total, my_slots.reshape(-1))
    picked_low = product_left(slot_hot, two_low).astype(low)
    lifted, head_slope = gelu_parts(product(picked_low, dense_one) + parts[13])
    head_out, saved_head = norm_forward(lifted, parts[6], parts[7])
    head_group = Gather([head_out.astype(low)])
    head_group.line()
    head_group.plane()

    first_hot = one_hot(total, tokens * jnp.arange(seqs, dtype=jnp.int32))
    first_low = product_left(first_hot, two_low).astype(low)
    pooled = jnp.tanh(product(first_low, dense_two) + parts[14])
    pooled_low = pooled.astype(low)
    pair_logits = product(pooled_low, pair_cols[1])
    pair_top = jnp.max(pair_logits, axis=-1, keepdims=True)
    pair_total = pair_top + jnp.log(
        jnp.sum(jnp.exp(pair_logits - pair_top), axis=-1, keepdims=True)
    )
    pair_hit = jnp.arange(2, dtype=jnp.int32)[None, :] == nsp_labels.reshape(-1, 1)
    pair_local = jnp.sum(pair_total[:, 0] - jnp.sum(jnp.where(pair_hit, pair_logits, 0.0), axis=1))

    vocab_bias = lax.dynamic_slice_in_dim(parts[15], me * vocab_rows, vocab_rows, 0)
    head_group.core()
    (heads,) = head_group.finish()
    logits = product_right(heads, table_low) + vocab_bias
    top = jnp.max(logits, axis=-1)
    local_totals = top + jnp.log(jnp.sum(jnp.exp(logits - top[:, None]), axis=-1))
    all_totals = share_small(local_totals.reshape(-1, LANES))
    highest = jnp.max(all_totals, axis=0)
    log_totals = (highest + jnp.log(jnp.sum(jnp.exp(all_totals - highest), axis=0))).reshape(-1)
    vocab_index = me * vocab_rows + jnp.arange(vocab_rows, dtype=jnp.int32)
    hit = vocab_index[None, :] == all_labels[:, None]
    target_local = jnp.sum(all_counted[:, None] * jnp.where(hit, logits, 0.0))
    grad_logits = (
        (jnp.exp(logits - log_totals[:, None]) - hit.astype(jnp.float32))
        * (all_counted * inv_count)[:, None]
    ).astype(low)
    middle = width // 2
    head_sum = Scatter(
        [
            (product(grad_logits, side).reshape(devices, picked, middle), number)
            for number, side in enumerate((table_low[:, :middle], table_low[:, middle:]))
        ]
    )
    sent = head_sum.send()
    grad_table = product_left(pin(grad_logits, sent), heads)
    masked_shared = jnp.sum(all_counted * pin(log_totals, sent))
    head_sum.receive()
    for _ in range(1, bits_of(lax.axis_size("wide"))):
        head_sum.step()
    grad_vocab = jnp.sum(grad_logits.astype(jnp.float32), axis=0)
    vocab_pad = -(-vocab_rows // (8 * LANES)) * 8 * LANES
    all_vocab = share_small(jnp.pad(grad_vocab, (0, vocab_pad - vocab_rows)).reshape(-1, LANES))
    head_sum.line()
    grad_head = jnp.concatenate(head_sum.finish(grad_table, all_vocab), axis=1)

    def owners(values):
        return values.reshape(devices, -1, values.shape[1])

    def column_sum(values):
        return jnp.sum(values.astype(jnp.float32), axis=0, keepdims=True)

    grad_gelu, grad_head_gain, grad_head_shift = norm_backward(grad_head, saved_head, parts[6])
    grad_transform = (grad_gelu * head_slope).astype(low)
    grad_dense_zero = product_left(picked_low, grad_transform)
    grad_pair_logits = (
        (jnp.exp(pair_logits - pair_total) - pair_hit.astype(jnp.float32)) * inv_seqs
    ).astype(low)
    grad_classifier = product_left(pooled_low, grad_pair_logits)
    grad_pooled = product_right(grad_pair_logits, pair_cols[1])
    grad_pool_pre = (grad_pooled * (1.0 - pooled * pooled)).astype(low)
    grad_pooler = product_left(first_low, grad_pool_pre)
    grad_two = exact(
        slot_hot.astype(jnp.float32), product_right(grad_transform, dense_one)
    ) + exact(first_hot.astype(jnp.float32), product_right(grad_pool_pre, dense_two))
    grad_outer, grad_inner, grad_sum_one, grad_branch, grad_context, feed_rows = feed_back(
        grad_two, saved_two, parts[4], slope, feed_out, feed_in, saved_one, parts[2], output_all
    )
    grad_feed_out = product_left(grad_outer, active_low)
    grad_feed_in = product_left(one_low, grad_inner)
    feed_sum = Scatter(
        [
            (owners(grad_feed_in), 0),
            (owners(grad_dense_zero), 0),
            (owners(grad_feed_out), 1),
            (owners(grad_pooler), 1),
        ]
    )
    feed_sum.send()
    came = feed_sum.receive()
    sent = feed_sum.send()
    grad_context = pin(grad_context, came, sent)
    grad_mixed = attend_back(lengths, mixed, grad_context, tokens)
    came = feed_sum.receive()
    sent = feed_sum.send()
    grad_mixed = pin(grad_mixed, came, sent)
    in_sum = Scatter(
        [
            (owners(product_left(normed_low, grad_mixed[:, : 2 * width])), 0),
            (owners(product_left(normed_low, grad_mixed[:, 2 * width :])), 1),
            (owners(product_left(context_low, pin(grad_branch, grad_mixed))), 1),
        ]
    )
    sent = in_sum.send()
    feed_came = [feed_sum.receive()]
    while feed_sum.dims[0]:
        feed_came.append(feed_sum.step())
    in_came = in_sum.receive()
    embedded_low, grad_small = embed_back(
        lengths,
        pin(grad_mixed, sent),
        input_all,
        grad_sum_one,
        saved_zero,
        parts[0],
        feed_rows,
        (
            grad_classifier.T,
            grad_head_gain[None],
            grad_head_shift[None],
            column_sum(grad_transform),
            column_sum(grad_pool_pre),
        ),
        tokens,
    )
    embedded_low, grad_small = pin((embedded_low, grad_small), feed_came, in_came)
    in_away = in_sum.send()
    embedded_low, grad_small = pin((embedded_low, grad_small), in_away)
    word_sums = [
        (product(mine_first, side).reshape(devices, ahead, middle), number)
        for number, side in enumerate((embedded_low[:, :middle], embedded_low[:, middle:]))
    ]
    vector_count = (vector_each * devices - devices * vocab_rows) // width
    last_sum = Scatter(word_sums + [(owners(grad_small), 1)])
    last_away = last_sum.send()
    in_came = in_sum.receive()
    feed_sum.hold(last_away)
    feed_away = feed_sum.line()
    in_sum.hold(feed_away)
    in_away = in_sum.send()
    last_sum.receive()
    last_sum.hold(in_away)
    last_away = last_sum.send()
    in_sum.receive()
    while in_sum.dims[0]:
        in_sum.step()
    in_sum.hold(last_away)
    in_away = in_sum.line()
    last_sum.receive()
    while last_sum.dims[0]:
        last_sum.step()
    sent = last_sum.line()
    sum_feed_in, sum_dense, sum_feed_out, sum_pooler = feed_sum.finish(sent)
    sum_mixed, sum_value, sum_output = in_sum.finish(sent)
    words_left, words_right, sum_small = last_sum.finish()
    sum_input = jnp.concatenate([sum_mixed, sum_value], axis=1)

    def return_more(state):
        turn, grad_table = state
        own, mine = picks(turn * ahead)
        back = lax.psum_scatter(
            product(mine, embedded_low), AXES, scatter_dimension=0, tiled=True
        )
        return turn + 1, grad_table + exact(own.T.astype(jnp.float32), back)

    _, grad_table = lax.while_loop(
        lambda state: state[0] < rounds, return_more, (jnp.int32(1), grad_table)
    )

    def halves(values):
        high = values.astype(low)
        return high, (values - high.astype(jnp.float32)).astype(low)

    table_high, table_rest = halves(grad_table)
    chosen = product(own_first, table_high) + product(own_first, table_rest)
    table_square = jnp.sum(grad_table * grad_table)
    present = jnp.sum(own_first.astype(jnp.float32), axis=1, keepdims=True)
    words_own = jnp.concatenate([words_left, words_right], axis=1)
    table_square = table_square + jnp.sum(present * words_own * (words_own + 2.0 * chosen))

    sum_vector = sum_small[:, tokens + 4 : tokens + 4 + vector_count]
    pieces = [
        sum_small[:, :tokens],
        jnp.moveaxis(sum_small[:, tokens : tokens + 4].reshape(depth, 2, 2), 1, 0),
        sum_input,
        sum_output,
        jnp.stack([sum_dense, sum_pooler]),
        jnp.stack([sum_feed_in, sum_feed_out]),
    ]
    vector_flat = depth * vector_count
    vector_pad = -(-vector_flat // LANES) * LANES
    all_vector = share_small(
        jnp.pad(sum_vector.reshape(-1), (0, vector_pad - vector_flat)).reshape(-1, LANES)
    )
    squares = table_square + sum(
        (jnp.sum(item * item) for item in pieces + [sum_vector, grad_vocab])
    )
    scalars = jnp.stack([squares, target_local, pair_local])
    totals = jnp.sum(share_small(jnp.pad(scalars, (0, LANES - 3))[None])[:, 0, :3], axis=0)
    grad_table = grad_table + product_left(
        jnp.concatenate([own_first, own_first], axis=0),
        jnp.concatenate(halves(words_own), axis=0),
    )
    grad_vector = jnp.concatenate(
        [
            all_vector.reshape(devices, -1)[:, :vector_flat]
            .reshape(devices * depth, vector_count)
            .T.reshape(-1),
            all_vocab.reshape(devices, -1)[:, :vocab_rows].reshape(-1),
        ]
    )
    pieces = (
        [grad_table]
        + pieces
        + [lax.dynamic_slice_in_dim(grad_vector, me * vector_each, vector_each, 0)]
    )
    norm = jnp.sqrt(totals[0])
    masked_total = masked_shared - totals[1]
    pair_total_sum = totals[2]
    factor = CLIP_NORM / (norm + 1e-06)
    correct_one = 1.0 - BETA_ONE**STEP_COUNT
    correct_two = 1.0 - BETA_TWO**STEP_COUNT
    updated = []
    for number in range(8):
        turned = (lambda item: item.T) if number == 1 else (lambda item: item)
        master = turned(masters[number])
        grad = pieces[number] * factor
        moment_one = BETA_ONE * turned(firsts[number]) + (1.0 - BETA_ONE) * grad
        moment_two = BETA_TWO * turned(seconds[number]) + (1.0 - BETA_TWO) * grad * grad
        direction = moment_one / correct_one / (jnp.sqrt(moment_two / correct_two) + ADAM_EPS)
        decay = DECAY_RATE if number < 7 else 0.0
        updated.extend(
            [
                turned(master - LEARN_RATE * (direction + decay * master)),
                turned(moment_one),
                turned(moment_two),
            ]
        )
    masked_sums = jnp.stack([masked_total, masked_count])
    return (masked_sums, pair_total_sum, norm) + tuple(updated)


def solution(mesh):
    placed = (
        P(None, ("wide", "narrow"), None),
        P(None, ("wide", "narrow")),
        P(None, ("wide", "narrow"), None),
        P(None, ("wide", "narrow"), None),
        P(None, ("wide", "narrow")),
        P(("wide", "narrow"), None),
        P(("wide", "narrow"), None),
        P(("wide", "narrow"), None),
        P(None, ("wide", "narrow")),
        P(None, ("wide", "narrow")),
        P(None, ("wide", "narrow")),
        P(None, ("wide", "narrow"), None),
        P(None, ("wide", "narrow"), None),
        P(None, ("wide", "narrow"), None),
        P(("wide", "narrow"), None),
        P(("wide", "narrow"), None),
        P(("wide", "narrow"), None),
        P(("wide", "narrow"), None),
        P(("wide", "narrow"), None),
        P(("wide", "narrow"), None),
        P(None, ("wide", "narrow"), None),
        P(None, ("wide", "narrow"), None),
        P(None, ("wide", "narrow"), None),
        P(None, ("wide", "narrow"), None),
        P(None, ("wide", "narrow"), None),
        P(None, ("wide", "narrow"), None),
        P(("wide", "narrow")),
        P(("wide", "narrow")),
        P(("wide", "narrow")),
    )
    return jax.shard_map(
        shards,
        mesh=mesh,
        in_specs=placed,
        out_specs=(
            P(),
            P(),
            P(),
            P(("wide", "narrow"), None),
            P(("wide", "narrow"), None),
            P(("wide", "narrow"), None),
            P(None, ("wide", "narrow")),
            P(None, ("wide", "narrow")),
            P(None, ("wide", "narrow")),
            P(None, ("wide", "narrow"), None),
            P(None, ("wide", "narrow"), None),
            P(None, ("wide", "narrow"), None),
            P(("wide", "narrow"), None),
            P(("wide", "narrow"), None),
            P(("wide", "narrow"), None),
            P(("wide", "narrow"), None),
            P(("wide", "narrow"), None),
            P(("wide", "narrow"), None),
            P(None, ("wide", "narrow"), None),
            P(None, ("wide", "narrow"), None),
            P(None, ("wide", "narrow"), None),
            P(None, ("wide", "narrow"), None),
            P(None, ("wide", "narrow"), None),
            P(None, ("wide", "narrow"), None),
            P(("wide", "narrow")),
            P(("wide", "narrow")),
            P(("wide", "narrow")),
        ),
        check_vma=False,
    )
```

```python
from functools import partial

import jax
import jax.numpy as jnp
from jax import lax
from jax.experimental import pallas as pl
from jax.experimental.pallas import tpu as pltpu
from jax.sharding import PartitionSpec as P

D = 768
HEAD = 64
FF = 3072
STEP_COUNT = 10


NORM_EPS = 1e-12
CLIP_NORM = 0.02
BETA_ONE = 0.9
BETA_TWO = 0.999
ADAM_EPS = 1e-08
DECAY_RATE = 0.01
LEARN_RATE = 0.1
MASKED_FILL = -1000000000.0
AXES = ("wide", "narrow")
ROWS_AHEAD = 96
LANES = 128


def product(left, right):
    return jnp.dot(left, right, preferred_element_type=jnp.float32)


def product_right(left, right):
    return lax.dot_general(
        left, right, (((1,), (1,)), ((), ())), preferred_element_type=jnp.float32
    )


def product_left(left, right):
    return lax.dot_general(
        left, right, (((0,), (0,)), ((), ())), preferred_element_type=jnp.float32
    )


def norm_forward(values, gain, shift):
    average = jnp.mean(values, axis=-1, keepdims=True)
    centered = values - average
    spread = jnp.mean(centered * centered, axis=-1, keepdims=True)
    inverse = lax.rsqrt(spread + NORM_EPS)
    normal = centered * inverse
    return (normal * gain + shift, (normal, inverse))


def norm_backward(grad, saved, gain):
    normal, inverse = saved
    scaled = grad * gain
    inner = (
        scaled
        - jnp.mean(scaled, axis=-1, keepdims=True)
        - normal * jnp.mean(scaled * normal, axis=-1, keepdims=True)
    )
    return (inner * inverse, jnp.sum(grad * normal, axis=0), jnp.sum(grad, axis=0))


def gelu_exact(values):
    return jax.nn.gelu(values, approximate=False)


def gelu_back(values, grad):
    return jax.vjp(gelu_exact, values)[1](grad)[0]


def split_vectors(vectors):
    extents = [D] * 11 + [FF] + [D] * 3
    pieces = []
    start = 0
    for extent in extents:
        pieces.append(vectors[start : start + extent])
        start += extent
    pieces.append(vectors[start:])
    return pieces


def bits_of(size):
    return size.bit_length() - 1


def orders():
    far = [("wide", bit) for bit in range(1, bits_of(lax.axis_size("wide")))]
    return far, far[::-1]


CORE = ("wide", 0)


def my_bit(dim):
    return (lax.axis_index(dim[0]) >> dim[1]) & 1


def swap(values, dim):
    size = lax.axis_size(dim[0])
    return lax.ppermute(values, dim[0], [(i, i ^ (1 << dim[1])) for i in range(size)])


def pin(values, *others):
    return lax.optimization_barrier((values, others))[0]


def place_blocks(spreads, starts, middle, me_ref, *refs):
    count = len(spreads[0])
    outs = refs[8 : 8 + len(starts) - 1]
    held = refs[8 + len(outs) : 10 + len(outs)]
    arrive, leave = refs[10 + len(outs) :]
    me = me_ref[0]
    inward, outward = [], []
    for side in range(2):
        pieces = refs[4 * side : 4 * side + 4]
        each = pieces[0].shape[0]
        left = 0 if side == 0 else middle
        right = middle if side == 0 else starts[-1]
        for code, offset in enumerate(spreads[side]):
            number = side * count + code
            inward.append(
                pltpu.make_async_copy(
                    pieces[code // each].at[code % each], held[side].at[code], arrive.at[number]
                )
            )
            group = []
            for out_ref, start, stop in zip(outs, starts, starts[1:]):
                low, high = max(start, left), min(stop, right)
                if low < high:
                    group.append(
                        pltpu.make_async_copy(
                            held[side].at[code, :, :, low - left : high - left],
                            out_ref.at[me ^ offset, :, :, low - start : high - start],
                            leave.at[number, len(group)],
                        )
                    )
            outward.append(group)
    for copy in inward:
        copy.start()
    for first, group in zip(inward, outward):
        first.wait()
        for copy in group:
            copy.start()
    for group in outward:
        for copy in group:
            copy.wait()


def reach(values, step):
    size = lax.axis_size("narrow")
    return lax.ppermute(values, "narrow", [(z, z ^ step) for z in range(size)])


def trade(blocks):
    return lax.all_to_all(blocks, "narrow", 0, 0)


class Gather:
    def __init__(self, arrays):
        self.columns = [array.shape[1] for array in arrays]
        self.rows = arrays[0].shape[0]
        total = sum(self.columns)
        self.middle = total // 2 // LANES * LANES
        self.packed = jnp.concatenate(arrays, axis=1) if len(arrays) > 1 else arrays[0]

    def line(self, *before):
        size = lax.axis_size("narrow")
        me = lax.axis_index("narrow")
        arrived = pin([reach(self.packed, step) for step in range(1, size)], *before)
        blocks = []
        for spot in range(size):
            chosen = self.packed
            for step in range(1, size):
                chosen = jnp.where(me == spot ^ step, arrived[step - 1], chosen)
            blocks.append(chosen)
        self.halves = [
            jnp.stack([block[:, : self.middle] for block in blocks])[None],
            jnp.stack([block[:, self.middle :] for block in blocks])[None],
        ]
        return self.halves

    def line_whole(self, *before):
        size = lax.axis_size("narrow")
        blocks = trade(jnp.broadcast_to(self.packed[None], (size,) + self.packed.shape))
        blocks = pin(blocks, *before)
        self.halves = [
            blocks[None, :, :, : self.middle],
            blocks[None, :, :, self.middle :],
        ]
        return self.halves

    def plane(self, first=(), last=()):
        self.pieces = []
        for held, order in zip(pin(self.halves, first), orders()):
            for dim in order[:-1]:
                held = jnp.concatenate([held, swap(held, dim)], axis=0)
            self.pieces.append([held])
        self.pieces = pin(self.pieces, last)
        for piece, order in zip(self.pieces, orders()):
            piece.append(swap(piece[0], order[-1]))
        return self.pieces

    def core(self):
        self.pieces = [half + [swap(piece, CORE) for piece in half] for half in self.pieces]
        return self.pieces

    def finish(self):
        pieces = self.pieces
        count = lax.axis_size("wide")
        spreads = [
            [
                sum(((code >> k) & 1) << dim[1] for k, dim in enumerate(order + [CORE]))
                for code in range(count)
            ]
            for order in orders()
        ]
        starts = [sum(self.columns[:k]) for k in range(len(self.columns) + 1)]
        line = lax.axis_size("narrow")
        dtype = self.packed.dtype
        me = lax.axis_index("wide").astype(jnp.int32).reshape(1)
        moved = 2 * count * line * self.rows * starts[-1] * dtype.itemsize
        outs = pl.pallas_call(
            partial(place_blocks, spreads, starts, self.middle),
            out_shape=tuple(
                jax.ShapeDtypeStruct((count, line, self.rows, columns), dtype)
                for columns in self.columns
            ),
            in_specs=[pl.BlockSpec(memory_space=pltpu.SMEM)]
            + [pl.BlockSpec(memory_space=pl.ANY)] * 8,
            out_specs=(pl.BlockSpec(memory_space=pl.ANY),) * len(self.columns),
            scratch_shapes=[
                pltpu.VMEM((count, line, self.rows, self.middle), dtype),
                pltpu.VMEM((count, line, self.rows, starts[-1] - self.middle), dtype),
                pltpu.SemaphoreType.DMA((2 * count,)),
                pltpu.SemaphoreType.DMA((2 * count, len(self.columns))),
            ],
            compiler_params=pltpu.CompilerParams(vmem_limit_bytes=40 << 20),
            cost_estimate=pl.CostEstimate(flops=0, bytes_accessed=moved, transcendentals=0),
        )(me, *pieces[0], *pieces[1])
        return [out.reshape(count * line * self.rows, -1) for out in outs]


class Scatter:
    def __init__(self, items):
        wide, line = lax.axis_size("wide"), lax.axis_size("narrow")
        self.terms, self.dims, self.fixed = [], [], []
        for blocks, which in items:
            labels = tuple(("wide", bit) for bit in range(bits_of(wide)))[::-1]
            shape = (2,) * bits_of(wide) + (line,) + blocks.shape[1:]
            self.terms.append([(blocks.reshape(shape), labels)])
            self.dims.append([CORE] + orders()[which][::-1])
            self.fixed.append({})

    def cut(self, number, fixed):
        total = None
        for array, labels in self.terms[number]:
            starts = [fixed.get(label, 0) for label in labels]
            sizes = [1 if label in fixed else 2 for label in labels]
            starts += [0, 0, 0]
            sizes += list(array.shape[-3:])
            starts = [jnp.asarray(start, jnp.int32) for start in starts]
            kept = [2 for label in labels if label not in fixed] + sizes[-3:]
            part = lax.dynamic_slice(array, starts, sizes).reshape(kept).astype(jnp.float32)
            total = part if total is None else total + part
        return total

    def send(self):
        self.away = []
        for number, dims in enumerate(self.dims):
            fixed = dict(self.fixed[number])
            fixed[dims[0]] = 1 - my_bit(dims[0])
            self.away.append(self.cut(number, fixed).astype(jnp.bfloat16))
        return self.away

    def receive(self):
        arrived = []
        for number, away in enumerate(self.away):
            dim = self.dims[number].pop(0)
            self.fixed[number][dim] = my_bit(dim)
            arrived.append(swap(away, dim))
            labels = self.terms[number][0][1]
            left = tuple(label for label in labels if label not in self.fixed[number])
            self.terms[number].append((arrived[-1], left))
        return arrived

    def step(self):
        self.send()
        return self.receive()

    def absorb(self, other):
        self.terms += other.terms
        self.fixed += other.fixed
        self.dims += other.dims

    def hold(self, *others):
        arrays = pin([[term[0] for term in terms] for terms in self.terms], *others)
        self.terms = [
            [(array, term[1]) for array, term in zip(held, terms)]
            for held, terms in zip(arrays, self.terms)
        ]

    def line(self):
        size = lax.axis_size("narrow")
        me = lax.axis_index("narrow")
        depth = min(terms[0][0].shape[-2] for terms in self.terms)
        flat = []
        for number, fixed in enumerate(self.fixed):
            block = self.cut(number, fixed)
            flat.extend(block[:, k : k + depth] for k in range(0, block.shape[1], depth))
        whole = jnp.concatenate(flat, axis=2) if len(flat) > 1 else flat[0]
        whole = lax.optimization_barrier(whole)
        self.goes = [
            lax.dynamic_index_in_dim(whole, me ^ step, 0, keepdims=False).astype(jnp.bfloat16)
            for step in range(1, size)
        ]
        self.own = lax.dynamic_index_in_dim(whole, me, 0, keepdims=False)
        return self.goes

    def finish(self, *before):
        arrived = [reach(item, step + 1) for step, item in enumerate(self.goes)]
        arrived = pin(arrived, *before)
        return self.apart(self.own + sum(item.astype(jnp.float32) for item in arrived))

    def line_whole(self, *before):
        depth = min(terms[0][0].shape[-2] for terms in self.terms)
        flat = []
        for number, fixed in enumerate(self.fixed):
            block = self.cut(number, fixed).astype(jnp.bfloat16)
            flat.extend(block[:, k : k + depth] for k in range(0, block.shape[1], depth))
        self.goes = pin(jnp.concatenate(flat, axis=2) if len(flat) > 1 else flat[0], *before)
        self.arrived = trade(self.goes)
        return self.arrived

    def finish_whole(self):
        return self.apart(jnp.sum(self.arrived.astype(jnp.float32), axis=0))

    def apart(self, total):
        depth = total.shape[0]
        results, start = [], 0
        for terms in self.terms:
            parts, columns = terms[0][0].shape[-2] // depth, terms[0][0].shape[-1]
            pieces = [
                total[:, start + k * columns : start + (k + 1) * columns] for k in range(parts)
            ]
            start += parts * columns
            results.append(jnp.concatenate(pieces, axis=0) if parts > 1 else pieces[0])
        return results


def share_small(values):
    count = lax.axis_size(AXES)
    spread = jnp.broadcast_to(values[None], (count,) + values.shape)
    return lax.all_to_all(spread, AXES, 0, 0)


def pack_kernel(length_ref, ids_ref, slot_ref, label_ref, out_ref):
    out_ref[...] = jnp.zeros_like(out_ref)
    micro, local, tokens = ids_ref.shape
    slots = slot_ref.shape[2]
    row = 0
    for index in range(micro * local):
        for start in range(0, tokens, LANES):
            out_ref[row : row + 1, :] = ids_ref[
                index // local, index % local : index % local + 1, start : start + LANES
            ]
            row += 1
    for ref in (slot_ref, label_ref):
        for index in range(micro * local):
            out_ref[row : row + 1, :slots] = ref[
                index // local, index % local : index % local + 1, :
            ]
            row += 1
    for index in range(micro * local):
        out_ref[row : row + 1, :] = jnp.full(
            (1, LANES), length_ref[index // local, index % local], jnp.int32
        )
        row += 1


def norm_back_rows(grad, normal, inverse, gain):
    scaled = grad * gain
    inner = (
        scaled
        - jnp.mean(scaled, axis=-1, keepdims=True)
        - normal * jnp.mean(scaled * normal, axis=-1, keepdims=True)
    )
    return (
        inner * inverse,
        jnp.sum(grad * normal, axis=0, keepdims=True),
        jnp.sum(grad, axis=0, keepdims=True),
    )


SMALL_ROWS = 32
VECTOR_AT = 4


def feed_back_kernel(
    grad_ref,
    normal_two_ref,
    inverse_two_ref,
    gain_two_ref,
    slope_ref,
    out_proj_ref,
    in_proj_ref,
    normal_one_ref,
    inverse_one_ref,
    gain_one_ref,
    attend_proj_ref,
    outer_ref,
    inner_ref,
    sum_ref,
    branch_ref,
    context_ref,
    rows_ref,
):
    @pl.when(pl.program_id(0) == 0)
    def _():
        rows_ref[...] = jnp.zeros_like(rows_ref)

    def add_row(place, row):
        at = VECTOR_AT + place
        rows_ref[at : at + 1, :] = rows_ref[at : at + 1, :] + row

    def column_sum(values):
        return jnp.sum(values.astype(jnp.float32), axis=0, keepdims=True)

    width = grad_ref.shape[1]
    grad, gain_sum, shift_sum = norm_back_rows(
        grad_ref[...], normal_two_ref[...], inverse_two_ref[...], gain_two_ref[...]
    )
    add_row(4, gain_sum)
    add_row(5, shift_sum)
    outer = grad.astype(jnp.bfloat16)
    outer_ref[...] = outer
    add_row(15, column_sum(outer))
    for number, start in enumerate(range(0, slope_ref.shape[1], width)):
        part = slice(start, start + width)
        inner = (product(outer, out_proj_ref[:, part]) * slope_ref[:, part]).astype(jnp.bfloat16)
        inner_ref[:, part] = inner
        add_row(11 + number, column_sum(inner))
        grad = grad + product_right(inner, in_proj_ref[:, part])
    grad, gain_sum, shift_sum = norm_back_rows(
        grad, normal_one_ref[...], inverse_one_ref[...], gain_one_ref[...]
    )
    add_row(2, gain_sum)
    add_row(3, shift_sum)
    sum_ref[...] = grad
    branch = grad.astype(jnp.bfloat16)
    branch_ref[...] = branch
    add_row(10, column_sum(branch))
    context_ref[...] = product_right(branch, attend_proj_ref[...]).astype(jnp.bfloat16)


def feed_back(grad, saved_two, gain_two, slope, feed_out, feed_in, saved_one, gain_one, output_all):
    rows, width = grad.shape
    inner = slope.shape[1]
    tile = 256 if rows % 256 == 0 else rows

    def tiled(columns):
        return pl.BlockSpec((tile, columns), lambda i: (i, 0))

    def whole(array):
        return pl.BlockSpec(array.shape, lambda i: (0, 0), pipeline_mode=pl.Buffered(1))

    low = jnp.bfloat16
    gain_two, gain_one = gain_two[None], gain_one[None]
    return pl.pallas_call(
        feed_back_kernel,
        grid=(rows // tile,),
        in_specs=[
            tiled(width),
            tiled(width),
            tiled(1),
            whole(gain_two),
            tiled(inner),
            whole(feed_out),
            whole(feed_in),
            tiled(width),
            tiled(1),
            whole(gain_one),
            whole(output_all),
        ],
        out_specs=(
            tiled(width),
            tiled(inner),
            tiled(width),
            tiled(width),
            tiled(width),
            pl.BlockSpec((SMALL_ROWS, width), lambda i: (0, 0)),
        ),
        out_shape=(
            jax.ShapeDtypeStruct((rows, width), low),
            jax.ShapeDtypeStruct((rows, inner), low),
            jax.ShapeDtypeStruct((rows, width), jnp.float32),
            jax.ShapeDtypeStruct((rows, width), low),
            jax.ShapeDtypeStruct((rows, width), low),
            jax.ShapeDtypeStruct((SMALL_ROWS, width), jnp.float32),
        ),
        compiler_params=pltpu.CompilerParams(vmem_limit_bytes=56 << 20),
        cost_estimate=pl.CostEstimate(
            flops=2 * rows * width * (2 * inner + width),
            bytes_accessed=rows * (6 * inner + 22 * width) + 2 * width * (2 * inner + width),
            transcendentals=0,
        ),
    )(
        grad,
        *saved_two,
        gain_two,
        slope,
        feed_out,
        feed_in,
        *saved_one,
        gain_one,
        output_all,
    )


def embed_back_kernel(
    length_ref,
    mixed_ref,
    proj_ref,
    sum_ref,
    normal_ref,
    inverse_ref,
    gain_ref,
    feed_rows_ref,
    pair_rows_ref,
    head_gain_ref,
    head_shift_ref,
    transform_ref,
    pool_ref,
    low_ref,
    small_ref,
    position_ref,
    rows_ref,
):
    step = pl.program_id(0)
    tokens, width = sum_ref.shape

    @pl.when(step == 0)
    def _():
        position_ref[...] = jnp.zeros_like(position_ref)
        rows_ref[...] = jnp.zeros_like(rows_ref)
        rows_ref[:SMALL_ROWS, :] = feed_rows_ref[...]
        rows_ref[2:4, :] = pair_rows_ref[...]
        for place, ref in ((6, head_gain_ref), (7, head_shift_ref), (16, transform_ref), (17, pool_ref)):
            rows_ref[VECTOR_AT + place : VECTOR_AT + place + 1, :] = ref[...]

    def add_row(at, row):
        rows_ref[at : at + 1, :] = rows_ref[at : at + 1, :] + row

    def column_sum(values):
        return jnp.sum(values.astype(jnp.float32), axis=0, keepdims=True)

    grad = sum_ref[...]
    for number in range(3):
        grad = grad + product_right(
            mixed_ref[:, number * width : (number + 1) * width],
            proj_ref[:, number * width : (number + 1) * width],
        )
    grad, gain_sum, shift_sum = norm_back_rows(
        grad, normal_ref[...], inverse_ref[...], gain_ref[...]
    )
    low_ref[...] = grad.astype(jnp.bfloat16)
    position_ref[...] = position_ref[...] + grad
    second = lax.broadcasted_iota(jnp.int32, (tokens, 1), 0) >= length_ref[step] // 2
    late = jnp.sum(jnp.where(second, grad, 0.0), axis=0, keepdims=True)
    early = jnp.sum(jnp.where(second, 0.0, grad), axis=0, keepdims=True)
    add_row(0, early)
    add_row(1, late)
    add_row(VECTOR_AT, gain_sum)
    add_row(VECTOR_AT + 1, shift_sum)
    add_row(VECTOR_AT + 8, column_sum(mixed_ref[:, :width]))
    add_row(VECTOR_AT + 9, column_sum(mixed_ref[:, 2 * width :]))

    @pl.when(step == pl.num_programs(0) - 1)
    def _():
        small_ref[:, :tokens] = position_ref[...].T
        small_ref[:, tokens:] = rows_ref[...].T


def embed_back(lengths, grad_mixed, input_all, grad_sum, saved, gain, feed_rows, head_rows, tokens):
    rows, width = grad_sum.shape
    gain = gain[None]

    def tiled(columns):
        return pl.BlockSpec((tokens, columns), lambda i, lengths: (i, 0))

    def whole(array):
        return pl.BlockSpec(
            array.shape, lambda i, lengths: (0, 0), pipeline_mode=pl.Buffered(1)
        )

    small = jax.ShapeDtypeStruct((width, tokens + LANES), jnp.float32)
    return pl.pallas_call(
        embed_back_kernel,
        grid_spec=pltpu.PrefetchScalarGridSpec(
            num_scalar_prefetch=1,
            grid=(rows // tokens,),
            in_specs=[
                tiled(3 * width),
                whole(input_all),
                tiled(width),
                tiled(width),
                tiled(1),
                whole(gain),
                whole(feed_rows),
            ]
            + [whole(item) for item in head_rows],
            out_specs=(tiled(width), whole(small)),
            scratch_shapes=[
                pltpu.VMEM((tokens, width), jnp.float32),
                pltpu.VMEM((LANES, width), jnp.float32),
            ],
        ),
        out_shape=(jax.ShapeDtypeStruct((rows, width), jnp.bfloat16), small),
        compiler_params=pltpu.CompilerParams(vmem_limit_bytes=48 << 20),
        cost_estimate=pl.CostEstimate(
            flops=6 * rows * width * width,
            bytes_accessed=rows * width * 16 + 6 * width * width,
            transcendentals=0,
        ),
    )(lengths, grad_mixed, input_all, grad_sum, *saved, gain, feed_rows, *head_rows)


def square_kernel(count, *refs):
    terms, extra_ref, out_ref = refs[:count], refs[count], refs[count + 1]
    total = jnp.zeros((1, 1), jnp.float32)
    for ref in terms:
        rows = jnp.sum(ref[...] * ref[...], axis=1, keepdims=True)
        total = total + jnp.sum(rows, axis=0, keepdims=True)
    spot = lax.broadcasted_iota(jnp.int32, out_ref.shape, 1)
    out_ref[...] = extra_ref[...] + jnp.where(spot == 0, total, 0.0)


def add_squares(arrays, extra):
    return pl.pallas_call(
        partial(square_kernel, len(arrays)),
        out_shape=jax.ShapeDtypeStruct(extra.shape, jnp.float32),
    )(*arrays, extra)


def stepped(master, first, second, grad, decay):
    correct_one = 1.0 - BETA_ONE**STEP_COUNT
    correct_two = 1.0 - BETA_TWO**STEP_COUNT
    moment_one = BETA_ONE * first + (1.0 - BETA_ONE) * grad
    moment_two = BETA_TWO * second + (1.0 - BETA_TWO) * grad * grad
    direction = moment_one / correct_one / (jnp.sqrt(moment_two / correct_two) + ADAM_EPS)
    return master - LEARN_RATE * (direction + decay * master), moment_one, moment_two


def update_kernel(layout, factor_ref, *refs):
    count = len(layout)
    olds, refs = refs[: 3 * count], refs[3 * count :]
    grads, outs = refs[: -3 * count], refs[-3 * count :]
    factor = factor_ref[0]
    used = 0
    for number, entries in enumerate(layout):
        for lead, widths in enumerate(entries):
            start = 0
            for columns in widths:
                at = (slice(None), slice(start, start + columns))
                at = (lead,) + at if len(entries) > 1 else at
                news = stepped(
                    *(ref[at] for ref in olds[3 * number : 3 * number + 3]),
                    grads[used][...] * factor,
                    DECAY_RATE,
                )
                for ref, new in zip(outs[3 * number : 3 * number + 3], news):
                    ref[at] = new
                start += columns
                used += 1


def entire(array):
    zeros = (0,) * array.ndim
    return pl.BlockSpec(array.shape, lambda i: zeros)


def update_many(factor, triples, grads):
    layout = [[[piece.shape[1] for piece in row] for row in rows] for rows in grads]
    flat = [piece for rows in grads for row in rows for piece in row]
    olds = [array for triple in triples for array in triple]
    return pl.pallas_call(
        partial(update_kernel, layout),
        out_shape=tuple(jax.ShapeDtypeStruct(array.shape, jnp.float32) for array in olds),
        grid=(1,),
        in_specs=[pl.BlockSpec(memory_space=pltpu.SMEM)] + [entire(item) for item in olds + flat],
        out_specs=tuple(entire(item) for item in olds),
        compiler_params=pltpu.CompilerParams(vmem_limit_bytes=60 << 20),
        cost_estimate=pl.CostEstimate(
            flops=20 * sum(item.size for item in flat),
            bytes_accessed=28 * sum(item.size for item in flat),
            transcendentals=sum(item.size for item in flat),
        ),
    )(factor.reshape(1), *olds, *flat)


def gelu_parts(values):
    below = 0.5 + 0.5 * lax.erf(values * (0.5**0.5))
    density = jnp.exp(-0.5 * values * values) * ((0.5 / jnp.pi) ** 0.5)
    return values * below, below + values * density


def softmax_head(queries, keys, masking):
    scores = product_right(queries * HEAD ** (-0.5), keys) + masking
    expo = jnp.exp(scores - jnp.max(scores, axis=-1, keepdims=True))
    return expo * (1.0 / jnp.sum(expo, axis=-1, keepdims=True))


def masking_row(tokens, length):
    alive = lax.broadcasted_iota(jnp.int32, (1, tokens), 1) < length
    return jnp.where(alive, 0.0, MASKED_FILL)


def attend_kernel(length_ref, query_ref, key_ref, value_ref, context_ref):
    masking = masking_row(query_ref.shape[0], length_ref[pl.program_id(0)])
    contexts = []
    for start in (0, HEAD):
        part = slice(start, start + HEAD)
        attention = softmax_head(query_ref[:, part], key_ref[:, part], masking)
        contexts.append(product(attention.astype(jnp.bfloat16), value_ref[:, part]))
    context_ref[...] = jnp.concatenate(contexts, axis=1).astype(jnp.bfloat16)


def attend_back_kernel(length_ref, query_ref, key_ref, value_ref, grad_ref, out_ref):
    masking = masking_row(query_ref.shape[0], length_ref[pl.program_id(0)])
    outs = ([], [], [])
    for start in (0, HEAD):
        part = slice(start, start + HEAD)
        queries, keys, values = query_ref[:, part], key_ref[:, part], value_ref[:, part]
        grad = grad_ref[:, part]
        attention = softmax_head(queries, keys, masking)
        grad_attention = product_right(grad, values)
        grad_scores = attention * (
            grad_attention - jnp.sum(grad_attention * attention, axis=-1, keepdims=True)
        )
        grad_raw = grad_scores.astype(jnp.bfloat16)
        outs[0].append(product(grad_raw, keys) * HEAD ** (-0.5))
        outs[1].append(product_left(grad_raw, queries * HEAD ** (-0.5)))
        outs[2].append(product_left(attention.astype(jnp.bfloat16), grad))
    for number, pair in enumerate(outs):
        start = number * (out_ref.shape[1] // 3) + pl.program_id(1) * LANES
        out_ref[:, pl.ds(pl.multiple_of(start, LANES), LANES)] = jnp.concatenate(
            pair, axis=1
        ).astype(jnp.bfloat16)


def head_specs(tokens, pairs, count):
    return [
        pl.BlockSpec((tokens, LANES), lambda s, h, lengths, k=k: (s, k * pairs + h))
        for k in range(count)
    ]


def attend(lengths, mixed, tokens):
    width = mixed.shape[1] // 3
    pairs = width // LANES
    rows = mixed.shape[0]
    return pl.pallas_call(
        attend_kernel,
        grid_spec=pltpu.PrefetchScalarGridSpec(
            num_scalar_prefetch=1,
            grid=(rows // tokens, pairs),
            in_specs=head_specs(tokens, pairs, 3),
            out_specs=head_specs(tokens, pairs, 1)[0],
        ),
        out_shape=jax.ShapeDtypeStruct((rows, width), jnp.bfloat16),
        compiler_params=pltpu.CompilerParams(vmem_limit_bytes=32 << 20),
        cost_estimate=pl.CostEstimate(
            flops=8 * rows * tokens * width,
            bytes_accessed=8 * rows * width,
            transcendentals=rows * tokens * width // HEAD,
        ),
    )(lengths, mixed, mixed, mixed)


def attend_back(lengths, mixed, grad_context, tokens):
    width = mixed.shape[1] // 3
    pairs = width // LANES
    rows = mixed.shape[0]
    out = jax.ShapeDtypeStruct((rows, 3 * width), jnp.bfloat16)
    return pl.pallas_call(
        attend_back_kernel,
        grid_spec=pltpu.PrefetchScalarGridSpec(
            num_scalar_prefetch=1,
            grid=(rows // tokens, pairs),
            in_specs=head_specs(tokens, pairs, 3) + head_specs(tokens, pairs, 1),
            out_specs=pl.BlockSpec((tokens, 3 * width), lambda s, h, lengths: (s, 0)),
        ),
        out_shape=out,
        compiler_params=pltpu.CompilerParams(vmem_limit_bytes=32 << 20),
        cost_estimate=pl.CostEstimate(
            flops=20 * rows * tokens * width,
            bytes_accessed=14 * rows * width,
            transcendentals=rows * tokens * width // HEAD,
        ),
    )(lengths, mixed, mixed, mixed, grad_context)


def one_hot(count, index):
    return (
        lax.broadcasted_iota(jnp.int32, (count, index.shape[0]), 0) == index[None, :]
    ).astype(jnp.bfloat16)


def exact(left, right):
    return jnp.dot(left, right, precision=lax.Precision.HIGHEST, preferred_element_type=jnp.float32)


def shards(
    token_ids,
    seq_lengths,
    mlm_slots,
    mlm_labels,
    nsp_labels,
    *weights,
):
    masters, firsts, seconds = weights[0::3], weights[1::3], weights[2::3]
    (
        table_master,
        position_master,
        pair_master,
        input_master,
        output_master,
        dense_master,
        feed_master,
        vector_master,
    ) = masters
    micro, local, tokens = token_ids.shape
    slots_each = mlm_slots.shape[2]
    devices = lax.axis_size(AXES)
    me = lax.axis_index(AXES)
    seqs = micro * local
    total = seqs * tokens
    picked = seqs * slots_each
    depth, width = input_master.shape[0], output_master.shape[1]
    inner_width = feed_master.shape[2]
    vocab_rows = table_master.shape[0]
    low = jnp.bfloat16
    places = jnp.arange(tokens, dtype=jnp.int32)

    id_rows = total // LANES
    pack_rows = -(-(id_rows + 3 * seqs) // 8) * 8
    packed = pl.pallas_call(
        pack_kernel,
        out_shape=jax.ShapeDtypeStruct((pack_rows, LANES), jnp.int32),
        in_specs=[pl.BlockSpec(memory_space=pltpu.SMEM)]
        + [pl.BlockSpec(memory_space=pltpu.VMEM)] * 3,
    )(seq_lengths, token_ids, mlm_slots, mlm_labels)
    spread = jnp.broadcast_to(packed[None], (devices,) + packed.shape)
    shared = lax.all_to_all(spread, AXES, 0, 0)
    all_ids = shared[:, :id_rows].reshape(devices * seqs, tokens)
    all_slots, all_labels = (
        shared[:, id_rows + k * seqs : id_rows + (k + 1) * seqs, :slots_each] for k in (0, 1)
    )
    all_lengths = shared[:, id_rows + 2 * seqs : id_rows + 3 * seqs, :1]
    all_counted = (all_slots < all_lengths).astype(jnp.float32).reshape(-1)
    all_labels = all_labels.reshape(-1)
    masked_count = jnp.sum(all_counted)
    inv_count = 1.0 / masked_count
    inv_seqs = 1.0 / (devices * seqs)

    table_low = table_master.astype(low)
    vector_each = vector_master.shape[0]
    vector_columns = -(-vector_each // depth)
    small_used = tokens + 4 + vector_columns
    small_columns = -(-small_used // LANES) * LANES
    small_low = jnp.concatenate(
        [
            position_master.T,
            jnp.moveaxis(pair_master, 0, 1).reshape(depth, 4),
            jnp.pad(vector_master, (0, depth * vector_columns - vector_each)).reshape(
                depth, vector_columns
            ),
            jnp.zeros((depth, small_columns - small_used), jnp.float32),
        ],
        axis=1,
    ).astype(low)
    first_group = Gather(pin([input_master.astype(low), small_low], spread))

    lane_rows = -(-vocab_rows // LANES)

    def split_ids(ids, alive):
        owner = ids // vocab_rows
        within = ids - owner * vocab_rows
        high = owner * lane_rows + within // LANES
        return owner, jnp.where(alive, high, -1), within % LANES

    _, all_high, all_low = split_ids(
        all_ids, places[None, :] < all_lengths.reshape(devices * seqs, 1)
    )
    hits = product_right(
        one_hot(devices * lane_rows, all_high.reshape(-1)), one_hot(LANES, all_low.reshape(-1))
    )
    used = (hits > 0).astype(jnp.float32)
    lane = jnp.arange(LANES)
    before = exact(used, (lane[:, None] < lane[None, :]).astype(jnp.float32))
    row_totals = jnp.sum(used, axis=1).reshape(devices, lane_rows)
    row_index = jnp.arange(lane_rows)
    earlier = jnp.sum(
        jnp.where(row_index[None, :, None] < row_index[None, None, :], row_totals[:, :, None], 0.0),
        axis=1,
    )
    rank = before + earlier.reshape(-1, 1)
    most = jnp.max(jnp.sum(row_totals, axis=1)).astype(jnp.int32)
    ahead = ROWS_AHEAD
    rounds = -(-most // ahead)

    lengths = seq_lengths.reshape(-1)
    my_alive = (places[None, :] < lengths[:, None]).reshape(-1)
    my_owner, my_high, my_low = split_ids(token_ids.reshape(-1), my_alive)
    looked = exact(rank.T, one_hot(devices * lane_rows, my_high).astype(jnp.float32))
    my_rank = jnp.sum(looked * one_hot(LANES, my_low).astype(jnp.float32), axis=0).astype(jnp.int32)

    own_rank = lax.dynamic_slice_in_dim(rank, me * lane_rows, lane_rows, 0).reshape(-1)[:vocab_rows]
    own_used = lax.dynamic_slice_in_dim(used, me * lane_rows, lane_rows, 0).reshape(-1)[:vocab_rows]
    own_slot = jnp.where(own_used > 0, own_rank.astype(jnp.int32), -1)

    def picks(start):
        own = one_hot(ahead, jnp.where(own_slot >= start, own_slot - start, -1))
        inside = my_alive & (my_rank >= start) & (my_rank < start + ahead)
        mine = one_hot(devices * ahead, jnp.where(inside, my_owner * ahead + my_rank - start, -1))
        return own, mine

    own_first, mine_first = picks(0)
    own_rows = product(own_first, table_low).astype(low)
    word_group = Gather([own_rows])
    first_group.line(own_rows)
    first_plane = first_group.plane()
    word_group.line()
    word_plane = word_group.plane()
    second_group = Gather(
        pin(
            [output_master.astype(low), feed_master[0].astype(low)],
            [half[0] for half in word_plane],
            first_plane,
        )
    )
    first_core = first_group.core()
    second_group.line(word_plane, first_core)
    word_group.pieces = pin(word_plane, first_core, all_counted, all_labels)
    input_all, small_all = first_group.finish()
    word_core = word_group.core()
    (word_rows,) = word_group.finish()
    second_plane = second_group.plane()
    third_group = Gather(
        pin(
            [
                feed_master[1].astype(low),
                dense_master[0].astype(low),
                dense_master[1].astype(low),
            ],
            word_plane,
            first_core,
        )
    )
    third_group.line([half[0] for half in second_plane])
    words = product_left(mine_first, word_rows)

    def fetch_more(state):
        turn, words = state
        own, mine = picks(turn * ahead)
        rows = lax.all_gather(product(own, table_low).astype(low), AXES, axis=0, tiled=True)
        return turn + 1, words + product_left(mine, rows)

    _, words = lax.while_loop(lambda state: state[0] < rounds, fetch_more, (jnp.int32(1), words))

    position = small_all[:, :tokens].T.astype(jnp.float32)
    pair_cols = jnp.moveaxis(small_all[:, tokens : tokens + 4].reshape(width, 2, 2), 1, 0)
    vectors = small_all[:, tokens + 4 : small_used].reshape(devices, depth * vector_columns)
    parts = split_vectors(vectors[:, :vector_each].reshape(-1).astype(jnp.float32))

    second = (places[None, :] >= lengths[:, None] // 2).reshape(-1)
    type_cols = pair_cols[0].astype(jnp.float32)
    embedded = (
        words
        + jnp.tile(position, (seqs, 1))
        + jnp.where(second[:, None], type_cols[:, 1], type_cols[:, 0])
    )
    normed, saved_zero = norm_forward(embedded, parts[0], parts[1])
    normed_low = normed.astype(low)
    bias_mixed = jnp.concatenate([parts[8], jnp.zeros((width,), jnp.float32), parts[9]])
    mixed = (product(normed_low, input_all) + bias_mixed).astype(low)
    third_group.plane()
    context_low = attend(lengths, mixed, tokens)
    second_group.pieces = pin(second_group.pieces, mixed)
    second_group.core()
    output_all, feed_in = second_group.finish()
    third_group.pieces = pin(third_group.pieces, context_low)
    third_group.core()
    feed_out, dense_one, dense_two = third_group.finish()
    branch = product(context_low, output_all) + parts[10]
    hidden_one, saved_one = norm_forward(normed + branch, parts[2], parts[3])
    one_low = hidden_one.astype(low)
    active, slope = gelu_parts(product(one_low, feed_in) + parts[11])
    active_low, slope = lax.optimization_barrier((active.astype(low), slope))
    outer = product_right(active_low, feed_out) + parts[12]
    hidden_two, saved_two = norm_forward(hidden_one + outer, parts[4], parts[5])
    two_low = hidden_two.astype(low)

    my_slots = mlm_slots.reshape(seqs, slots_each) + tokens * jnp.arange(seqs, dtype=jnp.int32)[:, None]
    slot_hot = one_hot(total, my_slots.reshape(-1))
    picked_low = product_left(slot_hot, two_low).astype(low)
    lifted, head_slope = gelu_parts(product(picked_low, dense_one) + parts[13])
    head_out, saved_head = norm_forward(lifted, parts[6], parts[7])
    head_group = Gather([head_out.astype(low)])
    head_group.line()
    head_group.plane()

    first_hot = one_hot(total, tokens * jnp.arange(seqs, dtype=jnp.int32))
    first_low = product_left(first_hot, two_low).astype(low)
    pooled = jnp.tanh(product(first_low, dense_two) + parts[14])
    pooled_low = pooled.astype(low)
    pair_logits = product(pooled_low, pair_cols[1])
    pair_top = jnp.max(pair_logits, axis=-1, keepdims=True)
    pair_total = pair_top + jnp.log(
        jnp.sum(jnp.exp(pair_logits - pair_top), axis=-1, keepdims=True)
    )
    pair_hit = jnp.arange(2, dtype=jnp.int32)[None, :] == nsp_labels.reshape(-1, 1)
    pair_local = jnp.sum(pair_total[:, 0] - jnp.sum(jnp.where(pair_hit, pair_logits, 0.0), axis=1))

    vocab_bias = lax.dynamic_slice_in_dim(parts[15], me * vocab_rows, vocab_rows, 0)
    head_group.core()
    (heads,) = head_group.finish()
    logits = product_right(heads, table_low) + vocab_bias
    top = jnp.max(logits, axis=-1)
    local_totals = top + jnp.log(jnp.sum(jnp.exp(logits - top[:, None]), axis=-1))
    all_totals = share_small(local_totals.reshape(-1, LANES))
    highest = jnp.max(all_totals, axis=0)
    log_totals = (highest + jnp.log(jnp.sum(jnp.exp(all_totals - highest), axis=0))).reshape(-1)
    vocab_index = me * vocab_rows + jnp.arange(vocab_rows, dtype=jnp.int32)
    hit = vocab_index[None, :] == all_labels[:, None]
    target_local = jnp.sum(all_counted[:, None] * jnp.where(hit, logits, 0.0))
    grad_logits = (
        (jnp.exp(logits - log_totals[:, None]) - hit.astype(jnp.float32))
        * (all_counted * inv_count)[:, None]
    ).astype(low)
    middle = width // 2
    head_sum = Scatter(
        [
            (product(grad_logits, side).reshape(devices, picked, middle), number)
            for number, side in enumerate((table_low[:, :middle], table_low[:, middle:]))
        ]
    )
    sent = head_sum.send()
    grad_table = product_left(pin(grad_logits, sent), heads)
    def halves(values):
        high = values.astype(low)
        return high, (values - high.astype(jnp.float32)).astype(low)

    table_high, table_rest = halves(grad_table)
    chosen = product(own_first, table_high) + product(own_first, table_rest)
    table_square = jnp.sum(grad_table * grad_table)
    present = jnp.sum(own_first.astype(jnp.float32), axis=1, keepdims=True)
    masked_shared = jnp.sum(all_counted * pin(log_totals, sent))
    head_sum.receive()
    for _ in range(1, bits_of(lax.axis_size("wide"))):
        head_sum.step()
    grad_vocab = jnp.sum(grad_logits.astype(jnp.float32), axis=0)
    vocab_pad = -(-vocab_rows // (8 * LANES)) * 8 * LANES
    grad_vocab = jnp.pad(grad_vocab, (0, vocab_pad - vocab_rows)).reshape(-1, LANES)
    all_vocab = share_small(grad_vocab)
    head_sum.line()
    grad_head = jnp.concatenate(head_sum.finish(grad_table, all_vocab, table_square, chosen), axis=1)

    def owners(values):
        return values.reshape(devices, -1, values.shape[1])

    def column_sum(values):
        return jnp.sum(values.astype(jnp.float32), axis=0, keepdims=True)

    grad_gelu, grad_head_gain, grad_head_shift = norm_backward(grad_head, saved_head, parts[6])
    grad_transform = (grad_gelu * head_slope).astype(low)
    grad_dense_zero = product_left(picked_low, grad_transform)
    grad_pair_logits = (
        (jnp.exp(pair_logits - pair_total) - pair_hit.astype(jnp.float32)) * inv_seqs
    ).astype(low)
    grad_classifier = product_left(pooled_low, grad_pair_logits)
    grad_pooled = product_right(grad_pair_logits, pair_cols[1])
    grad_pool_pre = (grad_pooled * (1.0 - pooled * pooled)).astype(low)
    grad_pooler = product_left(first_low, grad_pool_pre)
    grad_two = exact(
        slot_hot.astype(jnp.float32), product_right(grad_transform, dense_one)
    ) + exact(first_hot.astype(jnp.float32), product_right(grad_pool_pre, dense_two))
    grad_outer, grad_inner, grad_sum_one, grad_branch, grad_context, feed_rows = feed_back(
        grad_two, saved_two, parts[4], slope, feed_out, feed_in, saved_one, parts[2], output_all
    )
    grad_feed_out = product_left(grad_outer, active_low)
    grad_feed_in = product_left(one_low, grad_inner)
    feed_sum = Scatter(
        [
            (owners(grad_feed_in), 0),
            (owners(grad_dense_zero), 0),
            (owners(grad_feed_out), 1),
            (owners(grad_pooler), 1),
        ]
    )
    feed_sum.send()
    came = feed_sum.receive()
    sent = feed_sum.send()
    grad_context = pin(grad_context, came, sent)
    grad_mixed = attend_back(lengths, mixed, grad_context, tokens)
    came = feed_sum.receive()
    sent = feed_sum.send()
    grad_mixed = pin(grad_mixed, came, sent)
    in_sum = Scatter(
        [
            (owners(product_left(normed_low, grad_mixed[:, : 2 * width])), 0),
            (owners(product_left(normed_low, grad_mixed[:, 2 * width :])), 1),
            (owners(product_left(context_low, pin(grad_branch, grad_mixed))), 1),
        ]
    )
    sent = in_sum.send()
    feed_came = [feed_sum.receive()]
    while feed_sum.dims[0]:
        feed_came.append(feed_sum.step())
    in_came = in_sum.receive()
    embedded_low, grad_small = embed_back(
        lengths,
        pin(grad_mixed, sent),
        input_all,
        grad_sum_one,
        saved_zero,
        parts[0],
        feed_rows,
        (
            grad_classifier.T,
            grad_head_gain[None],
            grad_head_shift[None],
            column_sum(grad_transform),
            column_sum(grad_pool_pre),
        ),
        tokens,
    )
    embedded_low, grad_small = pin((embedded_low, grad_small), feed_came, in_came)
    in_away = in_sum.send()
    embedded_low, grad_small = pin((embedded_low, grad_small), in_away)
    word_sums = [
        (product(mine_first, side).reshape(devices, ahead, middle), number)
        for number, side in enumerate((embedded_low[:, :middle], embedded_low[:, middle:]))
    ]
    vector_count = (vector_each * devices - devices * vocab_rows) // width
    last_sum = Scatter(word_sums + [(owners(grad_small), 1)])
    last_away = last_sum.send()
    in_came = in_sum.receive()
    feed_sum.hold(last_away)
    feed_came = feed_sum.line_whole()
    in_sum.hold(feed_sum.goes)
    in_away = in_sum.send()
    last_sum.receive()
    last_sum.hold(in_away)
    last_away = last_sum.send()
    in_sum.receive()
    while in_sum.dims[0]:
        in_sum.step()
    in_sum.hold(last_away)
    in_away = in_sum.line()
    last_sum.receive()
    while last_sum.dims[0]:
        last_sum.step()
    sent = last_sum.line()
    sum_feed_in, sum_dense, sum_feed_out, sum_pooler = feed_sum.finish_whole()
    sum_mixed, sum_value, sum_output = in_sum.finish(sent)
    words_left, words_right, sum_small = last_sum.finish()

    def return_more(state):
        turn, grad_table, table_square = state
        own, mine = picks(turn * ahead)
        back = lax.psum_scatter(
            product(mine, embedded_low), AXES, scatter_dimension=0, tiled=True
        )
        chosen = exact(own.astype(jnp.float32), grad_table)
        present = jnp.sum(own.astype(jnp.float32), axis=1, keepdims=True)
        table_square = table_square + jnp.sum(present * back * (back + 2.0 * chosen))
        return turn + 1, grad_table + exact(own.T.astype(jnp.float32), back), table_square

    _, grad_table, table_square = lax.while_loop(
        lambda state: state[0] < rounds, return_more, (jnp.int32(1), grad_table, table_square)
    )
    words_own = jnp.concatenate([words_left, words_right], axis=1)
    table_square = table_square + jnp.sum(present * words_own * (words_own + 2.0 * chosen))

    sum_vector = sum_small[:, tokens + 4 : tokens + 4 + vector_count]
    sum_position = sum_small[:, :tokens]
    sum_pair = sum_small[:, tokens : tokens + 4]
    scalars = jnp.stack([table_square, target_local, pair_local])
    scalars = add_squares(
        [
            sum_small[:, : tokens + 4 + vector_count],
            sum_mixed,
            sum_value,
            sum_output,
            sum_dense,
            sum_pooler,
            sum_feed_in,
            sum_feed_out,
            grad_vocab,
        ],
        jnp.pad(scalars, (0, LANES - 3))[None],
    )
    totals = jnp.sum(share_small(scalars)[:, 0, :3], axis=0)
    vector_flat = depth * vector_count
    vector_pad = -(-vector_flat // LANES) * LANES
    flat_vector = jnp.pad(sum_vector.reshape(-1), (0, vector_pad - vector_flat))
    all_vector = share_small(pin(flat_vector.reshape(-1, LANES), totals))
    grad_table = grad_table + product_left(
        jnp.concatenate([own_first, own_first], axis=0),
        jnp.concatenate(halves(words_own), axis=0),
    )
    grad_vector = jnp.concatenate(
        [
            all_vector.reshape(devices, -1)[:, :vector_flat]
            .reshape(devices * depth, vector_count)
            .T.reshape(-1),
            all_vocab.reshape(devices, -1)[:, :vocab_rows].reshape(-1),
        ]
    )
    totals, grad_table = lax.optimization_barrier((totals, grad_table))
    norm = jnp.sqrt(totals[0])
    masked_total = masked_shared - totals[1]
    pair_total_sum = totals[2]
    factor = CLIP_NORM / (norm + 1e-06)

    def straight(number):
        return masters[number], firsts[number], seconds[number]

    position = tuple(item.T for item in straight(1))
    many = update_many(
        factor,
        [position] + [straight(number) for number in (3, 4, 5, 6)],
        [
            [[sum_position]],
            [[sum_mixed, sum_value]],
            [[sum_output]],
            [[sum_dense], [sum_pooler]],
            [[sum_feed_in], [sum_feed_out]],
        ],
    )
    pair_grad = jnp.moveaxis(sum_pair.reshape(depth, 2, 2), 1, 0)
    vector_grad = lax.dynamic_slice_in_dim(grad_vector, me * vector_each, vector_each, 0)
    updated = (
        stepped(*straight(0), grad_table * factor, DECAY_RATE)
        + tuple(item.T for item in many[:3])
        + stepped(*straight(2), pair_grad * factor, DECAY_RATE)
        + tuple(many[3:])
        + stepped(*straight(7), vector_grad * factor, 0.0)
    )
    masked_sums = jnp.stack([masked_total, masked_count])
    return (masked_sums, pair_total_sum, norm) + updated


def solution(mesh):
    placed = (
        P(None, ("wide", "narrow"), None),
        P(None, ("wide", "narrow")),
        P(None, ("wide", "narrow"), None),
        P(None, ("wide", "narrow"), None),
        P(None, ("wide", "narrow")),
        P(("wide", "narrow"), None),
        P(("wide", "narrow"), None),
        P(("wide", "narrow"), None),
        P(None, ("wide", "narrow")),
        P(None, ("wide", "narrow")),
        P(None, ("wide", "narrow")),
        P(None, ("wide", "narrow"), None),
        P(None, ("wide", "narrow"), None),
        P(None, ("wide", "narrow"), None),
        P(("wide", "narrow"), None),
        P(("wide", "narrow"), None),
        P(("wide", "narrow"), None),
        P(("wide", "narrow"), None),
        P(("wide", "narrow"), None),
        P(("wide", "narrow"), None),
        P(None, ("wide", "narrow"), None),
        P(None, ("wide", "narrow"), None),
        P(None, ("wide", "narrow"), None),
        P(None, ("wide", "narrow"), None),
        P(None, ("wide", "narrow"), None),
        P(None, ("wide", "narrow"), None),
        P(("wide", "narrow")),
        P(("wide", "narrow")),
        P(("wide", "narrow")),
    )
    return jax.shard_map(
        shards,
        mesh=mesh,
        in_specs=placed,
        out_specs=(
            P(),
            P(),
            P(),
            P(("wide", "narrow"), None),
            P(("wide", "narrow"), None),
            P(("wide", "narrow"), None),
            P(None, ("wide", "narrow")),
            P(None, ("wide", "narrow")),
            P(None, ("wide", "narrow")),
            P(None, ("wide", "narrow"), None),
            P(None, ("wide", "narrow"), None),
            P(None, ("wide", "narrow"), None),
            P(("wide", "narrow"), None),
            P(("wide", "narrow"), None),
            P(("wide", "narrow"), None),
            P(("wide", "narrow"), None),
            P(("wide", "narrow"), None),
            P(("wide", "narrow"), None),
            P(None, ("wide", "narrow"), None),
            P(None, ("wide", "narrow"), None),
            P(None, ("wide", "narrow"), None),
            P(None, ("wide", "narrow"), None),
            P(None, ("wide", "narrow"), None),
            P(None, ("wide", "narrow"), None),
            P(("wide", "narrow")),
            P(("wide", "narrow")),
            P(("wide", "narrow")),
        ),
        check_vma=False,
    )
```

```python
from functools import partial

import jax
import jax.numpy as jnp
from jax import lax
from jax.experimental import pallas as pl
from jax.experimental.pallas import tpu as pltpu
from jax.sharding import PartitionSpec as P

D = 768
HEAD = 64
FF = 3072
STEP_COUNT = 10


NORM_EPS = 1e-12
CLIP_NORM = 0.02
BETA_ONE = 0.9
BETA_TWO = 0.999
ADAM_EPS = 1e-08
DECAY_RATE = 0.01
LEARN_RATE = 0.1
MASKED_FILL = -1000000000.0
AXES = ("wide", "narrow")
ROWS_AHEAD = 96
LANES = 128


def product(left, right):
    return jnp.dot(left, right, preferred_element_type=jnp.float32)


def product_right(left, right):
    return lax.dot_general(
        left, right, (((1,), (1,)), ((), ())), preferred_element_type=jnp.float32
    )


def product_left(left, right):
    return lax.dot_general(
        left, right, (((0,), (0,)), ((), ())), preferred_element_type=jnp.float32
    )


def norm_forward(values, gain, shift):
    average = jnp.mean(values, axis=-1, keepdims=True)
    centered = values - average
    spread = jnp.mean(centered * centered, axis=-1, keepdims=True)
    inverse = lax.rsqrt(spread + NORM_EPS)
    normal = centered * inverse
    return (normal * gain + shift, (normal, inverse))


def norm_backward(grad, saved, gain):
    normal, inverse = saved
    scaled = grad * gain
    inner = (
        scaled
        - jnp.mean(scaled, axis=-1, keepdims=True)
        - normal * jnp.mean(scaled * normal, axis=-1, keepdims=True)
    )
    return (inner * inverse, jnp.sum(grad * normal, axis=0), jnp.sum(grad, axis=0))


def gelu_exact(values):
    return jax.nn.gelu(values, approximate=False)


def gelu_back(values, grad):
    return jax.vjp(gelu_exact, values)[1](grad)[0]


def split_vectors(vectors):
    extents = [D] * 11 + [FF] + [D] * 3
    pieces = []
    start = 0
    for extent in extents:
        pieces.append(vectors[start : start + extent])
        start += extent
    pieces.append(vectors[start:])
    return pieces


def bits_of(size):
    return size.bit_length() - 1


def orders():
    far = [("wide", bit) for bit in range(1, bits_of(lax.axis_size("wide")))]
    return far, far[::-1]


CORE = ("wide", 0)


def my_bit(dim):
    return (lax.axis_index(dim[0]) >> dim[1]) & 1


def swap(values, dim):
    size = lax.axis_size(dim[0])
    return lax.ppermute(values, dim[0], [(i, i ^ (1 << dim[1])) for i in range(size)])


def pin(values, *others):
    return lax.optimization_barrier((values, others))[0]


def place_blocks(spreads, starts, middle, me_ref, *refs):
    count = len(spreads[0])
    outs = refs[8 : 8 + len(starts) - 1]
    held = refs[8 + len(outs) : 10 + len(outs)]
    arrive, leave = refs[10 + len(outs) :]
    me = me_ref[0]
    inward, outward = [], []
    for side in range(2):
        pieces = refs[4 * side : 4 * side + 4]
        each = pieces[0].shape[0]
        left = 0 if side == 0 else middle
        right = middle if side == 0 else starts[-1]
        for code, offset in enumerate(spreads[side]):
            number = side * count + code
            inward.append(
                pltpu.make_async_copy(
                    pieces[code // each].at[code % each], held[side].at[code], arrive.at[number]
                )
            )
            group = []
            for out_ref, start, stop in zip(outs, starts, starts[1:]):
                low, high = max(start, left), min(stop, right)
                if low < high:
                    group.append(
                        pltpu.make_async_copy(
                            held[side].at[code, :, :, low - left : high - left],
                            out_ref.at[me ^ offset, :, :, low - start : high - start],
                            leave.at[number, len(group)],
                        )
                    )
            outward.append(group)
    for copy in inward:
        copy.start()
    for first, group in zip(inward, outward):
        first.wait()
        for copy in group:
            copy.start()
    for group in outward:
        for copy in group:
            copy.wait()


def reach(values, step):
    size = lax.axis_size("narrow")
    return lax.ppermute(values, "narrow", [(z, z ^ step) for z in range(size)])


def trade(blocks):
    return lax.all_to_all(blocks, "narrow", 0, 0)


class Gather:
    def __init__(self, arrays):
        self.columns = [array.shape[1] for array in arrays]
        self.rows = arrays[0].shape[0]
        total = sum(self.columns)
        self.middle = total // 2 // LANES * LANES
        self.packed = jnp.concatenate(arrays, axis=1) if len(arrays) > 1 else arrays[0]

    def line(self, *before):
        size = lax.axis_size("narrow")
        me = lax.axis_index("narrow")
        arrived = pin([reach(self.packed, step) for step in range(1, size)], *before)
        blocks = []
        for spot in range(size):
            chosen = self.packed
            for step in range(1, size):
                chosen = jnp.where(me == spot ^ step, arrived[step - 1], chosen)
            blocks.append(chosen)
        self.halves = [
            jnp.stack([block[:, : self.middle] for block in blocks])[None],
            jnp.stack([block[:, self.middle :] for block in blocks])[None],
        ]
        return self.halves

    def line_whole(self, *before):
        size = lax.axis_size("narrow")
        blocks = trade(jnp.broadcast_to(self.packed[None], (size,) + self.packed.shape))
        blocks = pin(blocks, *before)
        self.halves = [
            blocks[None, :, :, : self.middle],
            blocks[None, :, :, self.middle :],
        ]
        return self.halves

    def plane(self, first=(), last=()):
        self.pieces = []
        for held, order in zip(pin(self.halves, first), orders()):
            for dim in order[:-1]:
                held = jnp.concatenate([held, swap(held, dim)], axis=0)
            self.pieces.append([held])
        self.pieces = pin(self.pieces, last)
        for piece, order in zip(self.pieces, orders()):
            piece.append(swap(piece[0], order[-1]))
        return self.pieces

    def core(self):
        self.pieces = [half + [swap(piece, CORE) for piece in half] for half in self.pieces]
        return self.pieces

    def finish(self):
        pieces = self.pieces
        count = lax.axis_size("wide")
        spreads = [
            [
                sum(((code >> k) & 1) << dim[1] for k, dim in enumerate(order + [CORE]))
                for code in range(count)
            ]
            for order in orders()
        ]
        starts = [sum(self.columns[:k]) for k in range(len(self.columns) + 1)]
        line = lax.axis_size("narrow")
        dtype = self.packed.dtype
        me = lax.axis_index("wide").astype(jnp.int32).reshape(1)
        moved = 2 * count * line * self.rows * starts[-1] * dtype.itemsize
        outs = pl.pallas_call(
            partial(place_blocks, spreads, starts, self.middle),
            out_shape=tuple(
                jax.ShapeDtypeStruct((count, line, self.rows, columns), dtype)
                for columns in self.columns
            ),
            in_specs=[pl.BlockSpec(memory_space=pltpu.SMEM)]
            + [pl.BlockSpec(memory_space=pl.ANY)] * 8,
            out_specs=(pl.BlockSpec(memory_space=pl.ANY),) * len(self.columns),
            scratch_shapes=[
                pltpu.VMEM((count, line, self.rows, self.middle), dtype),
                pltpu.VMEM((count, line, self.rows, starts[-1] - self.middle), dtype),
                pltpu.SemaphoreType.DMA((2 * count,)),
                pltpu.SemaphoreType.DMA((2 * count, len(self.columns))),
            ],
            compiler_params=pltpu.CompilerParams(vmem_limit_bytes=40 << 20),
            cost_estimate=pl.CostEstimate(flops=0, bytes_accessed=moved, transcendentals=0),
        )(me, *pieces[0], *pieces[1])
        return [out.reshape(count * line * self.rows, -1) for out in outs]


class Scatter:
    def __init__(self, items):
        wide, line = lax.axis_size("wide"), lax.axis_size("narrow")
        self.terms, self.dims, self.fixed = [], [], []
        for blocks, which in items:
            labels = tuple(("wide", bit) for bit in range(bits_of(wide)))[::-1]
            shape = (2,) * bits_of(wide) + (line,) + blocks.shape[1:]
            self.terms.append([(blocks.reshape(shape), labels)])
            self.dims.append([CORE] + orders()[which][::-1])
            self.fixed.append({})

    def cut(self, number, fixed):
        total = None
        for array, labels in self.terms[number]:
            starts = [fixed.get(label, 0) for label in labels]
            sizes = [1 if label in fixed else 2 for label in labels]
            starts += [0, 0, 0]
            sizes += list(array.shape[-3:])
            starts = [jnp.asarray(start, jnp.int32) for start in starts]
            kept = [2 for label in labels if label not in fixed] + sizes[-3:]
            part = lax.dynamic_slice(array, starts, sizes).reshape(kept).astype(jnp.float32)
            total = part if total is None else total + part
        return total

    def send(self):
        self.away = []
        for number, dims in enumerate(self.dims):
            fixed = dict(self.fixed[number])
            fixed[dims[0]] = 1 - my_bit(dims[0])
            self.away.append(self.cut(number, fixed).astype(jnp.bfloat16))
        return self.away

    def receive(self):
        arrived = []
        for number, away in enumerate(self.away):
            dim = self.dims[number].pop(0)
            self.fixed[number][dim] = my_bit(dim)
            arrived.append(swap(away, dim))
            labels = self.terms[number][0][1]
            left = tuple(label for label in labels if label not in self.fixed[number])
            self.terms[number].append((arrived[-1], left))
        return arrived

    def step(self):
        self.send()
        return self.receive()

    def absorb(self, other):
        self.terms += other.terms
        self.fixed += other.fixed
        self.dims += other.dims

    def hold(self, *others):
        arrays = pin([[term[0] for term in terms] for terms in self.terms], *others)
        self.terms = [
            [(array, term[1]) for array, term in zip(held, terms)]
            for held, terms in zip(arrays, self.terms)
        ]

    def line(self):
        size = lax.axis_size("narrow")
        me = lax.axis_index("narrow")
        depth = min(terms[0][0].shape[-2] for terms in self.terms)
        flat = []
        for number, fixed in enumerate(self.fixed):
            block = self.cut(number, fixed)
            flat.extend(block[:, k : k + depth] for k in range(0, block.shape[1], depth))
        whole = jnp.concatenate(flat, axis=2) if len(flat) > 1 else flat[0]
        whole = lax.optimization_barrier(whole)
        self.goes = [
            lax.dynamic_index_in_dim(whole, me ^ step, 0, keepdims=False).astype(jnp.bfloat16)
            for step in range(1, size)
        ]
        self.own = lax.dynamic_index_in_dim(whole, me, 0, keepdims=False)
        return self.goes

    def finish(self, *before):
        arrived = [reach(item, step + 1) for step, item in enumerate(self.goes)]
        arrived = pin(arrived, *before)
        return self.apart(self.own + sum(item.astype(jnp.float32) for item in arrived))

    def line_whole(self, *before):
        depth = min(terms[0][0].shape[-2] for terms in self.terms)
        flat = []
        for number, fixed in enumerate(self.fixed):
            block = self.cut(number, fixed).astype(jnp.bfloat16)
            flat.extend(block[:, k : k + depth] for k in range(0, block.shape[1], depth))
        self.goes = pin(jnp.concatenate(flat, axis=2) if len(flat) > 1 else flat[0], *before)
        self.arrived = trade(self.goes)
        return self.arrived

    def finish_whole(self):
        return self.apart(jnp.sum(self.arrived.astype(jnp.float32), axis=0))

    def apart(self, total):
        depth = total.shape[0]
        results, start = [], 0
        for terms in self.terms:
            parts, columns = terms[0][0].shape[-2] // depth, terms[0][0].shape[-1]
            pieces = [
                total[:, start + k * columns : start + (k + 1) * columns] for k in range(parts)
            ]
            start += parts * columns
            results.append(jnp.concatenate(pieces, axis=0) if parts > 1 else pieces[0])
        return results


def share_small(values):
    count = lax.axis_size(AXES)
    spread = jnp.broadcast_to(values[None], (count,) + values.shape)
    return lax.all_to_all(spread, AXES, 0, 0)


def pack_kernel(length_ref, ids_ref, slot_ref, label_ref, out_ref):
    out_ref[...] = jnp.zeros_like(out_ref)
    micro, local, tokens = ids_ref.shape
    slots = slot_ref.shape[2]
    row = 0
    for index in range(micro * local):
        for start in range(0, tokens, LANES):
            out_ref[row : row + 1, :] = ids_ref[
                index // local, index % local : index % local + 1, start : start + LANES
            ]
            row += 1
    for ref in (slot_ref, label_ref):
        for index in range(micro * local):
            out_ref[row : row + 1, :slots] = ref[
                index // local, index % local : index % local + 1, :
            ]
            row += 1
    for index in range(micro * local):
        out_ref[row : row + 1, :] = jnp.full(
            (1, LANES), length_ref[index // local, index % local], jnp.int32
        )
        row += 1


def norm_back_rows(grad, normal, inverse, gain):
    scaled = grad * gain
    inner = (
        scaled
        - jnp.mean(scaled, axis=-1, keepdims=True)
        - normal * jnp.mean(scaled * normal, axis=-1, keepdims=True)
    )
    return (
        inner * inverse,
        jnp.sum(grad * normal, axis=0, keepdims=True),
        jnp.sum(grad, axis=0, keepdims=True),
    )


SMALL_ROWS = 32
VECTOR_AT = 4


def feed_back_kernel(
    grad_ref,
    normal_two_ref,
    inverse_two_ref,
    gain_two_ref,
    slope_ref,
    out_proj_ref,
    in_proj_ref,
    normal_one_ref,
    inverse_one_ref,
    gain_one_ref,
    attend_proj_ref,
    outer_ref,
    inner_ref,
    sum_ref,
    branch_ref,
    context_ref,
    rows_ref,
):
    @pl.when(pl.program_id(0) == 0)
    def _():
        rows_ref[...] = jnp.zeros_like(rows_ref)

    def add_row(place, row):
        at = VECTOR_AT + place
        rows_ref[at : at + 1, :] = rows_ref[at : at + 1, :] + row

    def column_sum(values):
        return jnp.sum(values.astype(jnp.float32), axis=0, keepdims=True)

    width = grad_ref.shape[1]
    grad, gain_sum, shift_sum = norm_back_rows(
        grad_ref[...], normal_two_ref[...], inverse_two_ref[...], gain_two_ref[...]
    )
    add_row(4, gain_sum)
    add_row(5, shift_sum)
    outer = grad.astype(jnp.bfloat16)
    outer_ref[...] = outer
    add_row(15, column_sum(outer))
    for number, start in enumerate(range(0, slope_ref.shape[1], width)):
        part = slice(start, start + width)
        inner = (product(outer, out_proj_ref[:, part]) * slope_ref[:, part]).astype(jnp.bfloat16)
        inner_ref[:, part] = inner
        add_row(11 + number, column_sum(inner))
        grad = grad + product_right(inner, in_proj_ref[:, part])
    grad, gain_sum, shift_sum = norm_back_rows(
        grad, normal_one_ref[...], inverse_one_ref[...], gain_one_ref[...]
    )
    add_row(2, gain_sum)
    add_row(3, shift_sum)
    sum_ref[...] = grad
    branch = grad.astype(jnp.bfloat16)
    branch_ref[...] = branch
    add_row(10, column_sum(branch))
    context_ref[...] = product_right(branch, attend_proj_ref[...]).astype(jnp.bfloat16)


def feed_back(grad, saved_two, gain_two, slope, feed_out, feed_in, saved_one, gain_one, output_all):
    rows, width = grad.shape
    inner = slope.shape[1]
    tile = 256 if rows % 256 == 0 else rows

    def tiled(columns):
        return pl.BlockSpec((tile, columns), lambda i: (i, 0))

    def whole(array):
        return pl.BlockSpec(array.shape, lambda i: (0, 0), pipeline_mode=pl.Buffered(1))

    low = jnp.bfloat16
    gain_two, gain_one = gain_two[None], gain_one[None]
    return pl.pallas_call(
        feed_back_kernel,
        grid=(rows // tile,),
        in_specs=[
            tiled(width),
            tiled(width),
            tiled(1),
            whole(gain_two),
            tiled(inner),
            whole(feed_out),
            whole(feed_in),
            tiled(width),
            tiled(1),
            whole(gain_one),
            whole(output_all),
        ],
        out_specs=(
            tiled(width),
            tiled(inner),
            tiled(width),
            tiled(width),
            tiled(width),
            pl.BlockSpec((SMALL_ROWS, width), lambda i: (0, 0)),
        ),
        out_shape=(
            jax.ShapeDtypeStruct((rows, width), low),
            jax.ShapeDtypeStruct((rows, inner), low),
            jax.ShapeDtypeStruct((rows, width), jnp.float32),
            jax.ShapeDtypeStruct((rows, width), low),
            jax.ShapeDtypeStruct((rows, width), low),
            jax.ShapeDtypeStruct((SMALL_ROWS, width), jnp.float32),
        ),
        compiler_params=pltpu.CompilerParams(vmem_limit_bytes=56 << 20),
        cost_estimate=pl.CostEstimate(
            flops=2 * rows * width * (2 * inner + width),
            bytes_accessed=rows * (6 * inner + 22 * width) + 2 * width * (2 * inner + width),
            transcendentals=0,
        ),
    )(
        grad,
        *saved_two,
        gain_two,
        slope,
        feed_out,
        feed_in,
        *saved_one,
        gain_one,
        output_all,
    )


def embed_back_kernel(
    length_ref,
    mixed_ref,
    proj_ref,
    sum_ref,
    normal_ref,
    inverse_ref,
    gain_ref,
    feed_rows_ref,
    pair_rows_ref,
    head_gain_ref,
    head_shift_ref,
    transform_ref,
    pool_ref,
    low_ref,
    small_ref,
    position_ref,
    rows_ref,
):
    step = pl.program_id(0)
    tokens, width = sum_ref.shape

    @pl.when(step == 0)
    def _():
        position_ref[...] = jnp.zeros_like(position_ref)
        rows_ref[...] = jnp.zeros_like(rows_ref)
        rows_ref[:SMALL_ROWS, :] = feed_rows_ref[...]
        rows_ref[2:4, :] = pair_rows_ref[...]
        for place, ref in ((6, head_gain_ref), (7, head_shift_ref), (16, transform_ref), (17, pool_ref)):
            rows_ref[VECTOR_AT + place : VECTOR_AT + place + 1, :] = ref[...]

    def add_row(at, row):
        rows_ref[at : at + 1, :] = rows_ref[at : at + 1, :] + row

    def column_sum(values):
        return jnp.sum(values.astype(jnp.float32), axis=0, keepdims=True)

    grad = sum_ref[...]
    for number in range(3):
        grad = grad + product_right(
            mixed_ref[:, number * width : (number + 1) * width],
            proj_ref[:, number * width : (number + 1) * width],
        )
    grad, gain_sum, shift_sum = norm_back_rows(
        grad, normal_ref[...], inverse_ref[...], gain_ref[...]
    )
    low_ref[...] = grad.astype(jnp.bfloat16)
    position_ref[...] = position_ref[...] + grad
    second = lax.broadcasted_iota(jnp.int32, (tokens, 1), 0) >= length_ref[step] // 2
    late = jnp.sum(jnp.where(second, grad, 0.0), axis=0, keepdims=True)
    early = jnp.sum(jnp.where(second, 0.0, grad), axis=0, keepdims=True)
    add_row(0, early)
    add_row(1, late)
    add_row(VECTOR_AT, gain_sum)
    add_row(VECTOR_AT + 1, shift_sum)
    add_row(VECTOR_AT + 8, column_sum(mixed_ref[:, :width]))
    add_row(VECTOR_AT + 9, column_sum(mixed_ref[:, 2 * width :]))

    @pl.when(step == pl.num_programs(0) - 1)
    def _():
        small_ref[:, :tokens] = position_ref[...].T
        small_ref[:, tokens:] = rows_ref[...].T


def embed_back(lengths, grad_mixed, input_all, grad_sum, saved, gain, feed_rows, head_rows, tokens):
    rows, width = grad_sum.shape
    gain = gain[None]

    def tiled(columns):
        return pl.BlockSpec((tokens, columns), lambda i, lengths: (i, 0))

    def whole(array):
        return pl.BlockSpec(
            array.shape, lambda i, lengths: (0, 0), pipeline_mode=pl.Buffered(1)
        )

    small = jax.ShapeDtypeStruct((width, tokens + LANES), jnp.float32)
    return pl.pallas_call(
        embed_back_kernel,
        grid_spec=pltpu.PrefetchScalarGridSpec(
            num_scalar_prefetch=1,
            grid=(rows // tokens,),
            in_specs=[
                tiled(3 * width),
                whole(input_all),
                tiled(width),
                tiled(width),
                tiled(1),
                whole(gain),
                whole(feed_rows),
            ]
            + [whole(item) for item in head_rows],
            out_specs=(tiled(width), whole(small)),
            scratch_shapes=[
                pltpu.VMEM((tokens, width), jnp.float32),
                pltpu.VMEM((LANES, width), jnp.float32),
            ],
        ),
        out_shape=(jax.ShapeDtypeStruct((rows, width), jnp.bfloat16), small),
        compiler_params=pltpu.CompilerParams(vmem_limit_bytes=48 << 20),
        cost_estimate=pl.CostEstimate(
            flops=6 * rows * width * width,
            bytes_accessed=rows * width * 16 + 6 * width * width,
            transcendentals=0,
        ),
    )(lengths, grad_mixed, input_all, grad_sum, *saved, gain, feed_rows, *head_rows)


def square_kernel(count, *refs):
    terms, extra_ref, out_ref = refs[:count], refs[count], refs[count + 1]
    total = jnp.zeros((1, 1), jnp.float32)
    for ref in terms:
        rows = jnp.sum(ref[...] * ref[...], axis=1, keepdims=True)
        total = total + jnp.sum(rows, axis=0, keepdims=True)
    spot = lax.broadcasted_iota(jnp.int32, out_ref.shape, 1)
    out_ref[...] = extra_ref[...] + jnp.where(spot == 0, total, 0.0)


def add_squares(arrays, extra):
    return pl.pallas_call(
        partial(square_kernel, len(arrays)),
        out_shape=jax.ShapeDtypeStruct(extra.shape, jnp.float32),
    )(*arrays, extra)


def stepped(master, first, second, grad, decay):
    correct_one = 1.0 - BETA_ONE**STEP_COUNT
    correct_two = 1.0 - BETA_TWO**STEP_COUNT
    moment_one = BETA_ONE * first + (1.0 - BETA_ONE) * grad
    moment_two = BETA_TWO * second + (1.0 - BETA_TWO) * grad * grad
    direction = moment_one / correct_one / (jnp.sqrt(moment_two / correct_two) + ADAM_EPS)
    return master - LEARN_RATE * (direction + decay * master), moment_one, moment_two


def update_kernel(layout, factor_ref, *refs):
    count = len(layout)
    olds, refs = refs[: 3 * count], refs[3 * count :]
    grads, outs = refs[: -3 * count], refs[-3 * count :]
    factor = factor_ref[0]
    used = 0
    for number, entries in enumerate(layout):
        for lead, widths in enumerate(entries):
            start = 0
            for columns in widths:
                at = (slice(None), slice(start, start + columns))
                at = (lead,) + at if len(entries) > 1 else at
                news = stepped(
                    *(ref[at] for ref in olds[3 * number : 3 * number + 3]),
                    grads[used][...] * factor,
                    DECAY_RATE,
                )
                for ref, new in zip(outs[3 * number : 3 * number + 3], news):
                    ref[at] = new
                start += columns
                used += 1


def entire(array):
    zeros = (0,) * array.ndim
    return pl.BlockSpec(array.shape, lambda i: zeros)


def update_many(factor, triples, grads):
    layout = [[[piece.shape[1] for piece in row] for row in rows] for rows in grads]
    flat = [piece for rows in grads for row in rows for piece in row]
    olds = [array for triple in triples for array in triple]
    return pl.pallas_call(
        partial(update_kernel, layout),
        out_shape=tuple(jax.ShapeDtypeStruct(array.shape, jnp.float32) for array in olds),
        grid=(1,),
        in_specs=[pl.BlockSpec(memory_space=pltpu.SMEM)] + [entire(item) for item in olds + flat],
        out_specs=tuple(entire(item) for item in olds),
        compiler_params=pltpu.CompilerParams(vmem_limit_bytes=60 << 20),
        cost_estimate=pl.CostEstimate(
            flops=20 * sum(item.size for item in flat),
            bytes_accessed=28 * sum(item.size for item in flat),
            transcendentals=sum(item.size for item in flat),
        ),
    )(factor.reshape(1), *olds, *flat)


def gelu_parts(values):
    below = 0.5 + 0.5 * lax.erf(values * (0.5**0.5))
    density = jnp.exp(-0.5 * values * values) * ((0.5 / jnp.pi) ** 0.5)
    return values * below, below + values * density


def softmax_head(queries, keys, masking):
    scores = product_right(queries * HEAD ** (-0.5), keys) + masking
    expo = jnp.exp(scores - jnp.max(scores, axis=-1, keepdims=True))
    return expo * (1.0 / jnp.sum(expo, axis=-1, keepdims=True))


def masking_row(tokens, length):
    alive = lax.broadcasted_iota(jnp.int32, (1, tokens), 1) < length
    return jnp.where(alive, 0.0, MASKED_FILL)


def attend_kernel(length_ref, query_ref, key_ref, value_ref, context_ref):
    masking = masking_row(query_ref.shape[0], length_ref[pl.program_id(0)])
    contexts = []
    for start in (0, HEAD):
        part = slice(start, start + HEAD)
        attention = softmax_head(query_ref[:, part], key_ref[:, part], masking)
        contexts.append(product(attention.astype(jnp.bfloat16), value_ref[:, part]))
    context_ref[...] = jnp.concatenate(contexts, axis=1).astype(jnp.bfloat16)


def attend_back_kernel(length_ref, query_ref, key_ref, value_ref, grad_ref, out_ref):
    masking = masking_row(query_ref.shape[0], length_ref[pl.program_id(0)])
    outs = ([], [], [])
    for start in (0, HEAD):
        part = slice(start, start + HEAD)
        queries, keys, values = query_ref[:, part], key_ref[:, part], value_ref[:, part]
        grad = grad_ref[:, part]
        attention = softmax_head(queries, keys, masking)
        grad_attention = product_right(grad, values)
        grad_scores = attention * (
            grad_attention - jnp.sum(grad_attention * attention, axis=-1, keepdims=True)
        )
        grad_raw = grad_scores.astype(jnp.bfloat16)
        outs[0].append(product(grad_raw, keys) * HEAD ** (-0.5))
        outs[1].append(product_left(grad_raw, queries * HEAD ** (-0.5)))
        outs[2].append(product_left(attention.astype(jnp.bfloat16), grad))
    for number, pair in enumerate(outs):
        start = number * (out_ref.shape[1] // 3) + pl.program_id(1) * LANES
        out_ref[:, pl.ds(pl.multiple_of(start, LANES), LANES)] = jnp.concatenate(
            pair, axis=1
        ).astype(jnp.bfloat16)


def head_specs(tokens, pairs, count):
    return [
        pl.BlockSpec((tokens, LANES), lambda s, h, lengths, k=k: (s, k * pairs + h))
        for k in range(count)
    ]


def attend(lengths, mixed, tokens):
    width = mixed.shape[1] // 3
    pairs = width // LANES
    rows = mixed.shape[0]
    return pl.pallas_call(
        attend_kernel,
        grid_spec=pltpu.PrefetchScalarGridSpec(
            num_scalar_prefetch=1,
            grid=(rows // tokens, pairs),
            in_specs=head_specs(tokens, pairs, 3),
            out_specs=head_specs(tokens, pairs, 1)[0],
        ),
        out_shape=jax.ShapeDtypeStruct((rows, width), jnp.bfloat16),
        compiler_params=pltpu.CompilerParams(vmem_limit_bytes=32 << 20),
        cost_estimate=pl.CostEstimate(
            flops=8 * rows * tokens * width,
            bytes_accessed=8 * rows * width,
            transcendentals=rows * tokens * width // HEAD,
        ),
    )(lengths, mixed, mixed, mixed)


def attend_back(lengths, mixed, grad_context, tokens):
    width = mixed.shape[1] // 3
    pairs = width // LANES
    rows = mixed.shape[0]
    out = jax.ShapeDtypeStruct((rows, 3 * width), jnp.bfloat16)
    return pl.pallas_call(
        attend_back_kernel,
        grid_spec=pltpu.PrefetchScalarGridSpec(
            num_scalar_prefetch=1,
            grid=(rows // tokens, pairs),
            in_specs=head_specs(tokens, pairs, 3) + head_specs(tokens, pairs, 1),
            out_specs=pl.BlockSpec((tokens, 3 * width), lambda s, h, lengths: (s, 0)),
        ),
        out_shape=out,
        compiler_params=pltpu.CompilerParams(vmem_limit_bytes=32 << 20),
        cost_estimate=pl.CostEstimate(
            flops=20 * rows * tokens * width,
            bytes_accessed=14 * rows * width,
            transcendentals=rows * tokens * width // HEAD,
        ),
    )(lengths, mixed, mixed, mixed, grad_context)


def one_hot(count, index):
    return (
        lax.broadcasted_iota(jnp.int32, (count, index.shape[0]), 0) == index[None, :]
    ).astype(jnp.bfloat16)


def exact(left, right):
    return jnp.dot(left, right, precision=lax.Precision.HIGHEST, preferred_element_type=jnp.float32)


def shards(
    token_ids,
    seq_lengths,
    mlm_slots,
    mlm_labels,
    nsp_labels,
    *weights,
):
    masters, firsts, seconds = weights[0::3], weights[1::3], weights[2::3]
    (
        table_master,
        position_master,
        pair_master,
        input_master,
        output_master,
        dense_master,
        feed_master,
        vector_master,
    ) = masters
    micro, local, tokens = token_ids.shape
    slots_each = mlm_slots.shape[2]
    devices = lax.axis_size(AXES)
    me = lax.axis_index(AXES)
    seqs = micro * local
    total = seqs * tokens
    picked = seqs * slots_each
    depth, width = input_master.shape[0], output_master.shape[1]
    inner_width = feed_master.shape[2]
    vocab_rows = table_master.shape[0]
    low = jnp.bfloat16
    places = jnp.arange(tokens, dtype=jnp.int32)

    id_rows = total // LANES
    pack_rows = -(-(id_rows + 3 * seqs) // 8) * 8
    packed = pl.pallas_call(
        pack_kernel,
        out_shape=jax.ShapeDtypeStruct((pack_rows, LANES), jnp.int32),
        in_specs=[pl.BlockSpec(memory_space=pltpu.SMEM)]
        + [pl.BlockSpec(memory_space=pltpu.VMEM)] * 3,
    )(seq_lengths, token_ids, mlm_slots, mlm_labels)
    spread = jnp.broadcast_to(packed[None], (devices,) + packed.shape)
    shared = lax.all_to_all(spread, AXES, 0, 0)
    all_ids = shared[:, :id_rows].reshape(devices * seqs, tokens)
    all_slots, all_labels = (
        shared[:, id_rows + k * seqs : id_rows + (k + 1) * seqs, :slots_each] for k in (0, 1)
    )
    all_lengths = shared[:, id_rows + 2 * seqs : id_rows + 3 * seqs, :1]
    all_counted = (all_slots < all_lengths).astype(jnp.float32).reshape(-1)
    all_labels = all_labels.reshape(-1)
    masked_count = jnp.sum(all_counted)
    inv_count = 1.0 / masked_count
    inv_seqs = 1.0 / (devices * seqs)

    table_low = table_master.astype(low)
    vector_each = vector_master.shape[0]
    vector_columns = -(-vector_each // depth)
    small_used = tokens + 4 + vector_columns
    small_columns = -(-small_used // LANES) * LANES
    small_low = jnp.concatenate(
        [
            position_master.T,
            jnp.moveaxis(pair_master, 0, 1).reshape(depth, 4),
            jnp.pad(vector_master, (0, depth * vector_columns - vector_each)).reshape(
                depth, vector_columns
            ),
            jnp.zeros((depth, small_columns - small_used), jnp.float32),
        ],
        axis=1,
    ).astype(low)
    first_group = Gather(pin([input_master.astype(low), small_low], spread))

    lane_rows = -(-vocab_rows // LANES)

    def split_ids(ids, alive):
        owner = ids // vocab_rows
        within = ids - owner * vocab_rows
        high = owner * lane_rows + within // LANES
        return owner, jnp.where(alive, high, -1), within % LANES

    _, all_high, all_low = split_ids(
        all_ids, places[None, :] < all_lengths.reshape(devices * seqs, 1)
    )
    hits = product_right(
        one_hot(devices * lane_rows, all_high.reshape(-1)), one_hot(LANES, all_low.reshape(-1))
    )
    used = (hits > 0).astype(jnp.float32)
    lane = jnp.arange(LANES)
    before = exact(used, (lane[:, None] < lane[None, :]).astype(jnp.float32))
    row_totals = jnp.sum(used, axis=1).reshape(devices, lane_rows)
    row_index = jnp.arange(lane_rows)
    earlier = jnp.sum(
        jnp.where(row_index[None, :, None] < row_index[None, None, :], row_totals[:, :, None], 0.0),
        axis=1,
    )
    rank = before + earlier.reshape(-1, 1)
    most = jnp.max(jnp.sum(row_totals, axis=1)).astype(jnp.int32)
    ahead = ROWS_AHEAD
    rounds = -(-most // ahead)

    lengths = seq_lengths.reshape(-1)
    my_alive = (places[None, :] < lengths[:, None]).reshape(-1)
    my_owner, my_high, my_low = split_ids(token_ids.reshape(-1), my_alive)
    looked = exact(rank.T, one_hot(devices * lane_rows, my_high).astype(jnp.float32))
    my_rank = jnp.sum(looked * one_hot(LANES, my_low).astype(jnp.float32), axis=0).astype(jnp.int32)

    own_rank = lax.dynamic_slice_in_dim(rank, me * lane_rows, lane_rows, 0).reshape(-1)[:vocab_rows]
    own_used = lax.dynamic_slice_in_dim(used, me * lane_rows, lane_rows, 0).reshape(-1)[:vocab_rows]
    own_slot = jnp.where(own_used > 0, own_rank.astype(jnp.int32), -1)

    def picks(start):
        own = one_hot(ahead, jnp.where(own_slot >= start, own_slot - start, -1))
        inside = my_alive & (my_rank >= start) & (my_rank < start + ahead)
        mine = one_hot(devices * ahead, jnp.where(inside, my_owner * ahead + my_rank - start, -1))
        return own, mine

    own_first, mine_first = picks(0)
    own_rows = product(own_first, table_low).astype(low)
    word_group = Gather([own_rows])
    first_group.line(own_rows)
    first_plane = first_group.plane()
    word_group.line()
    word_plane = word_group.plane()
    second_group = Gather(
        pin(
            [output_master.astype(low), feed_master[0].astype(low)],
            [half[0] for half in word_plane],
            first_plane,
        )
    )
    first_core = first_group.core()
    second_group.line(word_plane, first_core)
    word_group.pieces = pin(word_plane, first_core, all_counted, all_labels)
    input_all, small_all = first_group.finish()
    word_core = word_group.core()
    (word_rows,) = word_group.finish()
    second_plane = second_group.plane()
    third_group = Gather(
        pin(
            [
                feed_master[1].astype(low),
                dense_master[0].astype(low),
                dense_master[1].astype(low),
            ],
            word_plane,
            first_core,
        )
    )
    third_group.line([half[0] for half in second_plane])
    words = product_left(mine_first, word_rows)

    def fetch_more(state):
        turn, words = state
        own, mine = picks(turn * ahead)
        rows = lax.all_gather(product(own, table_low).astype(low), AXES, axis=0, tiled=True)
        return turn + 1, words + product_left(mine, rows)

    _, words = lax.while_loop(lambda state: state[0] < rounds, fetch_more, (jnp.int32(1), words))

    position = small_all[:, :tokens].T.astype(jnp.float32)
    pair_cols = jnp.moveaxis(small_all[:, tokens : tokens + 4].reshape(width, 2, 2), 1, 0)
    vectors = small_all[:, tokens + 4 : small_used].reshape(devices, depth * vector_columns)
    parts = split_vectors(vectors[:, :vector_each].reshape(-1).astype(jnp.float32))

    second = (places[None, :] >= lengths[:, None] // 2).reshape(-1)
    type_cols = pair_cols[0].astype(jnp.float32)
    embedded = (
        words
        + jnp.tile(position, (seqs, 1))
        + jnp.where(second[:, None], type_cols[:, 1], type_cols[:, 0])
    )
    normed, saved_zero = norm_forward(embedded, parts[0], parts[1])
    normed_low = normed.astype(low)
    bias_mixed = jnp.concatenate([parts[8], jnp.zeros((width,), jnp.float32), parts[9]])
    mixed = (product(normed_low, input_all) + bias_mixed).astype(low)
    third_group.plane()
    context_low = attend(lengths, mixed, tokens)
    second_group.pieces = pin(second_group.pieces, mixed)
    second_group.core()
    output_all, feed_in = second_group.finish()
    third_group.pieces = pin(third_group.pieces, context_low)
    third_group.core()
    feed_out, dense_one, dense_two = third_group.finish()
    branch = product(context_low, output_all) + parts[10]
    hidden_one, saved_one = norm_forward(normed + branch, parts[2], parts[3])
    one_low = hidden_one.astype(low)
    active, slope = gelu_parts(product(one_low, feed_in) + parts[11])
    active_low, slope = lax.optimization_barrier((active.astype(low), slope))
    outer = product_right(active_low, feed_out) + parts[12]
    hidden_two, saved_two = norm_forward(hidden_one + outer, parts[4], parts[5])
    two_low = hidden_two.astype(low)

    my_slots = mlm_slots.reshape(seqs, slots_each) + tokens * jnp.arange(seqs, dtype=jnp.int32)[:, None]
    slot_hot = one_hot(total, my_slots.reshape(-1))
    picked_low = product_left(slot_hot, two_low).astype(low)
    lifted, head_slope = gelu_parts(product(picked_low, dense_one) + parts[13])
    head_out, saved_head = norm_forward(lifted, parts[6], parts[7])
    head_group = Gather([head_out.astype(low)])
    head_group.line()
    head_group.plane()

    first_hot = one_hot(total, tokens * jnp.arange(seqs, dtype=jnp.int32))
    first_low = product_left(first_hot, two_low).astype(low)
    pooled = jnp.tanh(product(first_low, dense_two) + parts[14])
    pooled_low = pooled.astype(low)
    pair_logits = product(pooled_low, pair_cols[1])
    pair_top = jnp.max(pair_logits, axis=-1, keepdims=True)
    pair_total = pair_top + jnp.log(
        jnp.sum(jnp.exp(pair_logits - pair_top), axis=-1, keepdims=True)
    )
    pair_hit = jnp.arange(2, dtype=jnp.int32)[None, :] == nsp_labels.reshape(-1, 1)
    pair_local = jnp.sum(pair_total[:, 0] - jnp.sum(jnp.where(pair_hit, pair_logits, 0.0), axis=1))

    vocab_bias = lax.dynamic_slice_in_dim(parts[15], me * vocab_rows, vocab_rows, 0)
    head_group.core()
    (heads,) = head_group.finish()
    logits = product_right(heads, table_low) + vocab_bias
    top = jnp.max(logits, axis=-1)
    local_totals = top + jnp.log(jnp.sum(jnp.exp(logits - top[:, None]), axis=-1))
    all_totals = share_small(local_totals.reshape(-1, LANES))
    highest = jnp.max(all_totals, axis=0)
    log_totals = (highest + jnp.log(jnp.sum(jnp.exp(all_totals - highest), axis=0))).reshape(-1)
    vocab_index = me * vocab_rows + jnp.arange(vocab_rows, dtype=jnp.int32)
    hit = vocab_index[None, :] == all_labels[:, None]
    target_local = jnp.sum(all_counted[:, None] * jnp.where(hit, logits, 0.0))
    grad_logits = (
        (jnp.exp(logits - log_totals[:, None]) - hit.astype(jnp.float32))
        * (all_counted * inv_count)[:, None]
    ).astype(low)
    middle = width // 2
    head_sum = Scatter(
        [
            (product(grad_logits, side).reshape(devices, picked, middle), number)
            for number, side in enumerate((table_low[:, :middle], table_low[:, middle:]))
        ]
    )
    sent = head_sum.send()
    grad_table = product_left(pin(grad_logits, sent), heads)
    def halves(values):
        high = values.astype(low)
        return high, (values - high.astype(jnp.float32)).astype(low)

    table_high, table_rest = halves(grad_table)
    chosen = product(own_first, table_high) + product(own_first, table_rest)
    table_square = jnp.sum(grad_table * grad_table)
    present = jnp.sum(own_first.astype(jnp.float32), axis=1, keepdims=True)
    masked_shared = jnp.sum(all_counted * pin(log_totals, sent))
    head_sum.receive()
    for _ in range(1, bits_of(lax.axis_size("wide"))):
        head_sum.step()
    grad_vocab = jnp.sum(grad_logits.astype(jnp.float32), axis=0)
    vocab_pad = -(-vocab_rows // (8 * LANES)) * 8 * LANES
    grad_vocab = jnp.pad(grad_vocab, (0, vocab_pad - vocab_rows)).reshape(-1, LANES)
    all_vocab = share_small(grad_vocab)
    head_sum.line()
    grad_head = jnp.concatenate(head_sum.finish(grad_table, all_vocab, table_square, chosen), axis=1)

    def owners(values):
        return values.reshape(devices, -1, values.shape[1])

    def column_sum(values):
        return jnp.sum(values.astype(jnp.float32), axis=0, keepdims=True)

    grad_gelu, grad_head_gain, grad_head_shift = norm_backward(grad_head, saved_head, parts[6])
    grad_transform = (grad_gelu * head_slope).astype(low)
    grad_dense_zero = product_left(picked_low, grad_transform)
    grad_pair_logits = (
        (jnp.exp(pair_logits - pair_total) - pair_hit.astype(jnp.float32)) * inv_seqs
    ).astype(low)
    grad_classifier = product_left(pooled_low, grad_pair_logits)
    grad_pooled = product_right(grad_pair_logits, pair_cols[1])
    grad_pool_pre = (grad_pooled * (1.0 - pooled * pooled)).astype(low)
    grad_pooler = product_left(first_low, grad_pool_pre)
    grad_two = exact(
        slot_hot.astype(jnp.float32), product_right(grad_transform, dense_one)
    ) + exact(first_hot.astype(jnp.float32), product_right(grad_pool_pre, dense_two))
    grad_outer, grad_inner, grad_sum_one, grad_branch, grad_context, feed_rows = feed_back(
        grad_two, saved_two, parts[4], slope, feed_out, feed_in, saved_one, parts[2], output_all
    )
    grad_feed_out = product_left(grad_outer, active_low)
    grad_feed_in = product_left(one_low, grad_inner)
    feed_sum = Scatter(
        [
            (owners(grad_feed_in), 0),
            (owners(grad_dense_zero), 0),
            (owners(grad_feed_out), 1),
            (owners(grad_pooler), 1),
        ]
    )
    feed_sum.send()
    came = feed_sum.receive()
    sent = feed_sum.send()
    grad_context = pin(grad_context, came, sent)
    grad_mixed = attend_back(lengths, mixed, grad_context, tokens)
    came = feed_sum.receive()
    sent = feed_sum.send()
    grad_mixed = pin(grad_mixed, came, sent)
    in_sum = Scatter(
        [
            (owners(product_left(normed_low, grad_mixed[:, : 2 * width])), 0),
            (owners(product_left(normed_low, grad_mixed[:, 2 * width :])), 1),
            (owners(product_left(context_low, pin(grad_branch, grad_mixed))), 1),
        ]
    )
    sent = in_sum.send()
    feed_came = [feed_sum.receive()]
    while feed_sum.dims[0]:
        feed_came.append(feed_sum.step())
    in_came = in_sum.receive()
    embedded_low, grad_small = embed_back(
        lengths,
        pin(grad_mixed, sent),
        input_all,
        grad_sum_one,
        saved_zero,
        parts[0],
        feed_rows,
        (
            grad_classifier.T,
            grad_head_gain[None],
            grad_head_shift[None],
            column_sum(grad_transform),
            column_sum(grad_pool_pre),
        ),
        tokens,
    )
    embedded_low, grad_small = pin((embedded_low, grad_small), feed_came, in_came)
    in_away = in_sum.send()
    embedded_low, grad_small = pin((embedded_low, grad_small), in_away)
    word_sums = [
        (product(mine_first, side).reshape(devices, ahead, middle), number)
        for number, side in enumerate((embedded_low[:, :middle], embedded_low[:, middle:]))
    ]
    vector_count = (vector_each * devices - devices * vocab_rows) // width
    last_sum = Scatter(word_sums + [(owners(grad_small), 1)])
    last_away = last_sum.send()
    in_came = in_sum.receive()
    feed_sum.hold(last_away)
    feed_came = feed_sum.line_whole()
    in_sum.hold(feed_sum.goes)
    in_away = in_sum.send()
    last_sum.receive()
    last_sum.hold(in_away)
    last_away = last_sum.send()
    in_sum.receive()
    while in_sum.dims[0]:
        in_sum.step()
    in_sum.hold(last_away)
    in_away = in_sum.line()
    last_sum.receive()
    while last_sum.dims[0]:
        last_sum.step()
    sent = last_sum.line()
    sum_feed_in, sum_dense, sum_feed_out, sum_pooler = feed_sum.finish_whole()
    sum_mixed, sum_value, sum_output = in_sum.finish(sent)
    vocab_flat = pin(all_vocab, sent).reshape(devices, -1)[:, :vocab_rows].reshape(-1)
    words_left, words_right, sum_small = last_sum.finish(vocab_flat)

    def return_more(state):
        turn, grad_table, table_square = state
        own, mine = picks(turn * ahead)
        back = lax.psum_scatter(
            product(mine, embedded_low), AXES, scatter_dimension=0, tiled=True
        )
        chosen = exact(own.astype(jnp.float32), grad_table)
        present = jnp.sum(own.astype(jnp.float32), axis=1, keepdims=True)
        table_square = table_square + jnp.sum(present * back * (back + 2.0 * chosen))
        return turn + 1, grad_table + exact(own.T.astype(jnp.float32), back), table_square

    _, grad_table, table_square = lax.while_loop(
        lambda state: state[0] < rounds, return_more, (jnp.int32(1), grad_table, table_square)
    )
    words_own = jnp.concatenate([words_left, words_right], axis=1)
    table_square = table_square + jnp.sum(present * words_own * (words_own + 2.0 * chosen))

    sum_vector = sum_small[:, tokens + 4 : tokens + 4 + vector_count]
    sum_position = sum_small[:, :tokens]
    sum_pair = sum_small[:, tokens : tokens + 4]
    scalars = jnp.stack([table_square, target_local, pair_local])
    scalars = add_squares(
        [
            sum_small[:, : tokens + 4 + vector_count],
            sum_mixed,
            sum_value,
            sum_output,
            sum_dense,
            sum_pooler,
            sum_feed_in,
            sum_feed_out,
            grad_vocab,
        ],
        jnp.pad(scalars, (0, LANES - 3))[None],
    )
    totals = jnp.sum(share_small(scalars)[:, 0, :3], axis=0)
    vector_flat = depth * vector_count
    vector_pad = -(-vector_flat // LANES) * LANES
    flat_vector = jnp.pad(sum_vector.reshape(-1), (0, vector_pad - vector_flat))
    all_vector = share_small(pin(flat_vector.reshape(-1, LANES), totals))
    grad_table = grad_table + product_left(
        jnp.concatenate([own_first, own_first], axis=0),
        jnp.concatenate(halves(words_own), axis=0),
    )
    grad_vector = jnp.concatenate(
        [
            all_vector.reshape(devices, -1)[:, :vector_flat]
            .reshape(devices * depth, vector_count)
            .T.reshape(-1),
            vocab_flat,
        ]
    )
    totals, grad_table = lax.optimization_barrier((totals, grad_table))
    norm = jnp.sqrt(totals[0])
    masked_total = masked_shared - totals[1]
    pair_total_sum = totals[2]
    factor = CLIP_NORM / (norm + 1e-06)

    def straight(number):
        return masters[number], firsts[number], seconds[number]

    position = tuple(item.T for item in straight(1))
    many = update_many(
        factor,
        [position] + [straight(number) for number in (3, 4, 5, 6)],
        [
            [[sum_position]],
            [[sum_mixed, sum_value]],
            [[sum_output]],
            [[sum_dense], [sum_pooler]],
            [[sum_feed_in], [sum_feed_out]],
        ],
    )
    pair_grad = jnp.moveaxis(sum_pair.reshape(depth, 2, 2), 1, 0)
    vector_grad = lax.dynamic_slice_in_dim(grad_vector, me * vector_each, vector_each, 0)
    updated = (
        stepped(*straight(0), grad_table * factor, DECAY_RATE)
        + tuple(item.T for item in many[:3])
        + stepped(*straight(2), pair_grad * factor, DECAY_RATE)
        + tuple(many[3:])
        + stepped(*straight(7), vector_grad * factor, 0.0)
    )
    masked_sums = jnp.stack([masked_total, masked_count])
    return (masked_sums, pair_total_sum, norm) + updated


def solution(mesh):
    placed = (
        P(None, ("wide", "narrow"), None),
        P(None, ("wide", "narrow")),
        P(None, ("wide", "narrow"), None),
        P(None, ("wide", "narrow"), None),
        P(None, ("wide", "narrow")),
        P(("wide", "narrow"), None),
        P(("wide", "narrow"), None),
        P(("wide", "narrow"), None),
        P(None, ("wide", "narrow")),
        P(None, ("wide", "narrow")),
        P(None, ("wide", "narrow")),
        P(None, ("wide", "narrow"), None),
        P(None, ("wide", "narrow"), None),
        P(None, ("wide", "narrow"), None),
        P(("wide", "narrow"), None),
        P(("wide", "narrow"), None),
        P(("wide", "narrow"), None),
        P(("wide", "narrow"), None),
        P(("wide", "narrow"), None),
        P(("wide", "narrow"), None),
        P(None, ("wide", "narrow"), None),
        P(None, ("wide", "narrow"), None),
        P(None, ("wide", "narrow"), None),
        P(None, ("wide", "narrow"), None),
        P(None, ("wide", "narrow"), None),
        P(None, ("wide", "narrow"), None),
        P(("wide", "narrow")),
        P(("wide", "narrow")),
        P(("wide", "narrow")),
    )
    return jax.shard_map(
        shards,
        mesh=mesh,
        in_specs=placed,
        out_specs=(
            P(),
            P(),
            P(),
            P(("wide", "narrow"), None),
            P(("wide", "narrow"), None),
            P(("wide", "narrow"), None),
            P(None, ("wide", "narrow")),
            P(None, ("wide", "narrow")),
            P(None, ("wide", "narrow")),
            P(None, ("wide", "narrow"), None),
            P(None, ("wide", "narrow"), None),
            P(None, ("wide", "narrow"), None),
            P(("wide", "narrow"), None),
            P(("wide", "narrow"), None),
            P(("wide", "narrow"), None),
            P(("wide", "narrow"), None),
            P(("wide", "narrow"), None),
            P(("wide", "narrow"), None),
            P(None, ("wide", "narrow"), None),
            P(None, ("wide", "narrow"), None),
            P(None, ("wide", "narrow"), None),
            P(None, ("wide", "narrow"), None),
            P(None, ("wide", "narrow"), None),
            P(None, ("wide", "narrow"), None),
            P(("wide", "narrow")),
            P(("wide", "narrow")),
            P(("wide", "narrow")),
        ),
        check_vma=False,
    )
```
